32 devices in a mesh: dp: 16 (over z, x, core), seq: 2 (over y).
Axes of the slice: x: 2, y: 2, z: 4, core: 2. Of those that a mesh axis runs over, the one named last changes fastest.
Arguments:
- tokens: bfloat16 [8192, 1024], P(('dp', 'seq')), may hold values from -6 to 6
- memory: bfloat16 [8192, 1024], P(('dp', 'seq')), may hold values from -6 to 6
- attn_bank: bfloat16 [8192, 1024], P(('dp', 'seq')), may hold values from -2.828427 to 2.828427
- ffn_bank: bfloat16 [8192, 1024], P(('dp', 'seq')), may hold values from -0.375 to 0.375
- norm_params: float32 [6, 1024], replicated, may hold values from 0.1 to 1.9
- prefix: int32 [16], P('dp'), may hold values from 0 to 256, as said below
- cotangent: bfloat16 [8192, 1024], P(('dp', 'seq')), may hold values from -6 to 6
Outputs:
- output: float32 [8192, 1024], P(('dp', 'seq'))
- d_tokens: float32 [8192, 1024], P(('dp', 'seq'))
- d_memory: float32 [8192, 1024], P(('dp', 'seq'))
- d_attn_bank: float32 [8192, 1024], P(('dp', 'seq'))
- d_ffn_bank: float32 [8192, 1024], P(('dp', 'seq'))
- d_norm_params: float32 [6, 1024], replicated
The draws below stay inside these ranges and needn't reach their ends.
Inputs may be any that keep to these rules, and one draw needn't show every extreme that they name: `prefix`: 0 in some pair and 256 in another.
All inputs are finite; a program needn't handle non-finite values.
Results may differ from the reference program's by a relative error of at most 0.025.
Values may be sent and summed in bfloat16 or wider, within the bound.
A program may use at most 192 MiB of HBM per device.

```python
import jax
import jax.numpy as jnp
from jax import lax

D = 1024
HEADS = 16
HD = 64
FF = 4096
LEN = 512
PAIRS = 16
TOKENS = 8192


def draw_attn_bank(key, part):
    key = jax.random.fold_in(key, 11)
    normal = jax.random.truncated_normal(key, -4.0, 4.0, (8 * D, D), jnp.float32)
    block = jnp.arange(8 * D) // D
    factor = jnp.where((block == 3) | (block == 7), LEN ** 0.5, 1.0) * D ** (-0.5)
    return (normal * factor[:, None]).astype(jnp.bfloat16)


def draw_ffn_bank(key, part):
    key = jax.random.fold_in(key, 23)
    normal = jax.random.truncated_normal(key, -4.0, 4.0, (2 * FF, D), jnp.float32)
    upper = jnp.arange(2 * FF) >= FF
    factor = jnp.where(upper, 6.0 * FF ** (-0.5), D ** (-0.5))
    return (normal * factor[:, None]).astype(jnp.bfloat16)


def draw_prefix(key, part):
    key = jax.random.fold_in(key, 37)
    first, second, third = jax.random.split(key, 3)
    values = jax.random.randint(first, (PAIRS,), 0, LEN // 2 + 1)
    top_place = jax.random.randint(second, (), 0, PAIRS // 2)
    bottom_place = PAIRS // 2 + jax.random.randint(third, (), 0, PAIRS - PAIRS // 2)
    return values.at[top_place].set(LEN // 2).at[bottom_place].set(0).astype(jnp.int32)


def block_levels(rng, dims, shards, least, high):
    level, own = 1.0, jax.random.fold_in(rng, 6)
    for position, parts in shards:
        heights = jnp.exp(jax.random.uniform(jax.random.fold_in(own, position), (parts,), jnp.float32, least / len(shards), high / len(shards)))
        level = level * jnp.repeat(heights, dims[position] // parts).reshape([-1 if axis == position else 1 for axis in range(len(dims))])
    return level


def noise(stream_key, shape, scale, limit, pieces=(), held_as=jnp.bfloat16):
    values = jax.random.normal(stream_key, shape, jnp.float32) * scale
    if len(pieces) > 0:
        values = block_levels(stream_key, shape, pieces, -0.22, 0.18) * values
    return jnp.clip(values, min=-limit, max=limit).astype(held_as)


def setup_inputs(seed: int = 0) -> dict:
    key_list = jax.random.split(jax.random.key(seed), 8)
    tokens = noise(key_list[0], (TOKENS, D), 1.0, 6.0, ((0, 32),))
    memory = noise(key_list[1], (TOKENS, D), 1.0, 6.0, ((0, 32),))
    attn_bank = draw_attn_bank(jax.random.fold_in(key_list[7], 71), 0)
    ffn_bank = draw_ffn_bank(jax.random.fold_in(key_list[7], 71), 0)
    norm_params = jnp.clip(1.0 + 0.18 * jax.random.normal(key_list[4], (6, D), jnp.float32), 0.1, 1.9)
    prefix = draw_prefix(jax.random.fold_in(key_list[7], 71), 0)
    cotangent = noise(key_list[6], (TOKENS, D), 1.0, 6.0, ((0, 32),))
    return {"tokens": tokens, "memory": memory, "attn_bank": attn_bank, "ffn_bank": ffn_bank, "norm_params": norm_params, "prefix": prefix, "cotangent": cotangent}


alpha_scale = 300.0 ** 0.25
norm_eps = 1e-05
masked_score = -1e+30
precise = lax.Precision.HIGHEST

@jax.custom_vjp
def low(v):
    return lax.optimization_barrier(v.astype(jnp.bfloat16)).astype(jnp.float32)

@jax.custom_vjp
def low_back(v):
    return v

def low_keep(v):
    return (low(v), None)

def low_pass(kept, grad):
    return (grad,)

def back_keep(v):
    return (v, None)

def back_low(kept, grad):
    return (low(grad),)
low.defvjp(low_keep, low_pass)
low_back.defvjp(back_keep, back_low)

def rounded_both(value):
    return low_back(low(value))

def product(left, right):
    return jnp.dot(left, right, precision=precise, preferred_element_type=jnp.float32)

def product_nt(left, right):
    return jnp.dot(left, right.T, precision=precise, preferred_element_type=jnp.float32)

def layer_norm(summed, gain_row, shift_row):
    centred = summed - lax.optimization_barrier(jnp.mean(summed, axis=-1, keepdims=True))
    inv_std = lax.rsqrt(lax.optimization_barrier(jnp.mean(centred * centred, axis=-1, keepdims=True)) + norm_eps)
    return centred * inv_std * gain_row + shift_row

def split_heads(matrix):
    return matrix.reshape(matrix.shape[0], HEADS, HD).transpose(1, 0, 2)

def attention(queries, key_rows, value_rows, visible):
    length = queries.shape[0]

    def one_head(head_items):
        query_head, key_head, value_head = head_items
        scores = HD ** (-0.5) * product_nt(query_head, key_head)
        scores = low_back(jnp.where(visible, scores, masked_score))
        probs = jax.nn.softmax(scores, axis=-1)
        return product(low(probs), value_head)
    mixed_rows = lax.map(jax.checkpoint(one_head), (split_heads(queries), split_heads(key_rows), split_heads(value_rows)))
    return mixed_rows.transpose(1, 0, 2).reshape(length, HEADS * HD)

def forward(token_rows, memory_rows, attn_arg, ffn_arg, norm_arg, prefix_len):
    blocks = attn_arg.reshape(8, D, D)
    weight_in = ffn_arg[:FF]
    weight_out = ffn_arg[FF:]
    positions = jnp.arange(LEN, dtype=jnp.int32)
    visible = (positions[None, :] <= positions[:, None]) | (positions[None, :] < prefix_len)
    everywhere = jnp.ones((LEN, LEN), dtype=bool)
    query_self = rounded_both(product(token_rows, blocks[0]))
    key_self = rounded_both(product(token_rows, blocks[1]))
    value_self = rounded_both(product(token_rows, blocks[2]))
    mixed_self = rounded_both(attention(query_self, key_self, value_self, visible))
    first_out = layer_norm(alpha_scale * token_rows + low_back(product(mixed_self, blocks[3])), norm_arg[0], norm_arg[3])
    query_cross = rounded_both(product(low(first_out), blocks[4]))
    key_cross = rounded_both(product(memory_rows, blocks[5]))
    value_cross = rounded_both(product(memory_rows, blocks[6]))
    mixed_cross = rounded_both(attention(query_cross, key_cross, value_cross, everywhere))
    second_out = layer_norm(alpha_scale * first_out + low_back(product(mixed_cross, blocks[7])), norm_arg[1], norm_arg[4])
    hidden_pre = low_back(product_nt(low(second_out), weight_in))
    hidden_act = low(jax.nn.silu(hidden_pre))
    return layer_norm(alpha_scale * second_out + low_back(product(hidden_act, weight_out)), norm_arg[2], norm_arg[5])

def reference(tokens, memory, attn_bank, ffn_bank, norm_params, prefix, cotangent):
    attn_wide = attn_bank.astype(jnp.float32)
    ffn_wide = ffn_bank.astype(jnp.float32)
    norm_wide = norm_params.astype(jnp.float32)
    token_pairs = tokens.astype(jnp.float32).reshape(PAIRS, LEN, D)
    memory_pairs = memory.astype(jnp.float32).reshape(PAIRS, LEN, D)
    tangent_pairs = cotangent.astype(jnp.float32).reshape(PAIRS, LEN, D)

    def per_pair(totals, pair_items):
        token_rows, memory_rows, tangent_rows, prefix_len = pair_items

        def pair_forward(token_arg, memory_arg, attn_arg, ffn_arg, norm_arg):
            return forward(token_arg, memory_arg, attn_arg, ffn_arg, norm_arg, prefix_len)
        result, pullback = jax.vjp(pair_forward, token_rows, memory_rows, attn_wide, ffn_wide, norm_wide)
        token_grad, memory_grad, attn_grad, ffn_grad, norm_grad = pullback(tangent_rows)
        totals = (totals[0] + attn_grad, totals[1] + ffn_grad, totals[2] + norm_grad)
        return (totals, (result, token_grad, memory_grad))
    initial = (jnp.zeros((8 * D, D), jnp.float32), jnp.zeros((2 * FF, D), jnp.float32), jnp.zeros((6, D), jnp.float32))
    totals, outputs = lax.scan(per_pair, initial, (token_pairs, memory_pairs, tangent_pairs, prefix.astype(jnp.int32)))
    results, token_grads, memory_grads = outputs
    return (results.reshape(TOKENS, D), token_grads.reshape(TOKENS, D), memory_grads.reshape(TOKENS, D), totals[0], totals[1], totals[2])
```

```python
import functools

import jax
import jax.numpy as jnp
from jax import lax
from jax.experimental import pallas as pl
from jax.experimental.pallas import tpu as pltpu
from jax.sharding import PartitionSpec as P

HD = 64
PAIR = 2 * HD
TILE = 512
SUB = 16
LN_ROWS = 32

alpha_scale = 300.0**0.25
norm_eps = 1e-05
masked_score = -1e30
score_scale = HD**-0.5

BF = jnp.bfloat16
F32 = jnp.float32
MESH = pl.DeviceIdType.MESH


def dot(left, right):
    return jnp.dot(left, right, preferred_element_type=F32)


def dot_nt(left, right):
    return lax.dot_general(left, right, (((1,), (1,)), ((), ())), preferred_element_type=F32)


def dot_tn(left, right):
    return lax.dot_general(left, right, (((0,), (0,)), ((), ())), preferred_element_type=F32)


def turned(block):
    return block.astype(F32).T.astype(BF)


def cut(rows):
    units = rows // SUB
    small = (units * 3) // 16
    big = (units - 2 * small + 1) // 2
    sizes = [("xzy", big), ("yzx", units - 2 * small - big), ("zxy", small), ("zyx", small)]
    parts, start = [], 0
    for order, size in sizes:
        if size > 0:
            parts.append((order, start * SUB, size * SUB))
        start += size
    return parts


def slots_of(order, A):
    return 4 * A + 3 if order[0] != "z" else 4 * A + 1


class Layer:
    def __init__(self, A, R, T, parts, refs):
        self.A, self.R, self.T, self.parts = A, R, T, parts
        self.D = 1024
        self.nzx = self.D // (4 * R)
        self.nt = TILE // (2 * R)
        for name, ref in refs.items():
            setattr(self, name, ref)
        self.dp, self.y = lax.axis_index("dp"), lax.axis_index("seq")
        self.c = lax.rem(self.dp, 2)
        self.x = lax.rem(self.dp // 2, 2)
        self.z = self.dp // 4
        self.zx = self.dp // 2
        self.sib = (self.dp + 1 - 2 * self.c, self.y)
        self.near = {"x": (self.dp + 2 - 4 * self.x, self.y), "y": (self.dp, 1 - self.y)}
        self.up = (self.dp + 4, self.y)
        self.down = (self.dp - 4, self.y)
        self.partner = (self.dp - self.c + self.y, self.c)
        self.has_up = self.z < A - 1
        self.has_down = self.z > 0
        self.kept = self.c == self.y
        self.turns = [self.turn(j) for j in range(A)]


    def remote(self, src, dst, send, recv, device):
        return pltpu.make_async_remote_copy(
            src_ref=src, dst_ref=dst, send_sem=send, recv_sem=recv, device_id=device, device_id_type=MESH
        )

    def own(self, axis):
        return self.x if axis == "x" else self.y

    def spot(self, bank, part, z, x, y):
        order, start, rows = self.parts[part]
        row = pl.multiple_of(y * self.R + start, SUB)
        return self.wb.at[bank * 2 * self.A + z * 2 + x, :, pl.ds(row, rows), :]

    def place(self, axis, f, l):
        return (f, l) if axis == "x" else (l, f)


    def barrier(self):
        bar = pltpu.get_barrier_semaphore()

        def greet(device):
            pl.semaphore_signal(bar, inc=1, device_id=device, device_id_type=MESH)

        greet(self.sib)
        greet(self.near["x"])
        greet(self.near["y"])
        for other in range(self.A):

            @pl.when(self.z != other)
            def _():
                greet((self.dp + 4 * (other - self.z), self.y))

        @pl.when(jnp.logical_not(self.kept))
        def _():
            greet(self.partner)
            pl.semaphore_wait(bar, 3 + self.A)

        @pl.when(self.kept)
        def _():
            pl.semaphore_wait(bar, 2 + self.A)


    def ag_index(self, bank, part, z, x, y):
        return ((bank * len(self.parts) + part) * 2 * self.A + z * 2 + x) * 2 + y

    def ag_send(self, bank, part, z, x, y, kind, device):
        ref = self.spot(bank, part, z, x, y)
        slot = (bank * len(self.parts) + part) * 4 + kind
        self.remote(ref, ref, self.ag_s.at[slot], self.ag_r.at[self.ag_index(bank, part, z, x, y)], device).start()

    def ag_wait(self, bank, part, z, x, y):
        ref = self.spot(bank, part, z, x, y)
        self.remote(
            ref, ref, self.ag_s.at[0], self.ag_r.at[self.ag_index(bank, part, z, x, y)], self.sib
        ).wait_recv()

    def ag(self, bank):
        A = self.A
        steps = []
        for part, (order, _, _) in enumerate(self.parts):
            f, l = (order[0], order[2]) if order[0] != "z" else (order[1], order[2])
            steps.append((part, order[0] != "z", f, l, self.own(f), self.own(l)))

        def z_sends(part, f, fc, lc, w, z=None):
            z = self.z if z is None else z
            px, py = self.place(f, fc, lc)

            @pl.when(self.has_up)
            def _():
                self.ag_send(bank, part, z, px, py, w, self.up)

            @pl.when(self.has_down)
            def _():
                self.ag_send(bank, part, z, px, py, w, self.down)

        def send(part, f, fc, lc, z, kind, axis):
            px, py = self.place(f, fc, lc)
            self.ag_send(bank, part, z, px, py, kind, self.near[axis])

        for part, big, f, l, fo, lo in steps:
            if big:
                send(part, f, fo, lo, self.z, 2, f)
            z_sends(part, f, fo, lo, 0)
        for part, big, f, l, fo, lo in steps:
            if not big:
                send(part, f, fo, lo, self.z, 2, f)
            send(part, f, fo, lo, self.z, 3, l)
        yield
        for part, big, f, l, fo, lo in steps:
            px, py = self.place(f, 1 - fo, lo)
            if big:
                self.ag_wait(bank, part, self.z, px, py)
                z_sends(part, f, 1 - fo, lo, 1)
                send(part, f, 1 - fo, lo, self.z, 3, l)
                yield
        for d in range(1, A):
            for part, big, f, l, fo, lo in steps:
                for w in (0, 1) if big else (0,):
                    fc = fo if w == 0 else 1 - fo
                    px, py = self.place(f, fc, lo)

                    def arrived(z, on, device):
                        self.ag_wait(bank, part, z, px, py)

                        @pl.when(on)
                        def _():
                            self.ag_send(bank, part, z, px, py, w, device)

                        if not big:
                            send(part, f, fc, lo, z, 2, f)
                        send(part, f, fc, lo, z, 3, l)

                    @pl.when(self.z >= d)
                    def _():
                        arrived(self.z - d, self.has_up, self.up)

                    @pl.when(self.z + d < A)
                    def _():
                        arrived(self.z + d, self.has_down, self.down)

                    yield
            for part, big, f, l, fo, lo in steps:
                if not big:
                    px, py = self.place(f, 1 - fo, lo)

                    def crossed(z):
                        self.ag_wait(bank, part, z, px, py)
                        send(part, f, 1 - fo, lo, z, 3, l)

                    if d == 1:
                        crossed(self.z)

                    @pl.when(self.z >= d)
                    def _():
                        crossed(self.z - d)

                    @pl.when(self.z + d < A)
                    def _():
                        crossed(self.z + d)

                    yield
        for z in range(A):
            for part, big, f, l, fo, lo in steps:
                for w in (0, 1):
                    px, py = self.place(f, w, 1 - lo)
                    self.ag_wait(bank, part, z, px, py)
            yield

    def ag_drain(self, bank):
        A = self.A
        base = bank * 2 * A
        for part, (order, _, rows) in enumerate(self.parts):
            big = order[0] != "z"

            def sent(kind, count):
                ref = self.wb.at[base : base + count, :, pl.ds(0, rows), :]
                slot = (bank * len(self.parts) + part) * 4 + kind
                self.remote(ref, ref, self.ag_s.at[slot], self.ag_r.at[0], self.sib).wait_send()

            inner = jnp.logical_and(self.has_up, self.has_down)
            for kind in (0, 1) if big else (0,):

                @pl.when(inner)
                def _():
                    sent(kind, A + 1)

                @pl.when(jnp.logical_not(inner))
                def _():
                    sent(kind, 1)

            sent(2, 1 if big else A)
            sent(3, 2 * A)


    def turn(self, j):
        A = self.A
        mirrored = self.z >= A // 2
        w = jnp.where(mirrored, A - 1 - self.z, self.z)
        d = jnp.where(j < A - 1 - w, A - 1 - j, jnp.where(j < A - 1, j - (A - 1 - w), w))
        return jnp.where(mirrored, A - 1 - d, d)

    def rs_land(self, part, slot):
        return self.land[part].at[slot]

    def rs_index(self, part, slot):
        return sum(slots_of(order, self.A) for order, _, _ in self.parts[:part]) + slot

    def rs_send(self, bank, part, z, x, y, slot, kind, device):
        sem = (bank * len(self.parts) + part) * 4 + kind
        self.remote(
            self.spot(bank, part, z, x, y),
            self.rs_land(part, slot),
            self.rs_s.at[sem],
            self.rs_r.at[self.rs_index(part, slot)],
            device,
        ).start()

    def rs_wait(self, part, slot):
        ref = self.rs_land(part, slot)
        self.remote(ref, ref, self.rs_s.at[0], self.rs_r.at[self.rs_index(part, slot)], self.sib).wait_recv()

    def rs_add(self, bank, part, z, x, y, slot, out=None):
        self.rs_wait(part, slot)
        order, start, rows = self.parts[part]
        at = bank * 2 * self.A + z * 2 + x
        row = pl.multiple_of(y * self.R + start, SUB)

        @pl.loop(0, 2)
        def _(h):
            total = self.wb[at, h, pl.ds(row, rows), :].astype(F32) + self.land[part][slot, h].astype(F32)
            if out is None:
                self.wb[at, h, pl.ds(row, rows), :] = total.astype(BF)
            else:
                out[h, start : start + rows, :] = total

    def rs_first(self, bank, z):
        for part, (order, _, _) in enumerate(self.parts):
            l = order[2]
            f = "x" if l == "y" else "y"
            for w in (0, 1):
                px, py = self.place(f, w, 1 - self.own(l))
                self.rs_send(bank, part, z, px, py, z * 2 + w, 3, self.near[l])

    def rs(self, bank, out):
        A = self.A
        info = []
        for part, (order, _, _) in enumerate(self.parts):
            l = order[2]
            f = "x" if l == "y" else "y"
            info.append((part, order[0] != "z", f, l, self.own(f), self.own(l)))

        def chain(part, big, f, fc, lo, w, z, final):
            base = 2 * A + w * (A + 1) if big else 3 * A
            px, py = self.place(f, fc, lo)
            goes_up, goes_down = z > self.z, z < self.z

            def onward(device, next_z, up):
                slot = base + jnp.where(z == next_z, A if not up else z, z)
                self.rs_send(bank, part, z, px, py, slot, w, device)

            @pl.when(goes_up)
            def _():
                @pl.when(self.has_down)
                def _():
                    self.rs_add(bank, part, z, px, py, base + z)

                onward(self.up, self.z + 1, True)

            @pl.when(goes_down)
            def _():
                @pl.when(self.has_up)
                def _():
                    self.rs_add(bank, part, z, px, py, base + z)

                onward(self.down, self.z - 1, False)

            @pl.when(z == self.z)
            def _():
                ends = jnp.logical_and(self.has_down, self.has_up)

                @pl.when(ends)
                def _():
                    self.rs_add(bank, part, z, px, py, base + z)
                    self.rs_add(bank, part, z, px, py, base + A, final)

                @pl.when(jnp.logical_not(ends))
                def _():
                    self.rs_add(bank, part, z, px, py, base + jnp.where(self.has_down, z, A), final)

        for j in range(A):
            z = self.turns[j]
            for part, big, f, l, fo, lo in info:
                for w in (1, 0):
                    fc = fo if w == 0 else 1 - fo
                    px, py = self.place(f, fc, lo)
                    self.rs_add(bank, part, z, px, py, z * 2 + fc)
                    if big:
                        chain(part, big, f, fc, lo, w, z, None)
                    elif w == 1:
                        self.rs_send(bank, part, z, px, py, 2 * A + z, 2, self.near[f])
                    if big:
                        yield
                if not big:
                    yield
            for part, big, f, l, fo, lo in info:
                if not big:
                    px, py = self.place(f, fo, lo)
                    self.rs_add(bank, part, z, px, py, 2 * A + z)
                    chain(part, big, f, fo, lo, 0, z, out if j == A - 1 else None)
                    yield
        for part, big, f, l, fo, lo in info:
            if big:
                px, py = self.place(f, 1 - fo, lo)
                self.rs_send(bank, part, self.z, px, py, 4 * A + 2, 2, self.near[f])
        yield
        for part, big, f, l, fo, lo in info:
            if big:
                px, py = self.place(f, fo, lo)
                self.rs_add(bank, part, self.z, px, py, 4 * A + 2, out)
                yield

    def rs_drain(self, bank):
        A = self.A
        base = bank * 2 * A
        for part, (order, _, rows) in enumerate(self.parts):
            big = order[0] != "z"

            def sent(kind, count):
                ref = self.wb.at[base : base + count, :, pl.ds(0, rows), :]
                slot = (bank * len(self.parts) + part) * 4 + kind
                self.remote(ref, ref, self.rs_s.at[slot], self.rs_r.at[0], self.sib).wait_send()

            sent(0, A - 1)
            if big:
                sent(1, A - 1)
            sent(2, 1 if big else A)
            sent(3, 2 * A)


    def share(self, ref, k):
        rows = ref.at[pl.ds(pl.multiple_of(self.c * self.T, SUB), self.T), :]
        copy = self.remote(rows, rows, self.cg_s.at[k], self.cg_r.at[k], self.sib)
        copy.start()
        return copy

    def shared(self, ref, k):
        rows = ref.at[pl.ds(pl.multiple_of((1 - self.c) * self.T, SUB), self.T), :]
        mine = ref.at[pl.ds(pl.multiple_of(self.c * self.T, SUB), self.T), :]
        self.remote(rows, rows, self.cg_s.at[k], self.cg_r.at[k], self.sib).wait_recv()
        self.remote(mine, mine, self.cg_s.at[k], self.cg_r.at[k], self.sib).wait_send()

    def rows_of(self, which):
        return pl.ds(pl.multiple_of(which * self.T, SUB), self.T)

    def give(self, k, halves):
        buf = k % 2
        for h, value in enumerate(halves(self.rows_of(1 - self.c))):
            self.sb[buf, :, h * TILE : (h + 1) * TILE] = value.astype(BF)
        self.remote(self.sb.at[buf], self.rb.at[buf], self.ex_s.at[k], self.ex_r.at[k], self.sib).start()
        for h, value in enumerate(halves(self.rows_of(self.c))):
            self.pacc[:, h * TILE : (h + 1) * TILE] = value

    def taken(self, k):
        buf = k % 2
        self.remote(self.sb.at[buf], self.rb.at[buf], self.ex_s.at[k], self.ex_r.at[k], self.sib).wait()


    def wcol(self, b):
        return self.wb[pl.ds(b * self.nzx, self.nzx)].reshape(self.D, TILE)

    def wrow(self, b, h):
        return self.wb[pl.ds(b * self.nzx, self.nzx), h].reshape(TILE, TILE)

    def win(self, j, h):
        return self.wb[pl.ds(2 * self.A + j * self.nt, self.nt), h].reshape(TILE, TILE)

    def wout(self, j, h):
        return self.wb[pl.ds(3 * self.A + j * self.nt, self.nt), h].reshape(TILE, TILE)

    def project(self, dst, first, source, block, count):
        @pl.loop(0, count)
        def _(i):
            weight = self.wcol(block + i)
            for m in range(2):
                rows = slice(m * self.T, (m + 1) * self.T)
                dst[first + i, rows, :] = dot(source[rows, :], weight).astype(BF)


    def masks(self):
        lane = lax.broadcasted_iota(jnp.int32, (1, PAIR), 1)
        row = lax.broadcasted_iota(jnp.int32, (PAIR, 1), 0)
        return [(lane < HD), (lane >= HD)], (row < HD)

    def visible(self, tile):
        T = self.T
        key = lax.broadcasted_iota(jnp.int32, (2 * T, T), 0)
        query = lax.broadcasted_iota(jnp.int32, (2 * T, T), 1) + tile * T
        edge = self.pfx_now[0:1, 0:1]
        return jnp.logical_or(key <= query, key.astype(F32) < edge)

    def attend(self, p, qkv, o, lse, masked):
        T = self.T
        cols = pl.ds(pl.multiple_of(p * PAIR, PAIR), PAIR)
        heads, upper = self.masks()
        keys = qkv[1, :, cols]
        values_t = turned(qkv[2, :, cols])
        for tile in range(2):
            rows = slice(tile * T, (tile + 1) * T)
            query = qkv[0, rows, cols].astype(F32) * score_scale
            vis = self.visible(tile) if masked else None
            mixed = []
            for h in range(2):
                scores = dot_nt(keys, jnp.where(heads[h], query, 0.0).astype(BF))
                if masked:
                    scores = jnp.where(vis, scores, masked_score)
                highest = jnp.max(scores, axis=0, keepdims=True)
                exponent = jnp.exp(scores - highest)
                total = jnp.sum(exponent, axis=0, keepdims=True)
                lse[p, h : h + 1, rows] = highest + jnp.log(total)
                mixed.append(dot(values_t, exponent.astype(BF)) * (1.0 / total))
            o[rows, cols] = jnp.where(upper, mixed[0], mixed[1]).T.astype(BF)

    def attend_back(self, p, qkv, do, lse, masked):
        T = self.T
        cols = pl.ds(pl.multiple_of(p * PAIR, PAIR), PAIR)
        heads, upper = self.masks()
        keys, values = qkv[1, :, cols], qkv[2, :, cols]
        keys_t = turned(keys)
        dk = [0.0, 0.0]
        dv = [0.0, 0.0]
        for tile in range(2):
            rows = slice(tile * T, (tile + 1) * T)
            query = qkv[0, rows, cols]
            grad = do[rows, cols]
            query_wide = query.astype(F32) * score_scale
            grad_wide = grad.astype(F32)
            vis = self.visible(tile) if masked else None
            dq = []
            for h in range(2):
                scores = dot_nt(keys, jnp.where(heads[h], query_wide, 0.0).astype(BF))
                if masked:
                    scores = jnp.where(vis, scores, masked_score)
                probs = jnp.exp(scores - lse[p, h : h + 1, rows])
                dprobs = dot_nt(values, jnp.where(heads[h], grad_wide, 0.0).astype(BF))
                delta = jnp.sum(dprobs * probs, axis=0, keepdims=True)
                dscores = (probs * (dprobs - delta)).astype(BF)
                dq.append(dot(keys_t, dscores))
                dk[h] += dot(dscores, query)
                dv[h] += dot(probs.astype(BF), grad)
            self.dqkv[0, rows, cols] = (jnp.where(upper, dq[0], dq[1]) * score_scale).T.astype(BF)
        self.dqkv[1, :, cols] = (jnp.where(heads[0], dk[0], dk[1]) * score_scale).astype(BF)
        self.dqkv[2, :, cols] = jnp.where(heads[0], dv[0], dv[1]).astype(BF)


    def norm(self, summed):
        centred = summed - jnp.mean(summed, axis=-1, keepdims=True)
        inv = lax.rsqrt(jnp.mean(centred * centred, axis=-1, keepdims=True) + norm_eps)
        return centred * inv, inv

    def norm_back(self, k, dy, normed, inv):
        gain = self.norms[k : k + 1, :]
        self.ng[k : k + 1, :] += jnp.sum(dy * normed, axis=0, keepdims=True)
        self.ng[3 + k : 4 + k, :] += jnp.sum(dy, axis=0, keepdims=True)
        scaled = dy * gain
        plain = jnp.mean(scaled, axis=-1, keepdims=True)
        along = jnp.mean(scaled * normed, axis=-1, keepdims=True)
        return inv * (scaled - plain - normed * along)

    def norm_rows(self, body):
        @pl.loop(0, self.T // LN_ROWS)
        def _(i):
            own = pl.ds(pl.multiple_of(i * LN_ROWS, LN_ROWS), LN_ROWS)
            full = pl.ds(pl.multiple_of(self.c * self.T + i * LN_ROWS, LN_ROWS), LN_ROWS)
            body(own, full)


def pump(steps, count):
    for _ in range(count):
        next(steps, None)


def finish(steps):
    for _ in steps:
        pass


def in_loop(steps, index, turns, count):
    for turn in range(turns):

        @pl.when(index == turn)
        def _():
            pump(steps, count)


def kernel(A, R, T, parts, names, *arrays):
    s = Layer(A, R, T, parts, dict(zip(names, arrays)))
    s.land = [getattr(s, f"land{i}") for i in range(len(parts))]
    D = s.D
    away = jnp.logical_not(s.kept)
    s.ng[...] = jnp.zeros_like(s.ng)
    s.barrier()

    block = s.zx // s.nzx
    by_rows = jnp.logical_or(block == 3, block == 7)
    mine = pl.ds(pl.multiple_of(s.y * R, SUB), R)
    ffn_copy = pltpu.make_async_copy(s.ffn_piece, s.wb.at[2 * A + s.zx, :, mine, :], s.lc.at[0])
    ffn_copy.start()
    rows_copy = pltpu.make_async_copy(s.attn_piece, s.wb.at[s.zx, :, mine, :], s.lc.at[1])
    half_copy = pltpu.make_async_copy(s.attn_piece.at[s.c], s.wb.at[s.zx, s.c, mine, :], s.lc.at[2])
    half_send = s.remote(
        s.attn_piece.at[1 - s.c], s.wb.at[s.zx, s.c, mine, :], s.misc_s.at[0], s.misc_r.at[0], s.sib
    )
    half_recv = s.remote(
        s.attn_piece.at[1 - s.c], s.wb.at[s.zx, 1 - s.c, mine, :], s.misc_s.at[0], s.misc_r.at[0], s.sib
    )

    @pl.when(by_rows)
    def _():
        rows_copy.start()

    @pl.when(jnp.logical_not(by_rows))
    def _():
        half_copy.start()
        half_send.start()

    here = s.rows_of(s.c)
    there = s.rows_of(s.y)
    swaps = [
        (s.tokens, s.xf.at[here, :], s.xf.at[there, :]),
        (s.memory, s.mf.at[here, :], s.mf.at[there, :]),
        (s.pfx, s.pfx_now, s.pfx_now),
        (s.cot, s.cotb, s.cotb),
    ]

    @pl.when(s.kept)
    def _():
        for i, (src, dst, _) in enumerate(swaps):
            pltpu.make_async_copy(src, dst, s.lc.at[3 + i]).start()

    @pl.when(away)
    def _():
        for i, (src, _, dst) in enumerate(swaps):
            s.remote(src, dst, s.sw_s.at[i], s.sw_r.at[i], s.partner).start()

    @pl.when(by_rows)
    def _():
        rows_copy.wait()

    @pl.when(jnp.logical_not(by_rows))
    def _():
        half_copy.wait()
        half_send.wait_send()
        half_recv.wait_recv()

    gather = s.ag(0)
    next(gather)

    def swapped(i):
        src, dst, far = swaps[i]

        @pl.when(s.kept)
        def _():
            pltpu.make_async_copy(src, dst, s.lc.at[3 + i]).wait()

        @pl.when(away)
        def _():
            s.remote(src, far, s.sw_s.at[i], s.sw_r.at[i], s.partner).wait_send()
            s.remote(src, dst, s.sw_s.at[i], s.sw_r.at[i], s.partner).wait_recv()

    pump(gather, 4)
    swapped(0)
    s.share(s.xf, 0)
    swapped(1)
    s.share(s.mf, 1)
    swapped(2)
    pump(gather, 24)
    swapped(3)
    s.shared(s.xf, 0)
    s.shared(s.mf, 1)
    ffn_copy.wait()
    ffn = s.ag(1)
    next(ffn)
    finish(gather)

    s.project(s.qkv1, 0, s.xf, 0, 3)
    pump(ffn, 2)
    s.project(s.qkv2, 1, s.mf, 5, 2)
    pump(ffn, 2)

    @pl.loop(0, TILE // PAIR)
    def _(p):
        s.attend(p, s.qkv1, s.o1, s.lse1, True)
        in_loop(ffn, p, TILE // PAIR, 3)

    def branch(o, b):
        return lambda rows: [dot(o[rows, :], s.wrow(b, h)) for h in range(2)]

    s.give(0, branch(s.o1, 3))
    pump(ffn, 1)
    s.taken(0)

    def first_norm(own, full):
        summed = alpha_scale * s.xf[full, :].astype(F32) + s.pacc[own, :] + s.rb[0, own, :].astype(F32)
        normed, inv = s.norm(summed)
        s.dtok[own, :] = normed
        s.inv1[own, :] = inv
        result = normed * s.norms[0:1, :] + s.norms[3:4, :]
        s.nbuf[own, :] = result
        s.n1r[full, :] = result.astype(BF)

    s.norm_rows(first_norm)
    s.share(s.n1r, 2)
    pump(ffn, 2)
    s.shared(s.n1r, 2)

    s.project(s.qkv2, 0, s.n1r, 4, 1)

    @pl.loop(0, TILE // PAIR)
    def _(p):
        s.attend(p, s.qkv2, s.o2, s.lse2, False)
        in_loop(ffn, p, TILE // PAIR, 3)

    s.give(1, branch(s.o2, 7))
    pump(ffn, 1)
    s.taken(1)

    def second_norm(own, full):
        summed = alpha_scale * s.nbuf[own, :] + s.pacc[own, :] + s.rb[1, own, :].astype(F32)
        normed, inv = s.norm(summed)
        s.dmem[own, :] = normed
        s.inv2[own, :] = inv
        result = normed * s.norms[1:2, :] + s.norms[4:5, :]
        s.nbuf[own, :] = result
        s.n2r[full, :] = result.astype(BF)

    s.norm_rows(second_norm)
    s.share(s.n2r, 3)
    pump(ffn, 2)
    s.shared(s.n2r, 3)
    finish(ffn)

    tiles = 2 * A * R // TILE

    @pl.loop(0, tiles)
    def _(j):
        for m in range(2):
            rows = slice(m * T, (m + 1) * T)
            pre = dot_nt(s.n2r[rows, :TILE], s.win(j, 0)) + dot_nt(s.n2r[rows, TILE:], s.win(j, 1))
            gate = 1.0 / (1.0 + jnp.exp(-pre))
            s.act[tiles + j, rows, :] = (pre * gate).astype(BF)
            s.act[j, rows, :] = (gate * (1.0 + pre * (1.0 - gate))).astype(BF)

    def ffn_out(rows):
        return [sum(dot(s.act[tiles + j, rows, :], s.wout(j, h)) for j in range(tiles)) for h in range(2)]

    s.give(2, ffn_out)
    s.taken(2)

    def third_norm(own, full):
        summed = alpha_scale * s.nbuf[own, :] + s.pacc[own, :] + s.rb[0, own, :].astype(F32)
        normed, inv = s.norm(summed)
        result = normed * s.norms[2:3, :] + s.norms[5:6, :]
        s.out[own, :] = result
        s.osb[0, own, :] = result.astype(BF)
        grad = s.norm_back(2, s.cotb[own, :].astype(F32), normed, inv)
        s.nbuf[own, :] = grad
        s.ga[full, :] = grad.astype(BF)

    s.norm_rows(third_norm)
    s.share(s.ga, 4)

    def send_back(k):
        @pl.when(away)
        def _():
            s.remote(s.osb.at[k], s.orb.at[k], s.ob_s.at[k], s.ob_r.at[k], s.partner).start()

    send_back(0)
    s.ag_drain(0)
    s.ag_drain(1)
    s.shared(s.ga, 4)

    @pl.loop(0, tiles)
    def _(j):
        for m in range(2):
            rows = slice(m * T, (m + 1) * T)
            da = dot_nt(s.ga[rows, :TILE], s.wout(j, 0)) + dot_nt(s.ga[rows, TILE:], s.wout(j, 1))
            s.act[j, rows, :] = (da * s.act[j, rows, :].astype(F32)).astype(BF)

    def ffn_in(rows):
        return [sum(dot(s.act[j, rows, :], s.win(j, h)) for j in range(tiles)) for h in range(2)]

    s.give(3, ffn_in)

    @pl.loop(0, tiles)
    def _(j):
        hidden, grads = s.act[tiles + j], s.act[j]
        for h in range(2):
            cols = slice(h * TILE, (h + 1) * TILE)
            out_rows = dot_tn(hidden, s.ga[:, cols]).astype(BF)
            s.wb[pl.ds(3 * A + j * s.nt, s.nt), h] = out_rows.reshape(s.nt, 2 * R, TILE)
            in_rows = dot_tn(grads, s.n2r[:, cols]).astype(BF)
            s.wb[pl.ds(2 * A + j * s.nt, s.nt), h] = in_rows.reshape(s.nt, 2 * R, TILE)

    for j in range(A):
        s.rs_first(1, s.turns[j])
    spread = s.rs(1, s.dffn)
    s.taken(3)

    def second_back(own, full):
        dy = alpha_scale * s.nbuf[own, :] + s.pacc[own, :] + s.rb[1, own, :].astype(F32)
        grad = s.norm_back(1, dy, s.dmem[own, :], s.inv2[own, :])
        s.nbuf[own, :] = grad
        s.gb[full, :] = grad.astype(BF)

    s.norm_rows(second_back)
    s.share(s.gb, 5)
    pump(spread, 2)
    s.shared(s.gb, 5)

    def mixed_back(grad, o, b):
        for m in range(2):
            rows = slice(m * T, (m + 1) * T)
            s.do[rows, :] = (
                dot_nt(grad[rows, :TILE], s.wrow(b, 0)) + dot_nt(grad[rows, TILE:], s.wrow(b, 1))
            ).astype(BF)
        for h in range(2):
            cols = slice(h * TILE, (h + 1) * TILE)
            terms = dot_tn(o[...], grad[:, cols]).astype(BF)
            s.wb[pl.ds(b * s.nzx, s.nzx), h] = terms.reshape(s.nzx, 2 * R, TILE)

    def weight_terms(b, source, grad):
        for h in range(2):
            cols = slice(h * TILE, (h + 1) * TILE)
            terms = dot_tn(source[:, cols], grad).astype(BF)
            half = s.nzx // 2 if s.nzx > 1 else 0
            if half:
                s.wb[pl.ds(b * s.nzx + h * half, half)] = terms.reshape(half, 2, 2 * R, TILE)
            else:
                s.wb[b, h] = terms

    def spread_back(rows, blocks):
        halves = []
        for h in range(2):
            total = 0.0
            for b, k in blocks:
                total += dot_nt(s.dqkv[k, rows, :], s.wcol(b)[h * TILE : (h + 1) * TILE])
            halves.append(total)
        return halves

    mixed_back(s.gb, s.o2, 7)
    pump(spread, 2)

    @pl.loop(0, TILE // PAIR)
    def _(p):
        s.attend_back(p, s.qkv2, s.do, s.lse2, False)
        in_loop(spread, p, TILE // PAIR, 3)

    s.give(4, lambda rows: spread_back(rows, [(5, 1), (6, 2)]))
    pump(spread, 1)
    s.taken(4)

    def memory_rows(own, full):
        total = s.pacc[own, :] + s.rb[0, own, :].astype(F32)
        s.dmem[own, :] = total
        s.osb[1, own, :] = total.astype(BF)

    s.norm_rows(memory_rows)
    send_back(1)
    s.give(5, lambda rows: spread_back(rows, [(4, 0)]))
    pump(spread, 1)
    weight_terms(4, s.n1r, s.dqkv[0])
    weight_terms(5, s.mf, s.dqkv[1])
    weight_terms(6, s.mf, s.dqkv[2])
    pump(spread, 1)
    s.taken(5)

    def first_back(own, full):
        dy = alpha_scale * s.nbuf[own, :] + s.pacc[own, :] + s.rb[1, own, :].astype(F32)
        grad = s.norm_back(0, dy, s.dtok[own, :], s.inv1[own, :])
        s.nbuf[own, :] = grad
        s.ga[full, :] = grad.astype(BF)

    s.norm_rows(first_back)
    s.share(s.ga, 6)
    pump(spread, 2)
    s.shared(s.ga, 6)

    def norm_sum():
        for k, device in enumerate((s.sib, s.near["x"], s.near["y"])):
            copy = s.remote(s.ngs.at[k], s.ngr.at[k], s.nm_s.at[k], s.nm_r.at[k], device)
            s.ngs[k] = s.ng[...]
            copy.start()
            yield
            copy.wait()
            s.ng[...] = s.ng[...] + s.ngr[k]
        s.ngz[s.z] = s.ng[...]
        for other in range(A):

            @pl.when(s.z != other)
            def _():
                s.remote(
                    s.ng, s.ngz.at[s.z], s.nm_s.at[3 + other], s.nm_r.at[3 + s.z],
                    (s.dp + 4 * (other - s.z), s.y),
                ).start()

        yield
        for other in range(A):

            @pl.when(s.z != other)
            def _():
                s.remote(s.ng, s.ngz.at[other], s.nm_s.at[3 + other], s.nm_r.at[3 + other], s.sib).wait()

        total = s.ngz[0]
        for other in range(1, A):
            total = total + s.ngz[other]
        s.dnorm[...] = total[:6, :]
        yield

    sums = norm_sum()
    next(sums)

    mixed_back(s.ga, s.o1, 3)
    pump(spread, 2)
    next(sums)

    @pl.loop(0, TILE // PAIR)
    def _(p):
        s.attend_back(p, s.qkv1, s.do, s.lse1, True)
        in_loop(spread, p, TILE // PAIR, 4)

    next(sums)
    s.give(6, lambda rows: spread_back(rows, [(0, 0), (1, 1), (2, 2)]))
    next(sums)

    @pl.loop(0, 3)
    def _(k):
        weight_terms(k, s.xf, s.dqkv[k])

    finish(sums)
    s.taken(6)

    def token_rows(own, full):
        total = alpha_scale * s.nbuf[own, :] + s.pacc[own, :] + s.rb[0, own, :].astype(F32)
        s.dtok[own, :] = total
        s.osb[2, own, :] = total.astype(BF)

    s.norm_rows(token_rows)
    send_back(2)
    finish(spread)

    for k, device in enumerate((s.near["x"], s.near["y"])):
        pl.semaphore_signal(s.credit.at[k], inc=1, device_id=device, device_id_type=MESH)

    @pl.when(s.has_up)
    def _():
        pl.semaphore_signal(s.credit.at[2], inc=1, device_id=s.up, device_id_type=MESH)

    @pl.when(s.has_down)
    def _():
        pl.semaphore_signal(s.credit.at[3], inc=1, device_id=s.down, device_id_type=MESH)

    pl.semaphore_wait(s.credit.at[0], 1)
    pl.semaphore_wait(s.credit.at[1], 1)

    @pl.when(s.has_down)
    def _():
        pl.semaphore_wait(s.credit.at[2], 1)

    @pl.when(s.has_up)
    def _():
        pl.semaphore_wait(s.credit.at[3], 1)

    for j in range(A):
        s.rs_first(0, s.turns[j])

    @pl.when(away)
    def _():
        for k, dst in enumerate((s.out, s.dmem, s.dtok)):
            s.remote(s.osb.at[k], s.orb.at[k], s.ob_s.at[k], s.ob_r.at[k], s.partner).wait()

            @pl.loop(0, T // LN_ROWS)
            def _(i):
                own = pl.ds(pl.multiple_of(i * LN_ROWS, LN_ROWS), LN_ROWS)
                dst[own, :] = s.orb[k, own, :].astype(F32)

    finish(s.rs(0, s.fin))

    tail_send = s.remote(s.fin.at[1 - s.c], s.dattn.at[s.c], s.misc_s.at[1], s.misc_r.at[1], s.sib)
    tail_recv = s.remote(s.fin.at[1 - s.c], s.dattn.at[1 - s.c], s.misc_s.at[1], s.misc_r.at[1], s.sib)

    @pl.when(by_rows)
    def _():
        s.dattn[...] = s.fin[...]

    @pl.when(jnp.logical_not(by_rows))
    def _():
        tail_send.start()
        s.dattn[s.c] = s.fin[s.c]
        tail_send.wait_send()
        tail_recv.wait_recv()

    s.rs_drain(1)
    s.rs_drain(0)


def on_device(A, tokens, memory, attn_bank, ffn_bank, norm_params, prefix, cotangent):
    T, D = tokens.shape
    R = attn_bank.shape[0]
    parts = cut(R)
    groups = D // (4 * R)
    tiles = 2 * A * R // TILE

    def by_half(shard):
        return shard.reshape(R, 2, TILE).transpose(1, 0, 2)

    def by_core(shard):
        return shard.reshape(R, groups, 2, 2 * R).transpose(2, 0, 1, 3).reshape(2, R, TILE)

    block = (lax.axis_index("dp") // 2) // groups
    by_rows = jnp.logical_or(block == 3, block == 7)
    attn_piece = by_half(attn_bank)
    if groups > 1:
        attn_piece = jnp.where(by_rows, attn_piece, by_core(attn_bank))
    pfx = jnp.broadcast_to(prefix.astype(F32)[0], (8, 128))
    np_ = len(parts)
    slots = sum(slots_of(order, A) for order, _, _ in parts)

    inputs = dict(
        tokens=tokens,
        memory=memory,
        cot=cotangent,
        pfx=pfx,
        attn_piece=attn_piece,
        ffn_piece=by_half(ffn_bank),
        norms=norm_params,
    )
    in_vmem = ("pfx", "norms")
    outputs = dict(
        out=(T, D), dtok=(T, D), dmem=(T, D), dattn=(2, R, TILE), dffn=(2, R, TILE), dnorm=(6, D)
    )
    wide = lambda *shape: pltpu.VMEM(shape, F32)
    low = lambda *shape: pltpu.VMEM(shape, BF)
    dma = lambda count: pltpu.SemaphoreType.DMA((count,))
    scratch = dict(
        wb=low(4 * A, 2, 2 * R, TILE),
        xf=low(2 * T, D),
        mf=low(2 * T, D),
        n1r=low(2 * T, D),
        n2r=low(2 * T, D),
        ga=low(2 * T, D),
        gb=low(2 * T, D),
        cotb=low(T, D),
        act=low(2 * tiles, 2 * T, TILE),
        qkv1=low(3, 2 * T, TILE),
        qkv2=low(3, 2 * T, TILE),
        dqkv=low(3, 2 * T, TILE),
        o1=low(2 * T, TILE),
        o2=low(2 * T, TILE),
        do=low(2 * T, TILE),
        sb=low(2, T, D),
        rb=low(2, T, D),
        osb=low(3, T, D),
        orb=low(3, T, D),
        nbuf=wide(T, D),
        pacc=wide(T, D),
        fin=wide(2, R, TILE),
        pfx_now=wide(8, 128),
        lse1=wide(TILE // PAIR, 8, 2 * T),
        lse2=wide(TILE // PAIR, 8, 2 * T),
        inv1=wide(T, 1),
        inv2=wide(T, 1),
        ng=wide(8, D),
        ngs=wide(3, 8, D),
        ngr=wide(3, 8, D),
        ngz=wide(A, 8, D),
        lc=dma(7),
        misc_s=dma(2),
        misc_r=dma(2),
        sw_s=dma(4),
        sw_r=dma(4),
        ag_s=dma(2 * np_ * 4),
        ag_r=dma(2 * np_ * 4 * A),
        rs_s=dma(2 * np_ * 4),
        rs_r=dma(slots),
        cg_s=dma(7),
        cg_r=dma(7),
        ex_s=dma(7),
        ex_r=dma(7),
        ob_s=dma(3),
        ob_r=dma(3),
        nm_s=dma(3 + A),
        nm_r=dma(3 + A),
        credit=pltpu.SemaphoreType.REGULAR((4,)),
    )
    for i, (order, _, rows) in enumerate(parts):
        scratch[f"land{i}"] = low(slots_of(order, A), 2, rows, TILE)
    names = list(inputs) + list(outputs) + list(scratch)
    out, dtok, dmem, dattn, dffn, dnorm = pl.pallas_call(
        functools.partial(kernel, A, R, T, parts, names),
        out_shape=[jax.ShapeDtypeStruct(shape, F32) for shape in outputs.values()],
        in_specs=[pl.BlockSpec(memory_space=pltpu.VMEM if n in in_vmem else pl.ANY) for n in inputs],
        out_specs=[pl.BlockSpec(memory_space=pltpu.VMEM)] * len(outputs),
        scratch_shapes=list(scratch.values()),
        compiler_params=pltpu.CompilerParams(
            collective_id=0, has_side_effects=True, vmem_limit_bytes=64 * 2**20
        ),
        name="layer",
    )(*inputs.values())

    def half_back(pieces):
        return pieces.transpose(1, 0, 2).reshape(R, D)

    def core_back(pieces):
        return pieces.reshape(2, R, groups, 2 * R).transpose(1, 2, 0, 3).reshape(R, D)

    attn_rows = half_back(dattn)
    if groups > 1:
        attn_rows = jnp.where(by_rows, attn_rows, core_back(dattn))
    return (out, dtok, dmem, attn_rows, half_back(dffn), dnorm)


def solution(mesh):
    rows = P(("dp", "seq"), None)
    return jax.shard_map(
        functools.partial(on_device, mesh.shape["dp"] // 4),
        mesh=mesh,
        in_specs=(rows, rows, rows, rows, P(), P("dp"), rows),
        out_specs=(rows, rows, rows, rows, rows, P()),
        check_vma=False,
    )
```

```python
import functools

import jax
import jax.numpy as jnp
from jax import lax
from jax.experimental import pallas as pl
from jax.experimental.pallas import tpu as pltpu
from jax.sharding import PartitionSpec as P

HD = 64
PAIR = 2 * HD
TILE = 512
SUB = 16
LN_ROWS = 32
AHEAD = 8
GATHER = (5, 5, 3, 3)
SCATTER = (5, 5, 3, 3)

alpha_scale = 300.0**0.25
norm_eps = 1e-05
masked_score = -1e30
score_scale = HD**-0.5

BF = jnp.bfloat16
F32 = jnp.float32
MESH = pl.DeviceIdType.MESH


def dot(left, right):
    return jnp.dot(left, right, preferred_element_type=F32)


def dot_nt(left, right):
    return lax.dot_general(left, right, (((1,), (1,)), ((), ())), preferred_element_type=F32)


def dot_tn(left, right):
    return lax.dot_general(left, right, (((0,), (0,)), ((), ())), preferred_element_type=F32)


def turned(block):
    return block.astype(F32).T.astype(BF)


def cut(rows, split):
    units = rows // SUB
    shares = [(units * share + 8) // 16 for share in split[1:]]
    sizes = list(zip(("xzy", "yzx", "zxy", "zyx"), [units - sum(shares)] + shares))
    parts, start = [], 0
    for order, size in sizes:
        if size > 0:
            parts.append((order, start * SUB, size * SUB))
        start += size
    return parts


def slots_of(order, A):
    return 4 * A + 3 if order[0] != "z" else 4 * A + 1


class Layer:
    def __init__(self, A, R, T, ag_parts, rs_parts, refs):
        self.A, self.R, self.T = A, R, T
        self.ag_parts, self.rs_parts = ag_parts, rs_parts
        self.D = 1024
        self.nzx = self.D // (4 * R)
        self.nt = TILE // (2 * R)
        for name, ref in refs.items():
            setattr(self, name, ref)
        self.dp, self.y = lax.axis_index("dp"), lax.axis_index("seq")
        self.c = lax.rem(self.dp, 2)
        self.x = lax.rem(self.dp // 2, 2)
        self.z = self.dp // 4
        self.zx = self.dp // 2
        self.sib = (self.dp + 1 - 2 * self.c, self.y)
        self.near = {"x": (self.dp + 2 - 4 * self.x, self.y), "y": (self.dp, 1 - self.y)}
        self.up = (self.dp + 4, self.y)
        self.down = (self.dp - 4, self.y)
        self.partner = (self.dp - self.c + self.y, self.c)
        self.has_up = self.z < A - 1
        self.has_down = self.z > 0
        self.kept = self.c == self.y
        self.turns = [self.turn(j) for j in range(A)]


    def remote(self, src, dst, send, recv, device):
        return pltpu.make_async_remote_copy(
            src_ref=src, dst_ref=dst, send_sem=send, recv_sem=recv, device_id=device, device_id_type=MESH
        )

    def own(self, axis):
        return self.x if axis == "x" else self.y

    def spot(self, bank, part, z, x, y):
        order, start, rows = part
        row = pl.multiple_of(y * self.R + start, SUB)
        return self.wb.at[bank * 2 * self.A + z * 2 + x, :, pl.ds(row, rows), :]

    def place(self, axis, f, l):
        return (f, l) if axis == "x" else (l, f)


    def barrier(self):
        bar = pltpu.get_barrier_semaphore()

        def greet(device):
            pl.semaphore_signal(bar, inc=1, device_id=device, device_id_type=MESH)

        greet(self.sib)
        greet(self.near["x"])
        greet(self.near["y"])
        for other in range(self.A):

            @pl.when(self.z != other)
            def _():
                greet((self.dp + 4 * (other - self.z), self.y))

        @pl.when(jnp.logical_not(self.kept))
        def _():
            greet(self.partner)
            pl.semaphore_wait(bar, 3 + self.A)

        @pl.when(self.kept)
        def _():
            pl.semaphore_wait(bar, 2 + self.A)


    def ag_index(self, bank, part, z, x, y):
        return ((bank * len(self.ag_parts) + part) * 2 * self.A + z * 2 + x) * 2 + y

    def ag_send(self, bank, part, z, x, y, kind, device):
        ref = self.spot(bank, self.ag_parts[part], z, x, y)
        slot = (bank * len(self.ag_parts) + part) * 4 + kind
        self.remote(ref, ref, self.ag_s.at[slot], self.ag_r.at[self.ag_index(bank, part, z, x, y)], device).start()

    def ag_wait(self, bank, part, z, x, y):
        ref = self.spot(bank, self.ag_parts[part], z, x, y)
        self.remote(
            ref, ref, self.ag_s.at[0], self.ag_r.at[self.ag_index(bank, part, z, x, y)], self.sib
        ).wait_recv()

    def ag(self, bank):
        A = self.A
        info, steps = self.orders(self.ag_parts), []

        def z_sends(part, f, fc, lc, w):
            px, py = self.place(f, fc, lc)

            @pl.when(self.has_up)
            def _():
                self.ag_send(bank, part, self.z, px, py, w, self.up)

            @pl.when(self.has_down)
            def _():
                self.ag_send(bank, part, self.z, px, py, w, self.down)

        def send(part, f, fc, lc, z, kind, axis):
            px, py = self.place(f, fc, lc)
            self.ag_send(bank, part, z, px, py, kind, self.near[axis])

        def early():
            for part, big, f, l, fo, lo in info:
                if big:
                    send(part, f, fo, lo, self.z, 2, f)

        def begin():
            for part, big, f, l, fo, lo in info:
                z_sends(part, f, fo, lo, 0)
            for part, big, f, l, fo, lo in info:
                if not big:
                    send(part, f, fo, lo, self.z, 2, f)
                send(part, f, fo, lo, self.z, 3, l)

        def beside(part, big, f, l, fo, lo):
            px, py = self.place(f, 1 - fo, lo)
            self.ag_wait(bank, part, self.z, px, py)
            z_sends(part, f, 1 - fo, lo, 1)
            send(part, f, 1 - fo, lo, self.z, 3, l)

        def arrive(d, w, part, big, f, l, fo, lo):
            fc = fo if w == 0 else 1 - fo
            px, py = self.place(f, fc, lo)

            def arrived(z, on, device):
                self.ag_wait(bank, part, z, px, py)

                @pl.when(on)
                def _():
                    self.ag_send(bank, part, z, px, py, w, device)

                if not big:
                    send(part, f, fc, lo, z, 2, f)
                send(part, f, fc, lo, z, 3, l)

            @pl.when(self.z >= d)
            def _():
                arrived(self.z - d, self.has_up, self.up)

            @pl.when(self.z + d < A)
            def _():
                arrived(self.z + d, self.has_down, self.down)

        def cross(d, part, big, f, l, fo, lo):
            px, py = self.place(f, 1 - fo, lo)

            def crossed(z):
                self.ag_wait(bank, part, z, px, py)
                send(part, f, 1 - fo, lo, z, 3, l)

            self.planes_at(d, crossed)

        def end(d, w, part, big, f, l, fo, lo):
            px, py = self.place(f, w, 1 - lo)
            self.planes_at(d, lambda z: self.ag_wait(bank, part, z, px, py))

        bigs = [row for row in info if row[1]]
        smalls = [row for row in info if not row[1]]
        steps += [early, begin]
        for d in range(1, A):
            steps += [functools.partial(arrive, d, 0, *row) for row in info]
            if d == 1:
                steps += [functools.partial(beside, *row) for row in bigs]
            steps += [functools.partial(arrive, d, 1, *row) for row in bigs]
            steps += [functools.partial(cross, d - 1, *row) for row in smalls]
        steps += [functools.partial(cross, A - 1, *row) for row in smalls]
        for d in range(A):
            for row in info:
                for w in (0, 1):
                    steps.append(functools.partial(end, d, w, *row))
        return steps

    def planes_at(self, d, act):
        if d == 0:
            act(self.z)
            return

        @pl.when(self.z >= d)
        def _():
            act(self.z - d)

        @pl.when(self.z + d < self.A)
        def _():
            act(self.z + d)

    def orders(self, parts):
        info = []
        for part, (order, _, _) in enumerate(parts):
            l = order[2]
            f = "x" if l == "y" else "y"
            info.append((part, order[0] != "z", f, l, self.own(f), self.own(l)))
        return info

    def ag_drain(self, bank):
        A = self.A
        base = bank * 2 * A
        for part, (order, _, rows) in enumerate(self.ag_parts):
            big = order[0] != "z"

            def sent(kind, count):
                ref = self.wb.at[base : base + count, :, pl.ds(0, rows), :]
                slot = (bank * len(self.ag_parts) + part) * 4 + kind
                self.remote(ref, ref, self.ag_s.at[slot], self.ag_r.at[0], self.sib).wait_send()

            inner = jnp.logical_and(self.has_up, self.has_down)
            for kind in (0, 1) if big else (0,):

                @pl.when(inner)
                def _():
                    sent(kind, A + 1)

                @pl.when(jnp.logical_not(inner))
                def _():
                    sent(kind, 1)

            sent(2, 1 if big else A)
            sent(3, 2 * A)


    def turn(self, j):
        A = self.A
        mirrored = self.z >= A // 2
        w = jnp.where(mirrored, A - 1 - self.z, self.z)
        d = jnp.where(j < A - 1 - w, A - 1 - j, jnp.where(j < A - 1, j - (A - 1 - w), w))
        return jnp.where(mirrored, A - 1 - d, d)

    def rs_land(self, bank, part, slot, first):
        if bank == 0 and first:
            _, start, rows = self.rs_parts[part]
            return self.act.at[slot, :, start : start + rows, :]
        return self.land[part].at[slot]

    def rs_index(self, bank, part, slot, first):
        slots = [slots_of(order, self.A) + 3 for order, _, _ in self.rs_parts]
        group = 0 if bank == 1 else 1 if first else 2
        return group * sum(slots) + sum(slots[:part]) + slot

    def rs_send(self, bank, part, z, x, y, slot, kind, device):
        sem = (bank * len(self.rs_parts) + part) * 4 + kind
        self.remote(
            self.spot(bank, self.rs_parts[part], z, x, y),
            self.rs_land(bank, part, slot, kind == 3),
            self.rs_s.at[sem],
            self.rs_r.at[self.rs_index(bank, part, slot, kind == 3)],
            device,
        ).start()

    def rs_add(self, bank, part, z, x, y, slot, out=None, first=False):
        landed = self.rs_land(bank, part, slot, first)
        self.remote(
            landed, landed, self.rs_s.at[0], self.rs_r.at[self.rs_index(bank, part, slot, first)], self.sib
        ).wait_recv()
        order, start, rows = self.rs_parts[part]
        at = bank * 2 * self.A + z * 2 + x
        row = pl.multiple_of(y * self.R + start, SUB)

        @pl.loop(0, 2)
        def _(h):
            total = self.wb[at, h, pl.ds(row, rows), :].astype(F32) + landed[h].astype(F32)
            if out is None:
                self.wb[at, h, pl.ds(row, rows), :] = total.astype(BF)
            else:
                out[h, start : start + rows, :] = total

    def rs_firsts(self, bank):
        sends = []

        def send(z, w, part, big, f, l, fo, lo):
            fc = fo if w == 0 else 1 - fo
            px, py = self.place(f, fc, 1 - lo)
            self.rs_send(bank, part, z, px, py, z * 2 + fc, 3, self.near[l])

        for z in self.turns:
            for row in self.orders(self.rs_parts):
                for w in (1, 0):
                    sends.append(functools.partial(send, z, w, *row))
        return sends

    def rs_slot(self, bank, part, slot):
        if bank == 1:
            return slot
        A = self.A
        more = slots_of(self.rs_parts[part][0], A)
        slot = slot - 2 * A
        return jnp.where(slot < 2 * A, slot, slot - 2 * A + more)

    def chain(self, bank, part, big, f, fc, lo, w, z, final):
        A = self.A
        base = 2 * A + w * (A + 1) if big else 3 * A
        px, py = self.place(f, fc, lo)

        def slot(k):
            return self.rs_slot(bank, part, base + k)

        def onward(device, next_z, up):
            self.rs_send(bank, part, z, px, py, slot(z if up else jnp.where(z == next_z, A, z)), w, device)

        @pl.when(z > self.z)
        def _():
            @pl.when(self.has_down)
            def _():
                self.rs_add(bank, part, z, px, py, slot(z))

            onward(self.up, self.z + 1, True)

        @pl.when(z < self.z)
        def _():
            @pl.when(self.has_up)
            def _():
                self.rs_add(bank, part, z, px, py, slot(z))

            onward(self.down, self.z - 1, False)

        @pl.when(z == self.z)
        def _():
            inner = jnp.logical_and(self.has_down, self.has_up)

            @pl.when(inner)
            def _():
                self.rs_add(bank, part, z, px, py, slot(z))
                self.rs_add(bank, part, z, px, py, slot(A), final)

            @pl.when(jnp.logical_not(inner))
            def _():
                self.rs_add(bank, part, z, px, py, slot(jnp.where(self.has_down, z, A)), final)

    def rs_across(self, bank, j, sends):
        A, z = self.A, self.turns[j]

        def across(w, more, part, big, f, l, fo, lo):
            fc = fo if w == 0 else 1 - fo
            px, py = self.place(f, fc, lo)
            self.rs_add(bank, part, z, px, py, z * 2 + fc, first=True)
            if more:
                more()
            if w == 1 and not big:
                self.rs_send(bank, part, z, px, py, self.rs_slot(bank, part, 2 * A + z), 2, self.near[f])

        return [
            functools.partial(across, w, sends.pop(0) if sends else None, *row)
            for row in self.orders(self.rs_parts)
            for w in (1, 0)
        ]

    def rs_along(self, bank, j, out, bigs):
        A, z = self.A, self.turns[j]

        def along(w, part, big, f, l, fo, lo):
            if big:
                self.chain(bank, part, big, f, fo if w == 0 else 1 - fo, lo, w, z, None)
            else:
                px, py = self.place(f, fo, lo)
                self.rs_add(bank, part, z, px, py, self.rs_slot(bank, part, 2 * A + z))
                self.chain(bank, part, big, f, fo, lo, 0, z, out if j == A - 1 else None)

        return [
            functools.partial(along, w, *row)
            for row in self.orders(self.rs_parts)
            if row[1] == bigs
            for w in ((1, 0) if bigs else (0,))
        ]

    def rs_last(self, bank, out):
        A = self.A

        def go():
            for part, big, f, l, fo, lo in self.orders(self.rs_parts):
                if big:
                    px, py = self.place(f, 1 - fo, lo)
                    self.rs_send(bank, part, self.z, px, py, self.rs_slot(bank, part, 4 * A + 2), 2, self.near[f])

        def come(part, big, f, l, fo, lo):
            px, py = self.place(f, fo, lo)
            self.rs_add(bank, part, self.z, px, py, self.rs_slot(bank, part, 4 * A + 2), out)

        return [go] + [functools.partial(come, *row) for row in self.orders(self.rs_parts) if row[1]]

    def rs_ready(self):
        for go in (None, pl.semaphore_wait):
            self.z_credit(go)
            self.f_credit(go, 4)

    def rs(self, out1, out0):
        A = self.A
        sends1, sends0 = self.rs_firsts(1), self.rs_firsts(0)
        open1, sends1 = sends1[:AHEAD], sends1[AHEAD:]
        open0, sends0 = sends0[:AHEAD], sends0[AHEAD:]
        before, after = list(open1), list(open0)
        small1 = [self.rs_along(1, j, out1, False) for j in range(A)]
        small0 = [self.rs_along(0, j, out0, False) for j in range(A)]
        big1 = [self.rs_along(1, j, out1, True) for j in range(A)]
        big0 = [self.rs_along(0, j, out0, True) for j in range(A)]
        last1, last0 = self.rs_last(1, out1), self.rs_last(0, out0)
        for j in range(A):
            before += zipped(
                self.rs_across(1, j, sends1), (big1[j] if j < A - 1 else []) + (small1[j - 1] if j else [])
            )
        after += [self.rs_ready]
        after += zipped(self.rs_across(0, 0, sends0), big0[0] + big1[A - 1] + small1[A - 1])
        after += last1[:1]
        for j in range(1, A):
            after += zipped(self.rs_across(0, j, sends0), big0[j] + small0[j - 1])
            if j == 1:
                after += last1[1:]
        after += last0[:1] + small0[A - 1] + last0[1:]
        return before, after

    def f_credit(self, wait, at):
        for k, axis in enumerate("xy"):
            if wait:
                wait(self.credit.at[at + k], 1)
            else:
                pl.semaphore_signal(self.credit.at[at + k], inc=1, device_id=self.near[axis], device_id_type=MESH)

    def z_credit(self, wait):
        @pl.when(self.has_up)
        def _():
            if wait:
                wait(self.credit.at[3], 1)
            else:
                pl.semaphore_signal(self.credit.at[2], inc=1, device_id=self.up, device_id_type=MESH)

        @pl.when(self.has_down)
        def _():
            if wait:
                wait(self.credit.at[2], 1)
            else:
                pl.semaphore_signal(self.credit.at[3], inc=1, device_id=self.down, device_id_type=MESH)

    def rs_drain(self, bank):
        A = self.A
        base = bank * 2 * A
        for part, (order, _, rows) in enumerate(self.rs_parts):
            big = order[0] != "z"

            def sent(kind, count):
                ref = self.wb.at[base : base + count, :, pl.ds(0, rows), :]
                slot = (bank * len(self.rs_parts) + part) * 4 + kind
                self.remote(ref, ref, self.rs_s.at[slot], self.rs_r.at[0], self.sib).wait_send()

            sent(0, A - 1)
            if big:
                sent(1, A - 1)
            sent(2, 1 if big else A)
            sent(3, 2 * A)


    def share(self, ref, k):
        rows = ref.at[pl.ds(pl.multiple_of(self.c * self.T, SUB), self.T), :]
        copy = self.remote(rows, rows, self.cg_s.at[k], self.cg_r.at[k], self.sib)
        copy.start()
        return copy

    def shared(self, ref, k):
        rows = ref.at[pl.ds(pl.multiple_of((1 - self.c) * self.T, SUB), self.T), :]
        mine = ref.at[pl.ds(pl.multiple_of(self.c * self.T, SUB), self.T), :]
        self.remote(rows, rows, self.cg_s.at[k], self.cg_r.at[k], self.sib).wait_recv()
        self.remote(mine, mine, self.cg_s.at[k], self.cg_r.at[k], self.sib).wait_send()

    def rows_of(self, which):
        return pl.ds(pl.multiple_of(which * self.T, SUB), self.T)

    def give(self, k, halves):
        buf = k % 2
        for h, value in enumerate(halves(1 - self.c)):
            self.sb[buf, :, h * TILE : (h + 1) * TILE] = value.astype(BF)
        self.remote(self.sb.at[buf], self.rb.at[buf], self.ex_s.at[k], self.ex_r.at[k], self.sib).start()
        for h, value in enumerate(halves(self.c)):
            self.pacc[:, h * TILE : (h + 1) * TILE] = value

    def taken(self, k):
        buf = k % 2
        self.remote(self.sb.at[buf], self.rb.at[buf], self.ex_s.at[k], self.ex_r.at[k], self.sib).wait()


    def act_at(self, j, m):
        if self.nt == 1:
            return (j, m)
        half = self.nt // 2
        return (pl.ds(j * self.nt + m * half, half),)

    def act_get(self, j, m):
        return self.act[self.act_at(j, m)].reshape(self.T, TILE)

    def act_set(self, j, m, value):
        at = self.act_at(j, m)
        self.act[at] = value.astype(BF).reshape(self.act.at[at].shape)

    def act_all(self, j):
        return self.act[pl.ds(j * self.nt, self.nt)].reshape(2 * self.T, TILE)


    def wcol(self, b):
        return self.wb[pl.ds(b * self.nzx, self.nzx)].reshape(self.D, TILE)

    def wrow(self, b, h):
        return self.wb[pl.ds(b * self.nzx, self.nzx), h].reshape(TILE, TILE)

    def win(self, j, h):
        return self.wb[pl.ds(2 * self.A + j * self.nt, self.nt), h].reshape(TILE, TILE)

    def wout(self, j, h):
        return self.wb[pl.ds(3 * self.A + j * self.nt, self.nt), h].reshape(TILE, TILE)

    def project(self, dst, first, source, block, count):
        @pl.loop(0, count)
        def _(i):
            weight = self.wcol(block + i)
            for m in range(2):
                rows = slice(m * self.T, (m + 1) * self.T)
                dst[first + i, rows, :] = dot(source[rows, :], weight).astype(BF)


    def masks(self):
        lane = lax.broadcasted_iota(jnp.int32, (1, PAIR), 1)
        row = lax.broadcasted_iota(jnp.int32, (PAIR, 1), 0)
        return [(lane < HD), (lane >= HD)], (row < HD)

    def visible(self, tile):
        T = self.T
        key = lax.broadcasted_iota(jnp.int32, (2 * T, T), 0)
        query = lax.broadcasted_iota(jnp.int32, (2 * T, T), 1) + tile * T
        edge = self.pfx_now[0:1, 0:1]
        return jnp.logical_or(key <= query, key.astype(F32) < edge)

    def attend(self, p, qkv, o, lse, masked, point):
        T = self.T
        cols = pl.ds(pl.multiple_of(p * PAIR, PAIR), PAIR)
        heads, upper = self.masks()
        keys = qkv[1, :, cols]
        values_t = turned(qkv[2, :, cols])
        for tile in range(2):
            rows = slice(tile * T, (tile + 1) * T)
            query = qkv[0, rows, cols].astype(F32) * score_scale
            vis = self.visible(tile) if masked else None
            mixed = []
            for h in range(2):
                scores = dot_nt(keys, jnp.where(heads[h], query, 0.0).astype(BF))
                if masked:
                    scores = jnp.where(vis, scores, masked_score)
                highest = jnp.max(scores, axis=0, keepdims=True)
                exponent = jnp.exp(scores - highest)
                total = jnp.sum(exponent, axis=0, keepdims=True)
                lse[p, h : h + 1, rows] = highest + jnp.log(total)
                mixed.append(dot(values_t, exponent.astype(BF)) * (1.0 / total))
                point(2 * tile + h)
            o[rows, cols] = jnp.where(upper, mixed[0], mixed[1]).T.astype(BF)

    def attend_back(self, p, qkv, do, lse, masked, point):
        T = self.T
        cols = pl.ds(pl.multiple_of(p * PAIR, PAIR), PAIR)
        heads, upper = self.masks()
        keys, values = qkv[1, :, cols], qkv[2, :, cols]
        keys_t = turned(keys)
        dk = [0.0, 0.0]
        dv = [0.0, 0.0]
        for tile in range(2):
            rows = slice(tile * T, (tile + 1) * T)
            query = qkv[0, rows, cols]
            grad = do[rows, cols]
            query_wide = query.astype(F32) * score_scale
            grad_wide = grad.astype(F32)
            vis = self.visible(tile) if masked else None
            dq = []
            for h in range(2):
                scores = dot_nt(keys, jnp.where(heads[h], query_wide, 0.0).astype(BF))
                if masked:
                    scores = jnp.where(vis, scores, masked_score)
                probs = jnp.exp(scores - lse[p, h : h + 1, rows])
                dprobs = dot_nt(values, jnp.where(heads[h], grad_wide, 0.0).astype(BF))
                delta = jnp.sum(dprobs * probs, axis=0, keepdims=True)
                dscores = (probs * (dprobs - delta)).astype(BF)
                dq.append(dot(keys_t, dscores))
                dk[h] += dot(dscores, query)
                dv[h] += dot(probs.astype(BF), grad)
                point(2 * tile + h)
            self.dqkv[0, rows, cols] = (jnp.where(upper, dq[0], dq[1]) * score_scale).T.astype(BF)
        self.dqkv[1, :, cols] = (jnp.where(heads[0], dk[0], dk[1]) * score_scale).astype(BF)
        self.dqkv[2, :, cols] = jnp.where(heads[0], dv[0], dv[1]).astype(BF)


    def norm(self, summed):
        centred = summed - jnp.mean(summed, axis=-1, keepdims=True)
        inv = lax.rsqrt(jnp.mean(centred * centred, axis=-1, keepdims=True) + norm_eps)
        return centred * inv, inv

    def norm_back(self, k, dy, normed, inv):
        gain = self.norms[k : k + 1, :]
        self.ng[k : k + 1, :] += jnp.sum(dy * normed, axis=0, keepdims=True)
        self.ng[3 + k : 4 + k, :] += jnp.sum(dy, axis=0, keepdims=True)
        scaled = dy * gain
        plain = jnp.mean(scaled, axis=-1, keepdims=True)
        along = jnp.mean(scaled * normed, axis=-1, keepdims=True)
        return inv * (scaled - plain - normed * along)

    def norm_rows(self, body):
        @pl.loop(0, self.T // LN_ROWS)
        def _(i):
            own = pl.ds(pl.multiple_of(i * LN_ROWS, LN_ROWS), LN_ROWS)
            full = pl.ds(pl.multiple_of(self.c * self.T + i * LN_ROWS, LN_ROWS), LN_ROWS)
            body(own, full)


def zipped(first, second):
    first, second, steps = list(first), list(second), []
    while first or second:
        steps += first[:2] + second[:1]
        first, second = first[2:], second[1:]
    return steps


class Steps:
    def __init__(self, steps):
        self.steps = list(steps)

    def run(self, count):
        now, self.steps = self.steps[:count], self.steps[count:]
        for step in now:
            step()

    def finish(self):
        self.run(len(self.steps))

    def spread(self, index, turns, points, count=1):
        total = turns * points * count
        now, self.steps = self.steps[:total], self.steps[total:]

        def at(point):
            for turn in range(turns):
                place = (turn * points + point) * count
                if now[place : place + count]:

                    @pl.when(index == turn)
                    def _():
                        for step in now[place : place + count]:
                            step()

        return at


def kernel(A, R, T, ag_parts, rs_parts, names, *arrays):
    s = Layer(A, R, T, ag_parts, rs_parts, dict(zip(names, arrays)))
    s.land = [getattr(s, f"land{i}") for i in range(len(rs_parts))]
    D = s.D
    away = jnp.logical_not(s.kept)
    s.ng[...] = jnp.zeros_like(s.ng)
    s.barrier()

    block = s.zx // s.nzx
    by_rows = jnp.logical_or(block == 3, block == 7)
    mine = pl.ds(pl.multiple_of(s.y * R, SUB), R)
    ffn_copy = pltpu.make_async_copy(s.ffn_piece, s.wb.at[2 * A + s.zx, :, mine, :], s.lc.at[0])
    ffn_copy.start()
    rows_copy = pltpu.make_async_copy(s.attn_piece, s.wb.at[s.zx, :, mine, :], s.lc.at[1])
    half_copy = pltpu.make_async_copy(s.attn_piece.at[s.c], s.wb.at[s.zx, s.c, mine, :], s.lc.at[2])
    half_send = s.remote(
        s.attn_piece.at[1 - s.c], s.wb.at[s.zx, s.c, mine, :], s.misc_s.at[0], s.misc_r.at[0], s.sib
    )
    half_recv = s.remote(
        s.attn_piece.at[1 - s.c], s.wb.at[s.zx, 1 - s.c, mine, :], s.misc_s.at[0], s.misc_r.at[0], s.sib
    )

    @pl.when(by_rows)
    def _():
        rows_copy.start()

    @pl.when(jnp.logical_not(by_rows))
    def _():
        half_copy.start()
        half_send.start()

    here = s.rows_of(s.c)
    there = s.rows_of(s.y)
    swaps = [
        (s.tokens, s.xf.at[here, :], s.xf.at[there, :]),
        (s.memory, s.mf.at[here, :], s.mf.at[there, :]),
        (s.pfx, s.pfx_now, s.pfx_now),
        (s.cot, s.cotb, s.cotb),
    ]

    def swap(i):
        src, dst, far = swaps[i]

        @pl.when(s.kept)
        def _():
            pltpu.make_async_copy(src, dst, s.lc.at[3 + i]).start()

        @pl.when(away)
        def _():
            s.remote(src, far, s.sw_s.at[i], s.sw_r.at[i], s.partner).start()

    swap(0)
    swap(1)
    swap(2)

    @pl.when(by_rows)
    def _():
        rows_copy.wait()

    @pl.when(jnp.logical_not(by_rows))
    def _():
        half_copy.wait()
        half_send.wait_send()
        half_recv.wait_recv()

    gather, ffn = Steps(s.ag(0)), Steps(s.ag(1))
    gather.run(2)

    def swapped(i):
        src, dst, far = swaps[i]

        @pl.when(s.kept)
        def _():
            pltpu.make_async_copy(src, dst, s.lc.at[3 + i]).wait()

        @pl.when(away)
        def _():
            s.remote(src, far, s.sw_s.at[i], s.sw_r.at[i], s.partner).wait_send()
            s.remote(src, dst, s.sw_s.at[i], s.sw_r.at[i], s.partner).wait_recv()

    gather.run(14)
    ffn_copy.wait()
    ffn.run(1)
    gather.run(14)
    ffn.run(1)
    swap(3)
    for i in range(3):
        swapped(i)
    s.share(s.xf, 0)
    s.share(s.mf, 1)
    gather.finish()
    s.shared(s.xf, 0)
    s.shared(s.mf, 1)

    s.project(s.qkv1, 0, s.xf, 0, 3)
    ffn.run(2)
    s.project(s.qkv2, 1, s.mf, 5, 2)
    ffn.run(2)

    @pl.loop(0, TILE // PAIR)
    def _(p):
        s.attend(p, s.qkv1, s.o1, s.lse1, True, ffn.spread(p, TILE // PAIR, 4))

    def branch(o, b):
        return lambda which: [dot(o[s.rows_of(which), :], s.wrow(b, h)) for h in range(2)]

    s.give(0, branch(s.o1, 3))
    ffn.run(1)
    s.taken(0)

    def first_norm(own, full):
        summed = alpha_scale * s.xf[full, :].astype(F32) + s.pacc[own, :] + s.rb[0, own, :].astype(F32)
        normed, inv = s.norm(summed)
        s.dtok[own, :] = normed
        s.inv1[own, :] = inv
        result = normed * s.norms[0:1, :] + s.norms[3:4, :]
        s.nbuf[own, :] = result
        s.n1r[full, :] = result.astype(BF)

    s.norm_rows(first_norm)
    s.share(s.n1r, 2)
    ffn.run(2)
    s.shared(s.n1r, 2)

    s.project(s.qkv2, 0, s.n1r, 4, 1)

    @pl.loop(0, TILE // PAIR)
    def _(p):
        s.attend(p, s.qkv2, s.o2, s.lse2, False, ffn.spread(p, TILE // PAIR, 4))

    s.give(1, branch(s.o2, 7))
    ffn.run(1)
    s.taken(1)

    def second_norm(own, full):
        summed = alpha_scale * s.nbuf[own, :] + s.pacc[own, :] + s.rb[1, own, :].astype(F32)
        normed, inv = s.norm(summed)
        s.dmem[own, :] = normed
        s.inv2[own, :] = inv
        result = normed * s.norms[1:2, :] + s.norms[4:5, :]
        s.nbuf[own, :] = result
        s.n2r[full, :] = result.astype(BF)

    s.norm_rows(second_norm)
    s.share(s.n2r, 3)
    ffn.run(2)
    s.shared(s.n2r, 3)
    ffn.finish()
    swapped(3)

    tiles = 2 * A * R // TILE

    @pl.loop(0, tiles)
    def _(j):
        for m in range(2):
            rows = slice(m * T, (m + 1) * T)
            pre = dot_nt(s.n2r[rows, :TILE], s.win(j, 0)) + dot_nt(s.n2r[rows, TILE:], s.win(j, 1))
            gate = 1.0 / (1.0 + jnp.exp(-pre))
            s.act_set(tiles + j, m, pre * gate)
            s.act_set(j, m, gate * (1.0 + pre * (1.0 - gate)))

    def ffn_out(which):
        return [sum(dot(s.act_get(tiles + j, which), s.wout(j, h)) for j in range(tiles)) for h in range(2)]

    s.give(2, ffn_out)
    s.taken(2)

    def third_norm(own, full):
        summed = alpha_scale * s.nbuf[own, :] + s.pacc[own, :] + s.rb[0, own, :].astype(F32)
        normed, inv = s.norm(summed)
        result = normed * s.norms[2:3, :] + s.norms[5:6, :]
        s.out[own, :] = result
        s.osb[0, own, :] = result.astype(BF)
        grad = s.norm_back(2, s.cotb[own, :].astype(F32), normed, inv)
        s.nbuf[own, :] = grad
        s.ga[full, :] = grad.astype(BF)

    s.norm_rows(third_norm)
    s.share(s.ga, 4)

    def send_back(k):
        @pl.when(away)
        def _():
            s.remote(s.osb.at[k], s.orb.at[k], s.ob_s.at[k], s.ob_r.at[k], s.partner).start()

    send_back(0)
    s.ag_drain(0)
    s.ag_drain(1)
    s.shared(s.ga, 4)

    @pl.loop(0, tiles)
    def _(j):
        for m in range(2):
            rows = slice(m * T, (m + 1) * T)
            da = dot_nt(s.ga[rows, :TILE], s.wout(j, 0)) + dot_nt(s.ga[rows, TILE:], s.wout(j, 1))
            s.act_set(j, m, da * s.act_get(j, m).astype(F32))

    def ffn_in(which):
        return [sum(dot(s.act_get(j, which), s.win(j, h)) for j in range(tiles)) for h in range(2)]

    s.give(3, ffn_in)

    @pl.loop(0, tiles)
    def _(j):
        hidden, grads = s.act_all(tiles + j), s.act_all(j)
        for h in range(2):
            cols = slice(h * TILE, (h + 1) * TILE)
            out_rows = dot_tn(hidden, s.ga[:, cols]).astype(BF)
            s.wb[pl.ds(3 * A + j * s.nt, s.nt), h] = out_rows.reshape(s.nt, 2 * R, TILE)
            in_rows = dot_tn(grads, s.n2r[:, cols]).astype(BF)
            s.wb[pl.ds(2 * A + j * s.nt, s.nt), h] = in_rows.reshape(s.nt, 2 * R, TILE)

    s.f_credit(None, 0)
    spread, rest = (Steps(steps) for steps in s.rs(s.dffn, s.fin))
    spread.run(AHEAD)
    s.taken(3)

    def second_back(own, full):
        dy = alpha_scale * s.nbuf[own, :] + s.pacc[own, :] + s.rb[1, own, :].astype(F32)
        grad = s.norm_back(1, dy, s.dmem[own, :], s.inv2[own, :])
        s.nbuf[own, :] = grad
        s.gb[full, :] = grad.astype(BF)

    s.norm_rows(second_back)
    s.share(s.gb, 5)
    spread.run(3)
    s.shared(s.gb, 5)

    def mixed_back(grad, o, b):
        for m in range(2):
            rows = slice(m * T, (m + 1) * T)
            s.do[rows, :] = (
                dot_nt(grad[rows, :TILE], s.wrow(b, 0)) + dot_nt(grad[rows, TILE:], s.wrow(b, 1))
            ).astype(BF)
        for h in range(2):
            cols = slice(h * TILE, (h + 1) * TILE)
            terms = dot_tn(o[...], grad[:, cols]).astype(BF)
            s.wb[pl.ds(b * s.nzx, s.nzx), h] = terms.reshape(s.nzx, 2 * R, TILE)

    def weight_terms(b, source, grad):
        for h in range(2):
            cols = slice(h * TILE, (h + 1) * TILE)
            terms = dot_tn(source[:, cols], grad).astype(BF)
            half = s.nzx // 2 if s.nzx > 1 else 0
            if half:
                s.wb[pl.ds(b * s.nzx + h * half, half)] = terms.reshape(half, 2, 2 * R, TILE)
            else:
                s.wb[b, h] = terms

    def spread_back(which, blocks):
        rows = s.rows_of(which)
        halves = []
        for h in range(2):
            total = 0.0
            for b, k in blocks:
                total += dot_nt(s.dqkv[k, rows, :], s.wcol(b)[h * TILE : (h + 1) * TILE])
            halves.append(total)
        return halves

    mixed_back(s.gb, s.o2, 7)
    spread.run(3)

    @pl.loop(0, TILE // PAIR)
    def _(p):
        s.attend_back(p, s.qkv2, s.do, s.lse2, False, spread.spread(p, TILE // PAIR, 4))

    s.give(4, lambda which: spread_back(which, [(5, 1), (6, 2)]))
    spread.run(2)
    s.taken(4)

    def memory_rows(own, full):
        total = s.pacc[own, :] + s.rb[0, own, :].astype(F32)
        s.dmem[own, :] = total
        s.osb[1, own, :] = total.astype(BF)

    s.norm_rows(memory_rows)
    send_back(1)
    s.give(5, lambda which: spread_back(which, [(4, 0)]))
    spread.run(2)
    weight_terms(4, s.n1r, s.dqkv[0])
    weight_terms(5, s.mf, s.dqkv[1])
    weight_terms(6, s.mf, s.dqkv[2])
    spread.run(2)
    s.taken(5)

    def first_back(own, full):
        dy = alpha_scale * s.nbuf[own, :] + s.pacc[own, :] + s.rb[1, own, :].astype(F32)
        grad = s.norm_back(0, dy, s.dtok[own, :], s.inv1[own, :])
        s.nbuf[own, :] = grad
        s.ga[full, :] = grad.astype(BF)

    s.norm_rows(first_back)
    s.share(s.ga, 6)
    spread.run(3)
    s.shared(s.ga, 6)

    def norm_sum():
        for k, device in enumerate((s.sib, s.near["x"], s.near["y"])):
            copy = s.remote(s.ngs.at[k], s.ngr.at[k], s.nm_s.at[k], s.nm_r.at[k], device)
            s.ngs[k] = s.ng[...]
            copy.start()
            yield
            copy.wait()
            s.ng[...] = s.ng[...] + s.ngr[k]
        s.ngz[s.z] = s.ng[...]
        for other in range(A):

            @pl.when(s.z != other)
            def _():
                s.remote(
                    s.ng, s.ngz.at[s.z], s.nm_s.at[3 + other], s.nm_r.at[3 + s.z],
                    (s.dp + 4 * (other - s.z), s.y),
                ).start()

        yield
        for other in range(A):

            @pl.when(s.z != other)
            def _():
                s.remote(s.ng, s.ngz.at[other], s.nm_s.at[3 + other], s.nm_r.at[3 + other], s.sib).wait()

        total = s.ngz[0]
        for other in range(1, A):
            total = total + s.ngz[other]
        s.dnorm[...] = total[:6, :]
        yield

    sums = norm_sum()
    next(sums)

    mixed_back(s.ga, s.o1, 3)
    spread.run(3)
    next(sums)

    @pl.loop(0, TILE // PAIR)
    def _(p):
        s.attend_back(p, s.qkv1, s.do, s.lse1, True, spread.spread(p, TILE // PAIR, 4))

    next(sums)
    s.give(6, lambda which: spread_back(which, [(0, 0), (1, 1), (2, 2)]))
    next(sums)

    @pl.loop(0, 3)
    def _(k):
        weight_terms(k, s.xf, s.dqkv[k])

    next(sums, None)
    s.taken(6)

    def token_rows(own, full):
        total = alpha_scale * s.nbuf[own, :] + s.pacc[own, :] + s.rb[0, own, :].astype(F32)
        s.dtok[own, :] = total
        s.osb[2, own, :] = total.astype(BF)

    s.norm_rows(token_rows)
    send_back(2)
    spread.finish()
    s.f_credit(pl.semaphore_wait, 0)
    rest.run(AHEAD)

    @pl.when(away)
    def _():
        for k, dst in enumerate((s.out, s.dmem, s.dtok)):
            s.remote(s.osb.at[k], s.orb.at[k], s.ob_s.at[k], s.ob_r.at[k], s.partner).wait()

            @pl.loop(0, T // LN_ROWS)
            def _(i):
                own = pl.ds(pl.multiple_of(i * LN_ROWS, LN_ROWS), LN_ROWS)
                dst[own, :] = s.orb[k, own, :].astype(F32)

    rest.finish()

    tail_send = s.remote(s.fin.at[1 - s.c], s.dattn.at[s.c], s.misc_s.at[1], s.misc_r.at[1], s.sib)
    tail_recv = s.remote(s.fin.at[1 - s.c], s.dattn.at[1 - s.c], s.misc_s.at[1], s.misc_r.at[1], s.sib)

    @pl.when(by_rows)
    def _():
        s.dattn[...] = s.fin[...]

    @pl.when(jnp.logical_not(by_rows))
    def _():
        tail_send.start()
        s.dattn[s.c] = s.fin[s.c]
        tail_send.wait_send()
        tail_recv.wait_recv()

    s.rs_drain(1)
    s.rs_drain(0)


def on_device(A, tokens, memory, attn_bank, ffn_bank, norm_params, prefix, cotangent):
    T, D = tokens.shape
    R = attn_bank.shape[0]
    ag_parts, rs_parts = cut(R, GATHER), cut(R, SCATTER)
    groups = D // (4 * R)
    tiles = 2 * A * R // TILE

    def by_half(shard):
        return shard.reshape(R, 2, TILE).transpose(1, 0, 2)

    def by_core(shard):
        return shard.reshape(R, groups, 2, 2 * R).transpose(2, 0, 1, 3).reshape(2, R, TILE)

    block = (lax.axis_index("dp") // 2) // groups
    by_rows = jnp.logical_or(block == 3, block == 7)
    attn_piece = by_half(attn_bank)
    if groups > 1:
        attn_piece = jnp.where(by_rows, attn_piece, by_core(attn_bank))
    pfx = jnp.broadcast_to(prefix.astype(F32)[0], (8, 128))
    slots = sum(slots_of(order, A) + 3 for order, _, _ in rs_parts)

    inputs = dict(
        tokens=tokens,
        memory=memory,
        cot=cotangent,
        pfx=pfx,
        attn_piece=attn_piece,
        ffn_piece=by_half(ffn_bank),
        norms=norm_params,
    )
    in_vmem = ("pfx", "norms")
    outputs = dict(
        out=(T, D), dtok=(T, D), dmem=(T, D), dattn=(2, R, TILE), dffn=(2, R, TILE), dnorm=(6, D)
    )
    wide = lambda *shape: pltpu.VMEM(shape, F32)
    low = lambda *shape: pltpu.VMEM(shape, BF)
    dma = lambda count: pltpu.SemaphoreType.DMA((count,))
    scratch = dict(
        wb=low(4 * A, 2, 2 * R, TILE),
        xf=low(2 * T, D),
        mf=low(2 * T, D),
        n1r=low(2 * T, D),
        n2r=low(2 * T, D),
        ga=low(2 * T, D),
        gb=low(2 * T, D),
        cotb=low(T, D),
        act=low(2 * A, 2, R, TILE),
        qkv1=low(3, 2 * T, TILE),
        qkv2=low(3, 2 * T, TILE),
        dqkv=low(3, 2 * T, TILE),
        o1=low(2 * T, TILE),
        o2=low(2 * T, TILE),
        do=low(2 * T, TILE),
        sb=low(2, T, D),
        rb=low(2, T, D),
        osb=low(3, T, D),
        orb=low(3, T, D),
        nbuf=wide(T, D),
        pacc=wide(T, D),
        fin=wide(2, R, TILE),
        pfx_now=wide(8, 128),
        lse1=wide(TILE // PAIR, 8, 2 * T),
        lse2=wide(TILE // PAIR, 8, 2 * T),
        inv1=wide(T, 1),
        inv2=wide(T, 1),
        ng=wide(8, D),
        ngs=wide(3, 8, D),
        ngr=wide(3, 8, D),
        ngz=wide(A, 8, D),
        lc=dma(7),
        misc_s=dma(2),
        misc_r=dma(2),
        sw_s=dma(4),
        sw_r=dma(4),
        ag_s=dma(2 * len(ag_parts) * 4),
        ag_r=dma(2 * len(ag_parts) * 4 * A),
        rs_s=dma(2 * len(rs_parts) * 4),
        rs_r=dma(3 * slots),
        cg_s=dma(7),
        cg_r=dma(7),
        ex_s=dma(7),
        ex_r=dma(7),
        ob_s=dma(3),
        ob_r=dma(3),
        nm_s=dma(3 + A),
        nm_r=dma(3 + A),
        credit=pltpu.SemaphoreType.REGULAR((6,)),
    )
    for i, (order, _, rows) in enumerate(rs_parts):
        scratch[f"land{i}"] = low(slots_of(order, A) + (3 if order[0] != "z" else 1), 2, rows, TILE)
    names = list(inputs) + list(outputs) + list(scratch)
    out, dtok, dmem, dattn, dffn, dnorm = pl.pallas_call(
        functools.partial(kernel, A, R, T, ag_parts, rs_parts, names),
        out_shape=[jax.ShapeDtypeStruct(shape, F32) for shape in outputs.values()],
        in_specs=[pl.BlockSpec(memory_space=pltpu.VMEM if n in in_vmem else pl.ANY) for n in inputs],
        out_specs=[pl.BlockSpec(memory_space=pltpu.VMEM)] * len(outputs),
        scratch_shapes=list(scratch.values()),
        compiler_params=pltpu.CompilerParams(
            collective_id=0, has_side_effects=True, vmem_limit_bytes=64 * 2**20
        ),
        name="layer",
    )(*inputs.values())

    def half_back(pieces):
        return pieces.transpose(1, 0, 2).reshape(R, D)

    def core_back(pieces):
        return pieces.reshape(2, R, groups, 2 * R).transpose(1, 2, 0, 3).reshape(R, D)

    attn_rows = half_back(dattn)
    if groups > 1:
        attn_rows = jnp.where(by_rows, attn_rows, core_back(dattn))
    return (out, dtok, dmem, attn_rows, half_back(dffn), dnorm)


def solution(mesh):
    rows = P(("dp", "seq"), None)
    return jax.shard_map(
        functools.partial(on_device, mesh.shape["dp"] // 4),
        mesh=mesh,
        in_specs=(rows, rows, rows, rows, P(), P("dp"), rows),
        out_specs=(rows, rows, rows, rows, rows, P()),
        check_vma=False,
    )
```

```python
import functools

import jax
import jax.numpy as jnp
from jax import lax
from jax.experimental import pallas as pl
from jax.experimental.pallas import tpu as pltpu
from jax.sharding import PartitionSpec as P

HD = 64
PAIR = 2 * HD
TILE = 512
SUB = 16
LN_ROWS = 32
HANDS = 4
AHEAD = 8
ACROSS = 11.63
ALONG = 12.12
HOP = 9.52
LAG_BIG = 0.06
LAG_SMALL = 0.71
START = 12.51
FIRST = 3.0
SECOND = 10.05
GATHER = (5, 5, 3, 3)
SCATTER = (4, 6, 3, 3)

alpha_scale = 300.0**0.25
norm_eps = 1e-05
masked_score = -1e30
score_scale = HD**-0.5

BF = jnp.bfloat16
F32 = jnp.float32
MESH = pl.DeviceIdType.MESH


def dot(left, right):
    return jnp.dot(left, right, preferred_element_type=F32)


def dot_nt(left, right):
    return lax.dot_general(left, right, (((1,), (1,)), ((), ())), preferred_element_type=F32)


def dot_tn(left, right):
    return lax.dot_general(left, right, (((0,), (0,)), ((), ())), preferred_element_type=F32)


def turned(block):
    return block.astype(F32).T.astype(BF)


def cut(rows, split):
    units = rows // SUB
    shares = [(units * share + 8) // 16 for share in split[1:]]
    sizes = list(zip(("xzy", "yzx", "zxy", "zyx"), [units - sum(shares)] + shares))
    parts, start = [], 0
    for order, size in sizes:
        if size > 0:
            parts.append((order, start * SUB, size * SUB))
        start += size
    return parts


def slots_of(order, A):
    return 4 * A + 3 if order[0] != "z" else 4 * A + 1


def landing(order, A):
    return slots_of(order, A) + (3 if order[0] != "z" else 1)


class Layer:
    def __init__(self, A, R, T, ag_parts, rs_parts, refs):
        self.A, self.R, self.T = A, R, T
        self.ag_parts, self.rs_parts = ag_parts, rs_parts
        self.D = 1024
        self.nzx = self.D // (4 * R)
        self.nt = TILE // (2 * R)
        for name, ref in refs.items():
            setattr(self, name, ref)
        self.dp, self.y = lax.axis_index("dp"), lax.axis_index("seq")
        self.c = lax.rem(self.dp, 2)
        self.x = lax.rem(self.dp // 2, 2)
        self.z = self.dp // 4
        self.zx = self.dp // 2
        self.sib = (self.dp + 1 - 2 * self.c, self.y)
        self.near = {"x": (self.dp + 2 - 4 * self.x, self.y), "y": (self.dp, 1 - self.y)}
        self.up = (self.dp + 4, self.y)
        self.down = (self.dp - 4, self.y)
        self.partner = (self.dp - self.c + self.y, self.c)
        self.has_up = self.z < A - 1
        self.has_down = self.z > 0
        self.kept = self.c == self.y
        self.turns = [self.turn(j) for j in range(A)]


    def remote(self, src, dst, send, recv, device):
        return pltpu.make_async_remote_copy(
            src_ref=src, dst_ref=dst, send_sem=send, recv_sem=recv, device_id=device, device_id_type=MESH
        )

    def own(self, axis):
        return self.x if axis == "x" else self.y

    def spot(self, bank, part, z, x, y):
        order, start, rows = part
        row = pl.multiple_of(y * self.R + start, SUB)
        return self.wb.at[bank * 2 * self.A + z * 2 + x, :, pl.ds(row, rows), :]

    def place(self, axis, f, l):
        return (f, l) if axis == "x" else (l, f)


    def barrier(self):
        bar = pltpu.get_barrier_semaphore()

        def greet(device):
            pl.semaphore_signal(bar, inc=1, device_id=device, device_id_type=MESH)

        greet(self.sib)
        greet(self.near["x"])
        greet(self.near["y"])
        for other in range(self.A):

            @pl.when(self.z != other)
            def _():
                greet((self.dp + 4 * (other - self.z), self.y))

        @pl.when(jnp.logical_not(self.kept))
        def _():
            greet(self.partner)
            pl.semaphore_wait(bar, 3 + self.A)

        @pl.when(self.kept)
        def _():
            pl.semaphore_wait(bar, 2 + self.A)


    def ag_index(self, bank, part, z, x, y, last):
        base = (bank * len(self.ag_parts) + part) * (2 * self.A + 1)
        if last:
            return base + 2 * self.A
        return base + z * 2 + (x if self.ag_parts[part][0][2] == "y" else y)

    def ag_send(self, bank, part, z, x, y, kind, device):
        ref = self.spot(bank, self.ag_parts[part], z, x, y)
        recv = self.ag_r.at[self.ag_index(bank, part, z, x, y, kind == 3)]
        self.remote(ref, ref, self.ag_s.at[part * 4 + kind], recv, device).start()

    def ag_wait(self, bank, part, z, x, y):
        ref = self.spot(bank, self.ag_parts[part], z, x, y)
        recv = self.ag_r.at[self.ag_index(bank, part, z, x, y, False)]
        self.remote(ref, ref, self.ag_s.at[0], recv, self.sib).wait_recv()

    def ag_last(self, bank, part):
        _, _, rows = self.ag_parts[part]
        ref = self.wb.at[0 : 2 * self.A, :, pl.ds(0, rows), :]
        recv = self.ag_r.at[self.ag_index(bank, part, 0, 0, 0, True)]
        self.remote(ref, ref, self.ag_s.at[0], recv, self.sib).wait_recv()

    def ag(self, bank):
        A = self.A
        info, steps = self.orders(self.ag_parts), []

        def z_sends(part, f, fc, lc, w):
            px, py = self.place(f, fc, lc)

            @pl.when(self.has_up)
            def _():
                self.ag_send(bank, part, self.z, px, py, w, self.up)

            @pl.when(self.has_down)
            def _():
                self.ag_send(bank, part, self.z, px, py, w, self.down)

        def send(part, f, fc, lc, z, kind, axis):
            px, py = self.place(f, fc, lc)
            self.ag_send(bank, part, z, px, py, kind, self.near[axis])

        def early():
            for part, big, f, l, fo, lo in info:
                if big:
                    send(part, f, fo, lo, self.z, 2, f)

        def begin():
            for part, big, f, l, fo, lo in info:
                z_sends(part, f, fo, lo, 0)
            for part, big, f, l, fo, lo in info:
                if not big:
                    send(part, f, fo, lo, self.z, 2, f)
                send(part, f, fo, lo, self.z, 3, l)

        def beside(part, big, f, l, fo, lo):
            px, py = self.place(f, 1 - fo, lo)
            self.ag_wait(bank, part, self.z, px, py)
            z_sends(part, f, 1 - fo, lo, 1)
            send(part, f, 1 - fo, lo, self.z, 3, l)

        def arrive(d, w, part, big, f, l, fo, lo):
            fc = fo if w == 0 else 1 - fo
            px, py = self.place(f, fc, lo)

            def arrived(z, on, device):
                self.ag_wait(bank, part, z, px, py)

                @pl.when(on)
                def _():
                    self.ag_send(bank, part, z, px, py, w, device)

                if not big:
                    send(part, f, fc, lo, z, 2, f)
                send(part, f, fc, lo, z, 3, l)

            @pl.when(self.z >= d)
            def _():
                arrived(self.z - d, self.has_up, self.up)

            @pl.when(self.z + d < A)
            def _():
                arrived(self.z + d, self.has_down, self.down)

        def cross(d, part, big, f, l, fo, lo):
            px, py = self.place(f, 1 - fo, lo)

            def crossed(z):
                self.ag_wait(bank, part, z, px, py)
                send(part, f, 1 - fo, lo, z, 3, l)

            self.planes_at(d, crossed)

        bigs = [row for row in info if row[1]]
        smalls = [row for row in info if not row[1]]
        steps += [early, begin]
        for d in range(1, A):
            steps += [functools.partial(arrive, d, 0, *row) for row in info]
            if d == 1:
                steps += [functools.partial(beside, *row) for row in bigs]
            steps += [functools.partial(arrive, d, 1, *row) for row in bigs]
            steps += [functools.partial(cross, d - 1, *row) for row in smalls]
        steps += [functools.partial(cross, A - 1, *row) for row in smalls]
        steps += [functools.partial(self.ag_last, bank, row[0]) for row in info]
        return steps

    def planes_at(self, d, act):
        if d == 0:
            act(self.z)
            return

        @pl.when(self.z >= d)
        def _():
            act(self.z - d)

        @pl.when(self.z + d < self.A)
        def _():
            act(self.z + d)

    def orders(self, parts):
        info = []
        for part, (order, _, _) in enumerate(parts):
            l = order[2]
            f = "x" if l == "y" else "y"
            info.append((part, order[0] != "z", f, l, self.own(f), self.own(l)))
        return info

    def ag_drain(self):
        A = self.A
        inner = jnp.logical_and(self.has_up, self.has_down)
        for part, (order, _, rows) in enumerate(self.ag_parts):
            big = order[0] != "z"

            def sent(kind, count):
                ref = self.wb.at[0 : 2 * count, :, pl.ds(0, rows), :]
                self.remote(ref, ref, self.ag_s.at[part * 4 + kind], self.ag_r.at[0], self.sib).wait_send()

            for kind in (0, 1) if big else (0,):

                @pl.when(inner)
                def _():
                    sent(kind, A + 1)

                @pl.when(jnp.logical_not(inner))
                def _():
                    sent(kind, 1)

            sent(2, 1 if big else A)
            sent(3, 2 * A)


    def turn(self, j):
        A = self.A
        mirrored = self.z >= A // 2
        w = jnp.where(mirrored, A - 1 - self.z, self.z)
        d = jnp.where(j < A - 1 - w, A - 1 - j, jnp.where(j < A - 1, j - (A - 1 - w), w))
        return jnp.where(mirrored, A - 1 - d, d)

    def rs_land(self, bank, part, slot, first):
        if bank == 0 and first:
            _, start, rows = self.rs_parts[part]
            return self.act.at[slot, :, start : start + rows, :]
        return self.land[part].at[slot]

    def rs_index(self, bank, part, slot, first):
        room = [landing(order, self.A) for order, _, _ in self.rs_parts]
        if bank == 0 and first:
            return sum(room) + part * 2 * self.A + slot
        return sum(room[:part]) + slot

    def rs_send(self, bank, part, z, x, y, slot, kind, device):
        sem = part * 4 + kind
        self.remote(
            self.spot(bank, self.rs_parts[part], z, x, y),
            self.rs_land(bank, part, slot, kind == 3),
            self.rs_s.at[sem],
            self.rs_r.at[self.rs_index(bank, part, slot, kind == 3)],
            device,
        ).start()

    def rs_add(self, bank, part, z, x, y, slot, out=None, first=False):
        landed = self.rs_land(bank, part, slot, first)
        self.remote(
            landed, landed, self.rs_s.at[0], self.rs_r.at[self.rs_index(bank, part, slot, first)], self.sib
        ).wait_recv()
        order, start, rows = self.rs_parts[part]
        at = bank * 2 * self.A + z * 2 + x
        row = pl.multiple_of(y * self.R + start, SUB)

        @pl.loop(0, 2)
        def _(h):
            total = self.wb[at, h, pl.ds(row, rows), :].astype(F32) + landed[h].astype(F32)
            if out is None:
                self.wb[at, h, pl.ds(row, rows), :] = total.astype(BF)
            else:
                out[start : start + rows, pl.ds(pl.multiple_of(h * TILE, TILE), TILE)] = total

    def rs_firsts(self, bank):
        sends = []

        def send(z, w, part, big, f, l, fo, lo):
            fc = fo if w == 0 else 1 - fo
            px, py = self.place(f, fc, 1 - lo)
            self.rs_send(bank, part, z, px, py, z * 2 + fc, 3, self.near[l])

        for z in self.turns:
            for row in self.orders(self.rs_parts):
                for w in (1, 0):
                    sends.append(functools.partial(send, z, w, *row))
        return sends

    def rs_slot(self, bank, part, slot):
        if bank == 1:
            return slot
        A = self.A
        more = slots_of(self.rs_parts[part][0], A)
        slot = slot - 2 * A
        return jnp.where(slot < 2 * A, slot, slot - 2 * A + more)

    def chain(self, bank, part, big, f, fc, lo, w, z, final):
        A = self.A
        base = 2 * A + w * (A + 1) if big else 3 * A
        px, py = self.place(f, fc, lo)

        def slot(k):
            return self.rs_slot(bank, part, base + k)

        def onward(device, next_z, up):
            self.rs_send(bank, part, z, px, py, slot(z if up else jnp.where(z == next_z, A, z)), w, device)

        @pl.when(z > self.z)
        def _():
            @pl.when(self.has_down)
            def _():
                self.rs_add(bank, part, z, px, py, slot(z))

            onward(self.up, self.z + 1, True)

        @pl.when(z < self.z)
        def _():
            @pl.when(self.has_up)
            def _():
                self.rs_add(bank, part, z, px, py, slot(z))

            onward(self.down, self.z - 1, False)

        @pl.when(z == self.z)
        def _():
            inner = jnp.logical_and(self.has_down, self.has_up)

            @pl.when(inner)
            def _():
                self.rs_add(bank, part, z, px, py, slot(z))
                self.rs_add(bank, part, z, px, py, slot(A), final)

            @pl.when(jnp.logical_not(inner))
            def _():
                self.rs_add(bank, part, z, px, py, slot(jnp.where(self.has_down, z, A)), final)

    def rs_across(self, bank, j, sends, start):
        A, z = self.A, self.turns[j]

        def across(w, more, part, big, f, l, fo, lo):
            fc = fo if w == 0 else 1 - fo
            px, py = self.place(f, fc, lo)
            self.rs_add(bank, part, z, px, py, z * 2 + fc, first=True)
            if more:
                more()
            if w == 1 and not big:
                self.rs_send(bank, part, z, px, py, self.rs_slot(bank, part, 2 * A + z), 2, self.near[f])

        rows = [(w, row) for row in self.orders(self.rs_parts) for w in (1, 0)]
        return [
            (
                start + ACROSS * (j + (k + 1) / len(rows)),
                functools.partial(across, w, sends.pop(0) if sends else None, *row),
            )
            for k, (w, row) in enumerate(rows)
        ]

    def rs_along(self, bank, j, out, first, start):
        A, z = self.A, self.turns[j]
        at_end = jnp.logical_not(jnp.logical_and(self.has_up, self.has_down))

        def along(w, part, big, f, l, fo, lo):
            if big:
                self.chain(bank, part, big, f, fo if w == 0 else 1 - fo, lo, w, z, None)
            else:
                px, py = self.place(f, fo, lo)
                self.rs_add(bank, part, z, px, py, self.rs_slot(bank, part, 2 * A + z))
                self.chain(bank, part, big, f, fo, lo, 0, z, out if j == A - 1 else None)

        def only(role, step):
            @pl.when(role)
            def _():
                step()

        orders = self.orders(self.rs_parts)
        rows = [(w, row) for row in orders if row[1] for w in (1, 0)] + [(0, row) for row in orders if not row[1]]
        plane = min(j, A - 2 + (0.0 if j == A - 1 else -0.5))
        steps = []
        for k, (w, row) in enumerate(rows):
            step = functools.partial(along, w, *row)
            inner = start + ALONG * (plane + (k + 1) / len(rows)) + HOP
            lag = LAG_BIG if row[1] else LAG_SMALL
            end = first + ACROSS * (j + lag + (k + 1) / len(rows))
            if j == A - 1:
                steps.append((max(inner, end), step))
            else:
                steps.append((max(inner, end), functools.partial(only, jnp.logical_not(at_end), step)))
                steps.append((end, functools.partial(only, at_end, step)))
        return steps

    def rs_last(self, bank, out):
        A = self.A

        def go():
            for part, big, f, l, fo, lo in self.orders(self.rs_parts):
                if big:
                    px, py = self.place(f, 1 - fo, lo)
                    self.rs_send(bank, part, self.z, px, py, self.rs_slot(bank, part, 4 * A + 2), 2, self.near[f])

        def come(part, big, f, l, fo, lo):
            px, py = self.place(f, fo, lo)
            self.rs_add(bank, part, self.z, px, py, self.rs_slot(bank, part, 4 * A + 2), out)

        return [go] + [functools.partial(come, *row) for row in self.orders(self.rs_parts) if row[1]]

    def rs_ready(self):
        for go in (None, pl.semaphore_wait):
            self.z_credit(go)
            self.f_credit(go, 4)

    def rs(self, out1, out0):
        A = self.A
        due = []
        for bank, out, first, start in ((1, out1, 0.0, START), (0, out0, ACROSS * A + FIRST, ALONG * (A - 1) + SECOND)):
            sends = self.rs_firsts(bank)
            due += [(first if bank else first - FIRST / 4, step) for step in sends[:AHEAD]]
            sends = sends[AHEAD:]
            for j in range(A):
                due += self.rs_across(bank, j, sends, first)
                due += self.rs_along(bank, j, out, first, start)
            done = start + ALONG * (A - 1) + HOP
            go, *come = self.rs_last(bank, out)
            due += [(done, go)] + [(done + 2 * HOP, step) for step in come]
        due.append((ACROSS * A + FIRST / 2, self.rs_ready))
        return sorted(due, key=lambda step: step[0])

    def f_credit(self, wait, at):
        for k, axis in enumerate("xy"):
            if wait:
                wait(self.credit.at[at + k], 1)
            else:
                pl.semaphore_signal(self.credit.at[at + k], inc=1, device_id=self.near[axis], device_id_type=MESH)

    def z_credit(self, wait):
        @pl.when(self.has_up)
        def _():
            if wait:
                wait(self.credit.at[3], 1)
            else:
                pl.semaphore_signal(self.credit.at[2], inc=1, device_id=self.up, device_id_type=MESH)

        @pl.when(self.has_down)
        def _():
            if wait:
                wait(self.credit.at[2], 1)
            else:
                pl.semaphore_signal(self.credit.at[3], inc=1, device_id=self.down, device_id_type=MESH)

    def rs_drain(self):
        A = self.A
        for part, (order, _, rows) in enumerate(self.rs_parts):
            big = order[0] != "z"

            def sent(kind, count):
                ref = self.wb.at[0 : 2 * count, :, pl.ds(0, rows), :]
                self.remote(ref, ref, self.rs_s.at[part * 4 + kind], self.rs_r.at[0], self.sib).wait_send()

            sent(0, A - 1)
            if big:
                sent(1, A - 1)
            sent(2, 1 if big else A)
            sent(3, 2 * A)


    def share(self, ref, k):
        rows = ref.at[pl.ds(pl.multiple_of(self.c * self.T, SUB), self.T), :]
        copy = self.remote(rows, rows, self.cg_s.at[k], self.cg_r.at[k], self.sib)
        copy.start()
        return copy

    def shared(self, ref, k):
        rows = ref.at[pl.ds(pl.multiple_of((1 - self.c) * self.T, SUB), self.T), :]
        mine = ref.at[pl.ds(pl.multiple_of(self.c * self.T, SUB), self.T), :]
        self.remote(rows, rows, self.cg_s.at[k], self.cg_r.at[k], self.sib).wait_recv()
        self.remote(mine, mine, self.cg_s.at[k], self.cg_r.at[k], self.sib).wait_send()

    def rows_of(self, which):
        return pl.ds(pl.multiple_of(which * self.T, SUB), self.T)

    def give(self, k, halves):
        buf = k % 2
        for h, value in enumerate(halves(1 - self.c)):
            self.sb[buf, :, h * TILE : (h + 1) * TILE] = value.astype(BF)
        self.remote(self.sb.at[buf], self.rb.at[buf], self.ex_s.at[k], self.ex_r.at[k], self.sib).start()
        for h, value in enumerate(halves(self.c)):
            self.pacc[:, h * TILE : (h + 1) * TILE] = value

    def taken(self, k):
        buf = k % 2
        self.remote(self.sb.at[buf], self.rb.at[buf], self.ex_s.at[k], self.ex_r.at[k], self.sib).wait()


    def act_at(self, j, m):
        if self.nt == 1:
            return (j, m)
        half = self.nt // 2
        return (pl.ds(j * self.nt + m * half, half),)

    def act_get(self, j, m):
        return self.act[self.act_at(j, m)].reshape(self.T, TILE)

    def act_set(self, j, m, value):
        at = self.act_at(j, m)
        self.act[at] = value.astype(BF).reshape(self.act.at[at].shape)

    def act_all(self, j):
        return self.act[pl.ds(j * self.nt, self.nt)].reshape(2 * self.T, TILE)


    def wcol(self, b):
        return self.wb[pl.ds(b * self.nzx, self.nzx)].reshape(self.D, TILE)

    def wrow(self, b, h):
        return self.wb[pl.ds(b * self.nzx, self.nzx), h].reshape(TILE, TILE)

    def win(self, j, h):
        return self.wb[pl.ds(2 * self.A + j * self.nt, self.nt), h].reshape(TILE, TILE)

    def wout(self, j, h):
        return self.wb[pl.ds(3 * self.A + j * self.nt, self.nt), h].reshape(TILE, TILE)

    def project(self, dst, first, source, block, count):
        @pl.loop(0, count)
        def _(i):
            weight = self.wcol(block + i)
            for m in range(2):
                rows = slice(m * self.T, (m + 1) * self.T)
                dst[first + i, rows, :] = dot(source[rows, :], weight).astype(BF)


    def masks(self):
        lane = lax.broadcasted_iota(jnp.int32, (1, PAIR), 1)
        row = lax.broadcasted_iota(jnp.int32, (PAIR, 1), 0)
        return [(lane < HD), (lane >= HD)], (row < HD)

    def visible(self, tile):
        T = self.T
        key = lax.broadcasted_iota(jnp.int32, (2 * T, T), 0)
        query = lax.broadcasted_iota(jnp.int32, (2 * T, T), 1) + tile * T
        edge = self.pfx_now[0:1, 0:1]
        return jnp.logical_or(key <= query, key.astype(F32) < edge)

    def attend(self, p, qkv, o, lse, masked, point):
        T = self.T
        cols = pl.ds(pl.multiple_of(p * PAIR, PAIR), PAIR)
        heads, upper = self.masks()
        keys = qkv[1, :, cols]
        values_t = turned(qkv[2, :, cols])
        for tile in range(2):
            rows = slice(tile * T, (tile + 1) * T)
            query = qkv[0, rows, cols].astype(F32) * score_scale
            vis = self.visible(tile) if masked else None
            mixed = []
            for h in range(2):
                scores = dot_nt(keys, jnp.where(heads[h], query, 0.0).astype(BF))
                if masked:
                    scores = jnp.where(vis, scores, masked_score)
                highest = jnp.max(scores, axis=0, keepdims=True)
                exponent = jnp.exp(scores - highest)
                total = jnp.sum(exponent, axis=0, keepdims=True)
                lse[p, h : h + 1, rows] = highest + jnp.log(total)
                mixed.append(dot(values_t, exponent.astype(BF)) * (1.0 / total))
                point(2 * tile + h)
            o[rows, cols] = jnp.where(upper, mixed[0], mixed[1]).T.astype(BF)

    def attend_back(self, p, qkv, do, lse, masked, point):
        T = self.T
        cols = pl.ds(pl.multiple_of(p * PAIR, PAIR), PAIR)
        heads, upper = self.masks()
        keys, values = qkv[1, :, cols], qkv[2, :, cols]
        keys_t = turned(keys)
        dk = [0.0, 0.0]
        dv = [0.0, 0.0]
        for tile in range(2):
            rows = slice(tile * T, (tile + 1) * T)
            query = qkv[0, rows, cols]
            grad = do[rows, cols]
            query_wide = query.astype(F32) * score_scale
            grad_wide = grad.astype(F32)
            vis = self.visible(tile) if masked else None
            dq = []
            for h in range(2):
                scores = dot_nt(keys, jnp.where(heads[h], query_wide, 0.0).astype(BF))
                if masked:
                    scores = jnp.where(vis, scores, masked_score)
                probs = jnp.exp(scores - lse[p, h : h + 1, rows])
                dprobs = dot_nt(values, jnp.where(heads[h], grad_wide, 0.0).astype(BF))
                delta = jnp.sum(dprobs * probs, axis=0, keepdims=True)
                dscores = (probs * (dprobs - delta)).astype(BF)
                dq.append(dot(keys_t, dscores))
                dk[h] += dot(dscores, query)
                dv[h] += dot(probs.astype(BF), grad)
                point(2 * tile + h)
            self.dqkv[0, rows, cols] = (jnp.where(upper, dq[0], dq[1]) * score_scale).T.astype(BF)
        self.dqkv[1, :, cols] = (jnp.where(heads[0], dk[0], dk[1]) * score_scale).astype(BF)
        self.dqkv[2, :, cols] = jnp.where(heads[0], dv[0], dv[1]).astype(BF)


    def norm(self, summed):
        centred = summed - jnp.mean(summed, axis=-1, keepdims=True)
        inv = lax.rsqrt(jnp.mean(centred * centred, axis=-1, keepdims=True) + norm_eps)
        return centred * inv, inv

    def norm_back(self, k, dy, normed, inv):
        gain = self.norms[k : k + 1, :]
        self.ng[k : k + 1, :] += jnp.sum(dy * normed, axis=0, keepdims=True)
        self.ng[3 + k : 4 + k, :] += jnp.sum(dy, axis=0, keepdims=True)
        scaled = dy * gain
        plain = jnp.mean(scaled, axis=-1, keepdims=True)
        along = jnp.mean(scaled * normed, axis=-1, keepdims=True)
        return inv * (scaled - plain - normed * along)

    def norm_rows(self, body):
        @pl.loop(0, self.T // LN_ROWS)
        def _(i):
            own = pl.ds(pl.multiple_of(i * LN_ROWS, LN_ROWS), LN_ROWS)
            full = pl.ds(pl.multiple_of(self.c * self.T + i * LN_ROWS, LN_ROWS), LN_ROWS)
            body(own, full)


class Steps:
    def __init__(self, steps, limit=1e9):
        self.steps, self.limit = list(steps), limit

    def run(self, count):
        now, self.steps = self.steps[:count], self.steps[count:]
        for step in now:
            step()

    def finish(self):
        self.run(len(self.steps))

    def until(self, time):
        while self.steps and self.steps[0][0] <= min(time, self.limit):
            self.steps.pop(0)[1]()

    def timed(self, index, turns, points, start, length):
        groups = []
        for place in range(turns * points):
            time, group = start + length * (place + 1) / (turns * points), []
            while self.steps and self.steps[0][0] <= min(time, self.limit):
                group.append(self.steps.pop(0)[1])
            groups.append(group)

        def at(point):
            for turn in range(turns):
                if groups[turn * points + point]:

                    @pl.when(index == turn)
                    def _():
                        for step in groups[turn * points + point]:
                            step()

        return at

    def spread(self, index, turns, points, count=1):
        total = turns * points * count
        now, self.steps = self.steps[:total], self.steps[total:]

        def at(point):
            for turn in range(turns):
                place = (turn * points + point) * count
                if now[place : place + count]:

                    @pl.when(index == turn)
                    def _():
                        for step in now[place : place + count]:
                            step()

        return at


def kernel(A, R, T, ag_parts, rs_parts, names, *arrays):
    s = Layer(A, R, T, ag_parts, rs_parts, dict(zip(names, arrays)))
    s.land = [getattr(s, f"land{i}") for i in range(len(rs_parts))]
    D = s.D
    away = jnp.logical_not(s.kept)
    s.ng[...] = jnp.zeros_like(s.ng)
    s.pfx_own[...] = jnp.full(s.pfx_own.shape, s.pfx[0], jnp.int32).astype(F32)
    s.barrier()

    block = s.zx // s.nzx
    by_rows = jnp.logical_or(block == 3, block == 7)
    mine = pl.ds(pl.multiple_of(s.y * R, SUB), R)
    half = [pl.ds(pl.multiple_of(h * TILE, TILE), TILE) for h in (0, 1, s.c, 1 - s.c)]
    ffn_copies = [
        pltpu.make_async_copy(s.ffn_rows.at[:, half[h]], s.wb.at[2 * A + s.zx, h, mine, :], s.lc.at[h]) for h in (0, 1)
    ]
    rows_copies = [
        pltpu.make_async_copy(s.attn_rows.at[:, half[h]], s.wb.at[s.zx, h, mine, :], s.lc.at[2 + h]) for h in (0, 1)
    ]
    half_copy = pltpu.make_async_copy(s.attn_rows.at[:, half[2]], s.wb.at[s.zx, s.c, mine, :], s.lc.at[2])
    half_send = s.remote(
        s.attn_rows.at[:, half[3]], s.wb.at[s.zx, s.c, mine, :], s.misc_s.at[0], s.misc_r.at[0], s.sib
    )
    half_recv = s.remote(
        s.attn_rows.at[:, half[3]], s.wb.at[s.zx, 1 - s.c, mine, :], s.misc_s.at[0], s.misc_r.at[0], s.sib
    )
    for copy in ffn_copies:
        copy.start()

    @pl.when(by_rows)
    def _():
        for copy in rows_copies:
            copy.start()

    @pl.when(jnp.logical_not(by_rows))
    def _():
        half_copy.start()
        half_send.start()

    here = s.rows_of(s.c)
    there = s.rows_of(s.y)
    swaps = [
        (s.tokens, s.xf.at[here, :], s.xf.at[there, :]),
        (s.memory, s.mf.at[here, :], s.mf.at[there, :]),
        (s.pfx_own, s.pfx_now, s.pfx_now),
        (s.cot, s.cotb, s.cotb),
    ]

    def swap(i):
        src, dst, far = swaps[i]

        @pl.when(s.kept)
        def _():
            pltpu.make_async_copy(src, dst, s.lc.at[4 + i]).start()

        @pl.when(away)
        def _():
            s.remote(src, far, s.sw_s.at[i], s.sw_r.at[i], s.partner).start()

    swap(0)
    swap(1)
    swap(2)

    @pl.when(by_rows)
    def _():
        for copy in rows_copies:
            copy.wait()

    @pl.when(jnp.logical_not(by_rows))
    def _():
        half_copy.wait()
        half_send.wait_send()
        half_recv.wait_recv()

    gather, ffn = Steps(s.ag(0)), Steps(s.ag(1))
    gather.run(2)

    def swapped(i):
        src, dst, far = swaps[i]

        @pl.when(s.kept)
        def _():
            pltpu.make_async_copy(src, dst, s.lc.at[4 + i]).wait()

        @pl.when(away)
        def _():
            s.remote(src, far, s.sw_s.at[i], s.sw_r.at[i], s.partner).wait_send()
            s.remote(src, dst, s.sw_s.at[i], s.sw_r.at[i], s.partner).wait_recv()

    gather.run(14)
    for copy in ffn_copies:
        copy.wait()
    ffn.run(1)
    gather.run(14)
    ffn.run(1)
    swap(3)
    for i in range(3):
        swapped(i)
    s.share(s.xf, 0)
    s.share(s.mf, 1)
    gather.finish()
    s.shared(s.xf, 0)
    s.shared(s.mf, 1)

    s.project(s.qkv1, 0, s.xf, 0, 3)
    ffn.run(2)
    s.project(s.qkv2, 1, s.mf, 5, 2)
    ffn.run(2)

    @pl.loop(0, TILE // PAIR)
    def _(p):
        s.attend(p, s.qkv1, s.o1, s.lse1, True, ffn.spread(p, TILE // PAIR, 4))

    def branch(o, b):
        return lambda which: [dot(o[s.rows_of(which), :], s.wrow(b, h)) for h in range(2)]

    s.give(0, branch(s.o1, 3))
    ffn.run(1)
    s.taken(0)

    def first_norm(own, full):
        summed = alpha_scale * s.xf[full, :].astype(F32) + s.pacc[own, :] + s.rb[0, own, :].astype(F32)
        normed, inv = s.norm(summed)
        s.dtok[own, :] = normed
        s.inv1[own, :] = inv
        result = normed * s.norms[0:1, :] + s.norms[3:4, :]
        s.nbuf[own, :] = result
        s.n1r[full, :] = result.astype(BF)

    s.norm_rows(first_norm)
    s.share(s.n1r, 2)
    ffn.run(2)
    s.shared(s.n1r, 2)

    s.project(s.qkv2, 0, s.n1r, 4, 1)

    @pl.loop(0, TILE // PAIR)
    def _(p):
        s.attend(p, s.qkv2, s.o2, s.lse2, False, ffn.spread(p, TILE // PAIR, 4))

    s.give(1, branch(s.o2, 7))
    ffn.run(1)
    s.taken(1)

    def second_norm(own, full):
        summed = alpha_scale * s.nbuf[own, :] + s.pacc[own, :] + s.rb[1, own, :].astype(F32)
        normed, inv = s.norm(summed)
        s.dmem[own, :] = normed
        s.inv2[own, :] = inv
        result = normed * s.norms[1:2, :] + s.norms[4:5, :]
        s.nbuf[own, :] = result
        s.n2r[full, :] = result.astype(BF)

    s.norm_rows(second_norm)
    s.share(s.n2r, 3)
    ffn.run(2)
    s.shared(s.n2r, 3)
    ffn.finish()
    swapped(3)

    tiles = 2 * A * R // TILE

    @pl.loop(0, tiles)
    def _(j):
        for m in range(2):
            rows = slice(m * T, (m + 1) * T)
            pre = dot_nt(s.n2r[rows, :TILE], s.win(j, 0)) + dot_nt(s.n2r[rows, TILE:], s.win(j, 1))
            gate = 1.0 / (1.0 + jnp.exp(-pre))
            s.act_set(tiles + j, m, pre * gate)
            s.act_set(j, m, gate * (1.0 + pre * (1.0 - gate)))

    def ffn_out(which):
        return [sum(dot(s.act_get(tiles + j, which), s.wout(j, h)) for j in range(tiles)) for h in range(2)]

    s.give(2, ffn_out)
    s.taken(2)

    def third_norm(own, full):
        summed = alpha_scale * s.nbuf[own, :] + s.pacc[own, :] + s.rb[0, own, :].astype(F32)
        normed, inv = s.norm(summed)
        result = normed * s.norms[2:3, :] + s.norms[5:6, :]
        s.out[own, :] = result
        s.osb[0, own, :] = result.astype(BF)
        grad = s.norm_back(2, s.cotb[own, :].astype(F32), normed, inv)
        s.nbuf[own, :] = grad
        s.ga[full, :] = grad.astype(BF)

    s.norm_rows(third_norm)
    s.share(s.ga, 4)

    def send_back(k):
        @pl.when(away)
        def _():
            s.remote(s.osb.at[k], s.orb.at[k], s.ob_s.at[k], s.ob_r.at[k], s.partner).start()

    send_back(0)
    s.ag_drain()
    s.shared(s.ga, 4)

    @pl.loop(0, tiles)
    def _(j):
        for m in range(2):
            rows = slice(m * T, (m + 1) * T)
            da = dot_nt(s.ga[rows, :TILE], s.wout(j, 0)) + dot_nt(s.ga[rows, TILE:], s.wout(j, 1))
            s.act_set(j, m, da * s.act_get(j, m).astype(F32))

    def ffn_in(which):
        return [sum(dot(s.act_get(j, which), s.win(j, h)) for j in range(tiles)) for h in range(2)]

    s.give(3, ffn_in)

    @pl.loop(0, tiles)
    def _(j):
        hidden, grads = s.act_all(tiles + j), s.act_all(j)
        for h in range(2):
            cols = slice(h * TILE, (h + 1) * TILE)
            out_rows = dot_tn(hidden, s.ga[:, cols]).astype(BF)
            s.wb[pl.ds(3 * A + j * s.nt, s.nt), h] = out_rows.reshape(s.nt, 2 * R, TILE)
            in_rows = dot_tn(grads, s.n2r[:, cols]).astype(BF)
            s.wb[pl.ds(2 * A + j * s.nt, s.nt), h] = in_rows.reshape(s.nt, 2 * R, TILE)

    s.f_credit(None, 0)
    spread = Steps(s.rs(s.dffn, s.fin), ACROSS * A)
    spread.until(0.0)
    s.taken(3)

    def second_back(own, full):
        dy = alpha_scale * s.nbuf[own, :] + s.pacc[own, :] + s.rb[1, own, :].astype(F32)
        grad = s.norm_back(1, dy, s.dmem[own, :], s.inv2[own, :])
        s.nbuf[own, :] = grad
        s.gb[full, :] = grad.astype(BF)

    s.norm_rows(second_back)
    s.share(s.gb, 5)
    spread.until(3.0)
    s.shared(s.gb, 5)

    def mixed_back(grad, o, b):
        for m in range(2):
            rows = slice(m * T, (m + 1) * T)
            s.do[rows, :] = (
                dot_nt(grad[rows, :TILE], s.wrow(b, 0)) + dot_nt(grad[rows, TILE:], s.wrow(b, 1))
            ).astype(BF)
        for h in range(2):
            cols = slice(h * TILE, (h + 1) * TILE)
            terms = dot_tn(o[...], grad[:, cols]).astype(BF)
            s.wb[pl.ds(b * s.nzx, s.nzx), h] = terms.reshape(s.nzx, 2 * R, TILE)

    def weight_terms(b, source, grad):
        for h in range(2):
            cols = slice(h * TILE, (h + 1) * TILE)
            terms = dot_tn(source[:, cols], grad).astype(BF)
            half = s.nzx // 2 if s.nzx > 1 else 0
            if half:
                s.wb[pl.ds(b * s.nzx + h * half, half)] = terms.reshape(half, 2, 2 * R, TILE)
            else:
                s.wb[b, h] = terms

    def spread_back(which, blocks):
        rows = s.rows_of(which)
        halves = []
        for h in range(2):
            total = 0.0
            for b, k in blocks:
                total += dot_nt(s.dqkv[k, rows, :], s.wcol(b)[h * TILE : (h + 1) * TILE])
            halves.append(total)
        return halves

    mixed_back(s.gb, s.o2, 7)
    spread.until(5.0)

    @pl.loop(0, TILE // PAIR)
    def _(p):
        s.attend_back(p, s.qkv2, s.do, s.lse2, False, spread.timed(p, TILE // PAIR, 4, 5.0, 8.0))

    s.give(4, lambda which: spread_back(which, [(5, 1), (6, 2)]))
    spread.until(15.0)
    s.taken(4)

    def memory_rows(own, full):
        total = s.pacc[own, :] + s.rb[0, own, :].astype(F32)
        s.dmem[own, :] = total
        s.osb[1, own, :] = total.astype(BF)

    s.norm_rows(memory_rows)
    send_back(1)
    s.give(5, lambda which: spread_back(which, [(4, 0)]))
    spread.until(18.0)
    weight_terms(4, s.n1r, s.dqkv[0])
    weight_terms(5, s.mf, s.dqkv[1])
    weight_terms(6, s.mf, s.dqkv[2])
    spread.until(21.0)
    s.taken(5)

    def first_back(own, full):
        dy = alpha_scale * s.nbuf[own, :] + s.pacc[own, :] + s.rb[1, own, :].astype(F32)
        grad = s.norm_back(0, dy, s.dtok[own, :], s.inv1[own, :])
        s.nbuf[own, :] = grad
        s.ga[full, :] = grad.astype(BF)

    s.norm_rows(first_back)
    s.share(s.ga, 6)
    spread.until(24.0)
    s.shared(s.ga, 6)

    def norm_sum():
        for k, device in enumerate((s.sib, s.near["x"], s.near["y"])):
            copy = s.remote(s.ngs.at[k], s.ngr.at[k], s.nm_s.at[k], s.nm_r.at[k], device)
            s.ngs[k] = s.ng[...]
            copy.start()
            yield
            copy.wait()
            s.ng[...] = s.ng[...] + s.ngr[k]
        s.ngz[s.z] = s.ng[...]
        for other in range(A):

            @pl.when(s.z != other)
            def _():
                s.remote(
                    s.ng, s.ngz.at[s.z], s.nm_s.at[3 + other], s.nm_r.at[3 + s.z],
                    (s.dp + 4 * (other - s.z), s.y),
                ).start()

        yield
        for other in range(A):

            @pl.when(s.z != other)
            def _():
                s.remote(s.ng, s.ngz.at[other], s.nm_s.at[3 + other], s.nm_r.at[3 + other], s.sib).wait()

        total = s.ngz[0]
        for other in range(1, A):
            total = total + s.ngz[other]
        s.dnorm[...] = total[:6, :]
        yield

    sums = norm_sum()
    next(sums)

    mixed_back(s.ga, s.o1, 3)
    spread.until(27.0)
    next(sums)

    @pl.loop(0, TILE // PAIR)
    def _(p):
        s.attend_back(p, s.qkv1, s.do, s.lse1, True, spread.timed(p, TILE // PAIR, 4, 27.0, 9.0))

    next(sums)
    s.give(6, lambda which: spread_back(which, [(0, 0), (1, 1), (2, 2)]))
    next(sums)

    @pl.loop(0, 3)
    def _(k):
        weight_terms(k, s.xf, s.dqkv[k])

    next(sums, None)
    s.taken(6)

    def token_rows(own, full):
        total = alpha_scale * s.nbuf[own, :] + s.pacc[own, :] + s.rb[0, own, :].astype(F32)
        s.dtok[own, :] = total
        s.osb[2, own, :] = total.astype(BF)

    s.norm_rows(token_rows)
    send_back(2)
    spread.until(1e9)
    s.f_credit(pl.semaphore_wait, 0)
    spread.limit = 1e9
    spread.until(ACROSS * A + 4.0)

    @pl.when(away)
    def _():
        for k, dst in enumerate((s.out, s.dmem, s.dtok)):
            s.remote(s.osb.at[k], s.orb.at[k], s.ob_s.at[k], s.ob_r.at[k], s.partner).wait()

            @pl.loop(0, T // LN_ROWS)
            def _(i):
                own = pl.ds(pl.multiple_of(i * LN_ROWS, LN_ROWS), LN_ROWS)
                dst[own, :] = s.orb[k, own, :].astype(F32)

    spread.until(1e9)

    tail_send = s.remote(
        s.fin.at[:, half[3]], s.dattn.at[:, half[2]], s.misc_s.at[1], s.misc_r.at[1], s.sib
    )
    tail_recv = s.remote(
        s.fin.at[:, half[3]], s.dattn.at[:, half[3]], s.misc_s.at[1], s.misc_r.at[1], s.sib
    )

    @pl.when(by_rows)
    def _():
        s.dattn[...] = s.fin[...]

    @pl.when(jnp.logical_not(by_rows))
    def _():
        tail_send.start()
        s.dattn[:, half[2]] = s.fin[:, half[2]]
        tail_send.wait_send()
        tail_recv.wait_recv()

    s.rs_drain()


def hand_on(*refs):
    for src, dst in zip(refs[: len(refs) // 2], refs[len(refs) // 2 :]):
        dst[...] = src[...]


def hand_specs(outputs):
    return [
        pl.BlockSpec(shape, lambda i: (0, 0))
        if shape[0] % (8 * HANDS)
        else pl.BlockSpec((shape[0] // HANDS, shape[1]), lambda i: (i, 0))
        for shape in outputs.values()
    ]


def on_device(A, tokens, memory, attn_bank, ffn_bank, norm_params, prefix, cotangent):
    T, D = tokens.shape
    R = attn_bank.shape[0]
    ag_parts, rs_parts = cut(R, GATHER), cut(R, SCATTER)
    groups = D // (4 * R)
    tiles = 2 * A * R // TILE

    block = (lax.axis_index("dp") // 2) // groups
    by_rows = jnp.logical_or(block == 3, block == 7)
    attn_rows = attn_bank
    if groups > 1:
        by_core = attn_bank.reshape(R, groups, 2, 2 * R).transpose(0, 2, 1, 3).reshape(R, D)
        attn_rows = jnp.where(by_rows, attn_bank, by_core)
    slots = sum(landing(order, A) for order, _, _ in rs_parts)

    inputs = dict(
        tokens=tokens,
        memory=memory,
        cot=cotangent,
        pfx=prefix,
        attn_rows=attn_rows,
        ffn_rows=ffn_bank,
        norms=norm_params,
    )
    where = dict(pfx=pltpu.SMEM, norms=pltpu.VMEM)
    outputs = dict(
        out=(T, D), dtok=(T, D), dmem=(T, D), dattn=(R, D), dffn=(R, D), dnorm=(6, D)
    )
    wide = lambda *shape: pltpu.VMEM(shape, F32)
    low = lambda *shape: pltpu.VMEM(shape, BF)
    dma = lambda count: pltpu.SemaphoreType.DMA((count,))
    scratch = dict(
        wb=low(4 * A, 2, 2 * R, TILE),
        xf=low(2 * T, D),
        mf=low(2 * T, D),
        n1r=low(2 * T, D),
        n2r=low(2 * T, D),
        ga=low(2 * T, D),
        gb=low(2 * T, D),
        cotb=low(T, D),
        act=low(2 * A, 2, R, TILE),
        qkv1=low(3, 2 * T, TILE),
        qkv2=low(3, 2 * T, TILE),
        dqkv=low(3, 2 * T, TILE),
        o1=low(2 * T, TILE),
        o2=low(2 * T, TILE),
        do=low(2 * T, TILE),
        sb=low(2, T, D),
        rb=low(2, T, D),
        osb=low(3, T, D),
        orb=low(3, T, D),
        nbuf=wide(T, D),
        pacc=wide(T, D),
        fin=wide(R, D),
        pfx_own=wide(8, 128),
        pfx_now=wide(8, 128),
        lse1=wide(TILE // PAIR, 8, 2 * T),
        lse2=wide(TILE // PAIR, 8, 2 * T),
        inv1=wide(T, 1),
        inv2=wide(T, 1),
        ng=wide(8, D),
        ngs=wide(3, 8, D),
        ngr=wide(3, 8, D),
        ngz=wide(A, 8, D),
        lc=dma(8),
        misc_s=dma(2),
        misc_r=dma(2),
        sw_s=dma(4),
        sw_r=dma(4),
        ag_s=dma(len(ag_parts) * 4),
        ag_r=dma(2 * len(ag_parts) * (2 * A + 1)),
        rs_s=dma(len(rs_parts) * 4),
        rs_r=dma(slots + len(rs_parts) * 2 * A),
        cg_s=dma(7),
        cg_r=dma(7),
        ex_s=dma(7),
        ex_r=dma(7),
        ob_s=dma(3),
        ob_r=dma(3),
        nm_s=dma(3 + A),
        nm_r=dma(3 + A),
        credit=pltpu.SemaphoreType.REGULAR((6,)),
    )
    for i, (order, _, rows) in enumerate(rs_parts):
        scratch[f"land{i}"] = low(landing(order, A), 2, rows, TILE)
    names = list(inputs) + list(outputs) + list(scratch)
    results = pl.pallas_call(
        functools.partial(kernel, A, R, T, ag_parts, rs_parts, names),
        out_shape=[jax.ShapeDtypeStruct(shape, F32) for shape in outputs.values()],
        in_specs=[pl.BlockSpec(memory_space=where.get(n, pl.ANY)) for n in inputs],
        out_specs=[pl.BlockSpec(memory_space=pltpu.VMEM)] * len(outputs),
        scratch_shapes=list(scratch.values()),
        compiler_params=pltpu.CompilerParams(
            collective_id=0, has_side_effects=True, vmem_limit_bytes=64 * 2**20
        ),
        name="layer",
    )(*inputs.values())

    results = pl.pallas_call(
        hand_on,
        grid=(HANDS,),
        out_shape=[jax.ShapeDtypeStruct(shape, F32) for shape in outputs.values()],
        in_specs=hand_specs(outputs),
        out_specs=hand_specs(outputs),
        name="hand_on",
    )(*results)
    out, dtok, dmem, dattn, dffn, dnorm = results
    if groups > 1:
        by_core = dattn.reshape(R, 2, groups, 2 * R).transpose(0, 2, 1, 3).reshape(R, D)
        dattn = jnp.where(by_rows, dattn, by_core)
    return (out, dtok, dmem, dattn, dffn, dnorm)


def solution(mesh):
    rows = P(("dp", "seq"), None)
    return jax.shard_map(
        functools.partial(on_device, mesh.shape["dp"] // 4),
        mesh=mesh,
        in_specs=(rows, rows, rows, rows, P(), P("dp"), rows),
        out_specs=(rows, rows, rows, rows, rows, P()),
        check_vma=False,
    )
```

```python
import functools

import jax
import jax.numpy as jnp
from jax import lax
from jax.experimental import pallas as pl
from jax.experimental.pallas import tpu as pltpu
from jax.sharding import PartitionSpec as P

HD = 64
PAIR = 2 * HD
TILE = 512
SUB = 16
LN_ROWS = 32
HANDS = 4
AHEAD = 8
ACROSS = 11.63
ALONG = 12.12
HOP = 9.52
LAG_BIG = 0.06
LAG_SMALL = 0.71
START = 12.51
FIRST = 3.0
SECOND = 10.05
MIDDLE = 85.0
EARLY = 5.87
COME = 10.6
PLANE = 13.85
STEP = 1.58
BESIDE = 9.75
CROSS = 10.02
SECOND_BANK = 51.38
SWAPS = 35.59
LATE_SWAP = 64.42
GATHERED = 66.95
RATE = 1.06
GATHER = (5, 6, 2, 3)
SCATTER = (4, 6, 3, 3)

alpha_scale = 300.0**0.25
norm_eps = 1e-05
masked_score = -1e30
score_scale = HD**-0.5

BF = jnp.bfloat16
F32 = jnp.float32
MESH = pl.DeviceIdType.MESH


def dot(left, right):
    return jnp.dot(left, right, preferred_element_type=F32)


def dot_nt(left, right):
    return lax.dot_general(left, right, (((1,), (1,)), ((), ())), preferred_element_type=F32)


def dot_tn(left, right):
    return lax.dot_general(left, right, (((0,), (0,)), ((), ())), preferred_element_type=F32)


def turned(block):
    return block.astype(F32).T.astype(BF)


def cut(rows, split):
    units = rows // SUB
    shares = [(units * share + 8) // 16 for share in split[1:]]
    sizes = list(zip(("xzy", "yzx", "zxy", "zyx"), [units - sum(shares)] + shares))
    parts, start = [], 0
    for order, size in sizes:
        if size > 0:
            parts.append((order, start * SUB, size * SUB))
        start += size
    return parts


def slots_of(order, A):
    return 4 * A + 3 if order[0] != "z" else 4 * A + 1


def landing(order, A):
    return slots_of(order, A) + (3 if order[0] != "z" else 1)


class Layer:
    def __init__(self, A, R, T, ag_parts, rs_parts, refs):
        self.A, self.R, self.T = A, R, T
        self.ag_parts, self.rs_parts = ag_parts, rs_parts
        self.D = 1024
        self.nzx = self.D // (4 * R)
        self.nt = TILE // (2 * R)
        for name, ref in refs.items():
            setattr(self, name, ref)
        self.dp, self.y = lax.axis_index("dp"), lax.axis_index("seq")
        self.c = lax.rem(self.dp, 2)
        self.x = lax.rem(self.dp // 2, 2)
        self.z = self.dp // 4
        self.zx = self.dp // 2
        self.sib = (self.dp + 1 - 2 * self.c, self.y)
        self.near = {"x": (self.dp + 2 - 4 * self.x, self.y), "y": (self.dp, 1 - self.y)}
        self.up = (self.dp + 4, self.y)
        self.down = (self.dp - 4, self.y)
        self.partner = (self.dp - self.c + self.y, self.c)
        self.has_up = self.z < A - 1
        self.has_down = self.z > 0
        self.kept = self.c == self.y
        self.turns = [self.turn(j) for j in range(A)]


    def remote(self, src, dst, send, recv, device):
        return pltpu.make_async_remote_copy(
            src_ref=src, dst_ref=dst, send_sem=send, recv_sem=recv, device_id=device, device_id_type=MESH
        )

    def own(self, axis):
        return self.x if axis == "x" else self.y

    def spot(self, bank, part, z, x, y):
        order, start, rows = part
        row = pl.multiple_of(y * self.R + start, SUB)
        return self.wb.at[bank * 2 * self.A + z * 2 + x, :, pl.ds(row, rows), :]

    def place(self, axis, f, l):
        return (f, l) if axis == "x" else (l, f)


    def barrier(self):
        bar = pltpu.get_barrier_semaphore()

        def greet(device):
            pl.semaphore_signal(bar, inc=1, device_id=device, device_id_type=MESH)

        greet(self.sib)
        greet(self.near["x"])
        greet(self.near["y"])
        for other in range(self.A):

            @pl.when(self.z != other)
            def _():
                greet((self.dp + 4 * (other - self.z), self.y))

        @pl.when(jnp.logical_not(self.kept))
        def _():
            greet(self.partner)
            pl.semaphore_wait(bar, 3 + self.A)

        @pl.when(self.kept)
        def _():
            pl.semaphore_wait(bar, 2 + self.A)


    def ag_index(self, bank, part, z, x, y, last):
        base = (bank * len(self.ag_parts) + part) * (2 * self.A + 1)
        if last:
            return base + 2 * self.A
        return base + z * 2 + (x if self.ag_parts[part][0][2] == "y" else y)

    def ag_send(self, bank, part, z, x, y, kind, device):
        ref = self.spot(bank, self.ag_parts[part], z, x, y)
        recv = self.ag_r.at[self.ag_index(bank, part, z, x, y, kind == 3)]
        self.remote(ref, ref, self.ag_s.at[part * 4 + kind], recv, device).start()

    def ag_wait(self, bank, part, z, x, y):
        ref = self.spot(bank, self.ag_parts[part], z, x, y)
        recv = self.ag_r.at[self.ag_index(bank, part, z, x, y, False)]
        self.remote(ref, ref, self.ag_s.at[0], recv, self.sib).wait_recv()

    def ag_last(self, bank, part):
        _, _, rows = self.ag_parts[part]
        ref = self.wb.at[0 : 2 * self.A, :, pl.ds(0, rows), :]
        recv = self.ag_r.at[self.ag_index(bank, part, 0, 0, 0, True)]
        self.remote(ref, ref, self.ag_s.at[0], recv, self.sib).wait_recv()

    def ag(self, bank, start, latest=1e9):
        A = self.A
        info = self.orders(self.ag_parts)

        def z_sends(part, f, fc, lc, w):
            px, py = self.place(f, fc, lc)

            @pl.when(self.has_up)
            def _():
                self.ag_send(bank, part, self.z, px, py, w, self.up)

            @pl.when(self.has_down)
            def _():
                self.ag_send(bank, part, self.z, px, py, w, self.down)

        def send(part, f, fc, lc, z, kind, axis):
            px, py = self.place(f, fc, lc)
            self.ag_send(bank, part, z, px, py, kind, self.near[axis])

        def early():
            for part, big, f, l, fo, lo in info:
                if big:
                    send(part, f, fo, lo, self.z, 2, f)

        def begin():
            for part, big, f, l, fo, lo in info:
                z_sends(part, f, fo, lo, 0)
            for part, big, f, l, fo, lo in info:
                if not big:
                    send(part, f, fo, lo, self.z, 2, f)
                send(part, f, fo, lo, self.z, 3, l)

        def beside(part, big, f, l, fo, lo):
            px, py = self.place(f, 1 - fo, lo)
            self.ag_wait(bank, part, self.z, px, py)
            z_sends(part, f, 1 - fo, lo, 1)
            send(part, f, 1 - fo, lo, self.z, 3, l)

        def arrive(d, w, part, big, f, l, fo, lo):
            fc = fo if w == 0 else 1 - fo
            px, py = self.place(f, fc, lo)

            def arrived(z, on, device):
                self.ag_wait(bank, part, z, px, py)

                @pl.when(on)
                def _():
                    self.ag_send(bank, part, z, px, py, w, device)

                if not big:
                    send(part, f, fc, lo, z, 2, f)
                send(part, f, fc, lo, z, 3, l)

            @pl.when(self.z >= d)
            def _():
                arrived(self.z - d, self.has_up, self.up)

            @pl.when(self.z + d < A)
            def _():
                arrived(self.z + d, self.has_down, self.down)

        def cross(d, part, big, f, l, fo, lo):
            px, py = self.place(f, 1 - fo, lo)

            def crossed(z):
                self.ag_wait(bank, part, z, px, py)
                send(part, f, 1 - fo, lo, z, 3, l)

            self.planes_at(d, crossed)

        bigs = [row for row in info if row[1]]
        smalls = [row for row in info if not row[1]]
        due = [(start - EARLY, early), (start, begin)]
        for d in range(1, A):
            for k, row in enumerate(info):
                come = start + COME + PLANE * (d - 1) + STEP * k
                due.append((come, functools.partial(arrive, d, 0, *row)))
                if row[1]:
                    side = start + BESIDE + STEP * k
                    if d == 1:
                        due.append((side, functools.partial(beside, *row)))
                    due.append((max(come + STEP * len(info), side + 0.1), functools.partial(arrive, d, 1, *row)))
                else:
                    if d == 1:
                        due.append((start + CROSS + STEP * k, functools.partial(cross, 0, *row)))
                    over = start + CROSS + PLANE * d + STEP * k
                    due.append((max(over, come + 0.1), functools.partial(cross, d, *row)))
        return [(min(time, latest), step) for time, step in due]

    def planes_at(self, d, act):
        if d == 0:
            act(self.z)
            return

        @pl.when(self.z >= d)
        def _():
            act(self.z - d)

        @pl.when(self.z + d < self.A)
        def _():
            act(self.z + d)

    def orders(self, parts):
        info = []
        for part, (order, _, _) in enumerate(parts):
            l = order[2]
            f = "x" if l == "y" else "y"
            info.append((part, order[0] != "z", f, l, self.own(f), self.own(l)))
        return info

    def ag_drain(self):
        A = self.A
        inner = jnp.logical_and(self.has_up, self.has_down)
        for part, (order, _, rows) in enumerate(self.ag_parts):
            big = order[0] != "z"

            def sent(kind, count):
                ref = self.wb.at[0 : 2 * count, :, pl.ds(0, rows), :]
                self.remote(ref, ref, self.ag_s.at[part * 4 + kind], self.ag_r.at[0], self.sib).wait_send()

            for kind in (0, 1) if big else (0,):

                @pl.when(inner)
                def _():
                    sent(kind, A + 1)

                @pl.when(jnp.logical_not(inner))
                def _():
                    sent(kind, 1)

            sent(2, 1 if big else A)
            sent(3, 2 * A)


    def turn(self, j):
        A = self.A
        mirrored = self.z >= A // 2
        w = jnp.where(mirrored, A - 1 - self.z, self.z)
        d = jnp.where(j < A - 1 - w, A - 1 - j, jnp.where(j < A - 1, j - (A - 1 - w), w))
        return jnp.where(mirrored, A - 1 - d, d)

    def rs_land(self, bank, part, slot, first):
        if bank == 0 and first:
            _, start, rows = self.rs_parts[part]
            return self.act.at[slot, :, start : start + rows, :]
        return self.land[part].at[slot]

    def rs_index(self, bank, part, slot, first):
        room = [landing(order, self.A) for order, _, _ in self.rs_parts]
        if bank == 0 and first:
            return sum(room) + part * 2 * self.A + slot
        return sum(room[:part]) + slot

    def rs_send(self, bank, part, z, x, y, slot, kind, device):
        sem = part * 4 + kind
        self.remote(
            self.spot(bank, self.rs_parts[part], z, x, y),
            self.rs_land(bank, part, slot, kind == 3),
            self.rs_s.at[sem],
            self.rs_r.at[self.rs_index(bank, part, slot, kind == 3)],
            device,
        ).start()

    def rs_add(self, bank, part, z, x, y, slot, out=None, first=False):
        landed = self.rs_land(bank, part, slot, first)
        self.remote(
            landed, landed, self.rs_s.at[0], self.rs_r.at[self.rs_index(bank, part, slot, first)], self.sib
        ).wait_recv()
        order, start, rows = self.rs_parts[part]
        at = bank * 2 * self.A + z * 2 + x
        row = pl.multiple_of(y * self.R + start, SUB)

        @pl.loop(0, 2)
        def _(h):
            total = self.wb[at, h, pl.ds(row, rows), :].astype(F32) + landed[h].astype(F32)
            if out is None:
                self.wb[at, h, pl.ds(row, rows), :] = total.astype(BF)
            else:
                out[start : start + rows, pl.ds(pl.multiple_of(h * TILE, TILE), TILE)] = total

    def rs_firsts(self, bank):
        sends = []

        def send(z, w, part, big, f, l, fo, lo):
            fc = fo if w == 0 else 1 - fo
            px, py = self.place(f, fc, 1 - lo)
            self.rs_send(bank, part, z, px, py, z * 2 + fc, 3, self.near[l])

        for z in self.turns:
            for row in self.orders(self.rs_parts):
                for w in (1, 0):
                    sends.append(functools.partial(send, z, w, *row))
        return sends

    def rs_slot(self, bank, part, slot):
        if bank == 1:
            return slot
        A = self.A
        more = slots_of(self.rs_parts[part][0], A)
        slot = slot - 2 * A
        return jnp.where(slot < 2 * A, slot, slot - 2 * A + more)

    def chain(self, bank, part, big, f, fc, lo, w, z, final):
        A = self.A
        base = 2 * A + w * (A + 1) if big else 3 * A
        px, py = self.place(f, fc, lo)

        def slot(k):
            return self.rs_slot(bank, part, base + k)

        def onward(device, next_z, up):
            self.rs_send(bank, part, z, px, py, slot(z if up else jnp.where(z == next_z, A, z)), w, device)

        @pl.when(z > self.z)
        def _():
            @pl.when(self.has_down)
            def _():
                self.rs_add(bank, part, z, px, py, slot(z))

            onward(self.up, self.z + 1, True)

        @pl.when(z < self.z)
        def _():
            @pl.when(self.has_up)
            def _():
                self.rs_add(bank, part, z, px, py, slot(z))

            onward(self.down, self.z - 1, False)

        @pl.when(z == self.z)
        def _():
            inner = jnp.logical_and(self.has_down, self.has_up)

            @pl.when(inner)
            def _():
                self.rs_add(bank, part, z, px, py, slot(z))
                self.rs_add(bank, part, z, px, py, slot(A), final)

            @pl.when(jnp.logical_not(inner))
            def _():
                self.rs_add(bank, part, z, px, py, slot(jnp.where(self.has_down, z, A)), final)

    def rs_across(self, bank, j, sends, start):
        A, z = self.A, self.turns[j]

        def across(w, more, part, big, f, l, fo, lo):
            fc = fo if w == 0 else 1 - fo
            px, py = self.place(f, fc, lo)
            self.rs_add(bank, part, z, px, py, z * 2 + fc, first=True)
            if more:
                more()
            if w == 1 and not big:
                self.rs_send(bank, part, z, px, py, self.rs_slot(bank, part, 2 * A + z), 2, self.near[f])

        rows = [(w, row) for row in self.orders(self.rs_parts) for w in (1, 0)]
        return [
            (
                start + ACROSS * (j + (k + 1) / len(rows)),
                functools.partial(across, w, sends.pop(0) if sends else None, *row),
            )
            for k, (w, row) in enumerate(rows)
        ]

    def rs_along(self, bank, j, out, first, start):
        A, z = self.A, self.turns[j]
        at_end = jnp.logical_not(jnp.logical_and(self.has_up, self.has_down))

        def along(w, part, big, f, l, fo, lo):
            if big:
                self.chain(bank, part, big, f, fo if w == 0 else 1 - fo, lo, w, z, None)
            else:
                px, py = self.place(f, fo, lo)
                self.rs_add(bank, part, z, px, py, self.rs_slot(bank, part, 2 * A + z))
                self.chain(bank, part, big, f, fo, lo, 0, z, out if j == A - 1 else None)

        def only(role, step):
            @pl.when(role)
            def _():
                step()

        orders = self.orders(self.rs_parts)
        rows = [(w, row) for row in orders if row[1] for w in (1, 0)] + [(0, row) for row in orders if not row[1]]
        plane = min(j, A - 2 + (0.0 if j == A - 1 else -0.5))
        steps = []
        for k, (w, row) in enumerate(rows):
            step = functools.partial(along, w, *row)
            inner = start + ALONG * (plane + (k + 1) / len(rows)) + HOP
            lag = LAG_BIG if row[1] else LAG_SMALL
            end = first + ACROSS * (j + lag + (k + 1) / len(rows))
            if j == A - 1:
                steps.append((max(inner, end), step))
            else:
                steps.append((max(inner, end), functools.partial(only, jnp.logical_not(at_end), step)))
                steps.append((end, functools.partial(only, at_end, step)))
        return steps

    def rs_last(self, bank, out):
        A = self.A

        def go():
            for part, big, f, l, fo, lo in self.orders(self.rs_parts):
                if big:
                    px, py = self.place(f, 1 - fo, lo)
                    self.rs_send(bank, part, self.z, px, py, self.rs_slot(bank, part, 4 * A + 2), 2, self.near[f])

        def come(part, big, f, l, fo, lo):
            px, py = self.place(f, fo, lo)
            self.rs_add(bank, part, self.z, px, py, self.rs_slot(bank, part, 4 * A + 2), out)

        return [go] + [functools.partial(come, *row) for row in self.orders(self.rs_parts) if row[1]]

    def rs_ready(self):
        for go in (None, pl.semaphore_wait):
            self.z_credit(go)
            self.f_credit(go, 4)

    def rs(self, out1, out0):
        A = self.A
        due = []
        for bank, out, first, start in ((1, out1, 0.0, START), (0, out0, ACROSS * A + FIRST, ALONG * (A - 1) + SECOND)):
            sends = self.rs_firsts(bank)
            due += [(first if bank else first - FIRST / 4, step) for step in sends[:AHEAD]]
            sends = sends[AHEAD:]
            for j in range(A):
                due += self.rs_across(bank, j, sends, first)
                due += self.rs_along(bank, j, out, first, start)
            done = start + ALONG * (A - 1) + HOP
            go, *come = self.rs_last(bank, out)
            due += [(done, go)] + [(done + 2 * HOP, step) for step in come]
        due.append((ACROSS * A + FIRST / 2, self.rs_ready))
        return sorted(due, key=lambda step: step[0])

    def f_credit(self, wait, at):
        for k, axis in enumerate("xy"):
            if wait:
                wait(self.credit.at[at + k], 1)
            else:
                pl.semaphore_signal(self.credit.at[at + k], inc=1, device_id=self.near[axis], device_id_type=MESH)

    def z_credit(self, wait):
        @pl.when(self.has_up)
        def _():
            if wait:
                wait(self.credit.at[3], 1)
            else:
                pl.semaphore_signal(self.credit.at[2], inc=1, device_id=self.up, device_id_type=MESH)

        @pl.when(self.has_down)
        def _():
            if wait:
                wait(self.credit.at[2], 1)
            else:
                pl.semaphore_signal(self.credit.at[3], inc=1, device_id=self.down, device_id_type=MESH)

    def rs_drain(self):
        A = self.A
        for part, (order, _, rows) in enumerate(self.rs_parts):
            big = order[0] != "z"

            def sent(kind, count):
                ref = self.wb.at[0 : 2 * count, :, pl.ds(0, rows), :]
                self.remote(ref, ref, self.rs_s.at[part * 4 + kind], self.rs_r.at[0], self.sib).wait_send()

            sent(0, A - 1)
            if big:
                sent(1, A - 1)
            sent(2, 1 if big else A)
            sent(3, 2 * A)


    def share(self, ref, k):
        rows = ref.at[pl.ds(pl.multiple_of(self.c * self.T, SUB), self.T), :]
        copy = self.remote(rows, rows, self.cg_s.at[k], self.cg_r.at[k], self.sib)
        copy.start()
        return copy

    def shared(self, ref, k):
        rows = ref.at[pl.ds(pl.multiple_of((1 - self.c) * self.T, SUB), self.T), :]
        mine = ref.at[pl.ds(pl.multiple_of(self.c * self.T, SUB), self.T), :]
        self.remote(rows, rows, self.cg_s.at[k], self.cg_r.at[k], self.sib).wait_recv()
        self.remote(mine, mine, self.cg_s.at[k], self.cg_r.at[k], self.sib).wait_send()

    def rows_of(self, which):
        return pl.ds(pl.multiple_of(which * self.T, SUB), self.T)

    def give(self, k, halves):
        buf = k % 2
        for h, value in enumerate(halves(1 - self.c)):
            self.sb[buf, :, h * TILE : (h + 1) * TILE] = value.astype(BF)
        self.remote(self.sb.at[buf], self.rb.at[buf], self.ex_s.at[k], self.ex_r.at[k], self.sib).start()
        for h, value in enumerate(halves(self.c)):
            self.pacc[:, h * TILE : (h + 1) * TILE] = value

    def taken(self, k):
        buf = k % 2
        self.remote(self.sb.at[buf], self.rb.at[buf], self.ex_s.at[k], self.ex_r.at[k], self.sib).wait()


    def act_at(self, j, m):
        if self.nt == 1:
            return (j, m)
        half = self.nt // 2
        return (pl.ds(j * self.nt + m * half, half),)

    def act_get(self, j, m):
        return self.act[self.act_at(j, m)].reshape(self.T, TILE)

    def act_set(self, j, m, value):
        at = self.act_at(j, m)
        self.act[at] = value.astype(BF).reshape(self.act.at[at].shape)

    def act_all(self, j):
        return self.act[pl.ds(j * self.nt, self.nt)].reshape(2 * self.T, TILE)


    def wcol(self, b):
        return self.wb[pl.ds(b * self.nzx, self.nzx)].reshape(self.D, TILE)

    def wrow(self, b, h):
        return self.wb[pl.ds(b * self.nzx, self.nzx), h].reshape(TILE, TILE)

    def win(self, j, h):
        return self.wb[pl.ds(2 * self.A + j * self.nt, self.nt), h].reshape(TILE, TILE)

    def wout(self, j, h):
        return self.wb[pl.ds(3 * self.A + j * self.nt, self.nt), h].reshape(TILE, TILE)

    def project(self, dst, first, source, block, count):
        @pl.loop(0, count)
        def _(i):
            weight = self.wcol(block + i)
            for m in range(2):
                rows = slice(m * self.T, (m + 1) * self.T)
                dst[first + i, rows, :] = dot(source[rows, :], weight).astype(BF)


    def masks(self):
        lane = lax.broadcasted_iota(jnp.int32, (1, PAIR), 1)
        row = lax.broadcasted_iota(jnp.int32, (PAIR, 1), 0)
        return [(lane < HD), (lane >= HD)], (row < HD)

    def visible(self, tile):
        T = self.T
        key = lax.broadcasted_iota(jnp.int32, (2 * T, T), 0)
        query = lax.broadcasted_iota(jnp.int32, (2 * T, T), 1) + tile * T
        edge = self.pfx_now[0:1, 0:1]
        return jnp.logical_or(key <= query, key.astype(F32) < edge)

    def attend(self, p, qkv, o, lse, masked, point):
        T = self.T
        cols = pl.ds(pl.multiple_of(p * PAIR, PAIR), PAIR)
        heads, upper = self.masks()
        keys = qkv[1, :, cols]
        values_t = turned(qkv[2, :, cols])
        for tile in range(2):
            rows = slice(tile * T, (tile + 1) * T)
            query = qkv[0, rows, cols].astype(F32) * score_scale
            vis = self.visible(tile) if masked else None
            mixed = []
            for h in range(2):
                scores = dot_nt(keys, jnp.where(heads[h], query, 0.0).astype(BF))
                if masked:
                    scores = jnp.where(vis, scores, masked_score)
                highest = jnp.max(scores, axis=0, keepdims=True)
                exponent = jnp.exp(scores - highest)
                total = jnp.sum(exponent, axis=0, keepdims=True)
                lse[p, h : h + 1, rows] = highest + jnp.log(total)
                mixed.append(dot(values_t, exponent.astype(BF)) * (1.0 / total))
                point(2 * tile + h)
            o[rows, cols] = jnp.where(upper, mixed[0], mixed[1]).T.astype(BF)

    def attend_back(self, p, qkv, do, lse, masked, point):
        T = self.T
        cols = pl.ds(pl.multiple_of(p * PAIR, PAIR), PAIR)
        heads, upper = self.masks()
        keys, values = qkv[1, :, cols], qkv[2, :, cols]
        keys_t = turned(keys)
        dk = [0.0, 0.0]
        dv = [0.0, 0.0]
        for tile in range(2):
            rows = slice(tile * T, (tile + 1) * T)
            query = qkv[0, rows, cols]
            grad = do[rows, cols]
            query_wide = query.astype(F32) * score_scale
            grad_wide = grad.astype(F32)
            vis = self.visible(tile) if masked else None
            dq = []
            for h in range(2):
                scores = dot_nt(keys, jnp.where(heads[h], query_wide, 0.0).astype(BF))
                if masked:
                    scores = jnp.where(vis, scores, masked_score)
                probs = jnp.exp(scores - lse[p, h : h + 1, rows])
                dprobs = dot_nt(values, jnp.where(heads[h], grad_wide, 0.0).astype(BF))
                delta = jnp.sum(dprobs * probs, axis=0, keepdims=True)
                dscores = (probs * (dprobs - delta)).astype(BF)
                dq.append(dot(keys_t, dscores))
                dk[h] += dot(dscores, query)
                dv[h] += dot(probs.astype(BF), grad)
                point(2 * tile + h)
            self.dqkv[0, rows, cols] = (jnp.where(upper, dq[0], dq[1]) * score_scale).T.astype(BF)
        self.dqkv[1, :, cols] = (jnp.where(heads[0], dk[0], dk[1]) * score_scale).astype(BF)
        self.dqkv[2, :, cols] = jnp.where(heads[0], dv[0], dv[1]).astype(BF)


    def norm(self, summed):
        centred = summed - jnp.mean(summed, axis=-1, keepdims=True)
        inv = lax.rsqrt(jnp.mean(centred * centred, axis=-1, keepdims=True) + norm_eps)
        return centred * inv, inv

    def norm_back(self, k, dy, normed, inv):
        gain = self.norms[k : k + 1, :]
        self.ng[k : k + 1, :] += jnp.sum(dy * normed, axis=0, keepdims=True)
        self.ng[3 + k : 4 + k, :] += jnp.sum(dy, axis=0, keepdims=True)
        scaled = dy * gain
        plain = jnp.mean(scaled, axis=-1, keepdims=True)
        along = jnp.mean(scaled * normed, axis=-1, keepdims=True)
        return inv * (scaled - plain - normed * along)

    def norm_rows(self, body):
        @pl.loop(0, self.T // LN_ROWS)
        def _(i):
            own = pl.ds(pl.multiple_of(i * LN_ROWS, LN_ROWS), LN_ROWS)
            full = pl.ds(pl.multiple_of(self.c * self.T + i * LN_ROWS, LN_ROWS), LN_ROWS)
            body(own, full)


class Steps:
    def __init__(self, steps, limit=1e9):
        self.steps, self.limit = list(steps), limit

    def run(self, count):
        now, self.steps = self.steps[:count], self.steps[count:]
        for step in now:
            step()

    def finish(self):
        self.run(len(self.steps))

    def until(self, time):
        while self.steps and self.steps[0][0] <= min(time, self.limit):
            self.steps.pop(0)[1]()

    def timed(self, index, turns, points, start, length):
        groups = []
        for place in range(turns * points):
            time, group = start + length * (place + 1) / (turns * points), []
            while self.steps and self.steps[0][0] <= min(time, self.limit):
                group.append(self.steps.pop(0)[1])
            groups.append(group)

        def at(point):
            for turn in range(turns):
                if groups[turn * points + point]:

                    @pl.when(index == turn)
                    def _():
                        for step in groups[turn * points + point]:
                            step()

        return at

    def spread(self, index, turns, points, count=1):
        total = turns * points * count
        now, self.steps = self.steps[:total], self.steps[total:]

        def at(point):
            for turn in range(turns):
                place = (turn * points + point) * count
                if now[place : place + count]:

                    @pl.when(index == turn)
                    def _():
                        for step in now[place : place + count]:
                            step()

        return at


def kernel(A, R, T, ag_parts, rs_parts, names, *arrays):
    s = Layer(A, R, T, ag_parts, rs_parts, dict(zip(names, arrays)))
    s.land = [getattr(s, f"land{i}") for i in range(len(rs_parts))]
    D = s.D
    s.n2r, s.ga = s.nga.at[0], s.nga.at[1]
    away = jnp.logical_not(s.kept)
    s.ng[...] = jnp.zeros_like(s.ng)
    s.pfx_own[...] = jnp.full(s.pfx_own.shape, s.pfx[0], jnp.int32).astype(F32)
    s.barrier()

    block = s.zx // s.nzx
    by_rows = jnp.logical_or(block == 3, block == 7)
    mine = pl.ds(pl.multiple_of(s.y * R, SUB), R)
    half = [pl.ds(pl.multiple_of(h * TILE, TILE), TILE) for h in (0, 1, s.c, 1 - s.c)]
    ffn_copies = [
        pltpu.make_async_copy(s.ffn_rows.at[:, half[h]], s.wb.at[2 * A + s.zx, h, mine, :], s.lc.at[h]) for h in (0, 1)
    ]
    rows_copies = [
        pltpu.make_async_copy(s.attn_rows.at[:, half[h]], s.wb.at[s.zx, h, mine, :], s.lc.at[2 + h]) for h in (0, 1)
    ]
    half_copy = pltpu.make_async_copy(s.attn_rows.at[:, half[2]], s.wb.at[s.zx, s.c, mine, :], s.lc.at[2])
    half_send = s.remote(
        s.attn_rows.at[:, half[3]], s.wb.at[s.zx, s.c, mine, :], s.misc_s.at[0], s.misc_r.at[0], s.sib
    )
    half_recv = s.remote(
        s.attn_rows.at[:, half[3]], s.wb.at[s.zx, 1 - s.c, mine, :], s.misc_s.at[0], s.misc_r.at[0], s.sib
    )
    for copy in ffn_copies:
        copy.start()

    @pl.when(by_rows)
    def _():
        for copy in rows_copies:
            copy.start()

    @pl.when(jnp.logical_not(by_rows))
    def _():
        half_copy.start()
        half_send.start()

    here = s.rows_of(s.c)
    there = s.rows_of(s.y)
    swaps = [
        (s.tokens, s.xf.at[here, :], s.xf.at[there, :]),
        (s.memory, s.mf.at[here, :], s.mf.at[there, :]),
        (s.pfx_own, s.pfx_now, s.pfx_now),
        (s.cot, s.cotb, s.cotb),
    ]

    def swap(i):
        src, dst, far = swaps[i]

        @pl.when(s.kept)
        def _():
            pltpu.make_async_copy(src, dst, s.lc.at[4 + i]).start()

        @pl.when(away)
        def _():
            s.remote(src, far, s.sw_s.at[i], s.sw_r.at[i], s.partner).start()


    @pl.when(by_rows)
    def _():
        for copy in rows_copies:
            copy.wait()

    @pl.when(jnp.logical_not(by_rows))
    def _():
        half_copy.wait()
        half_send.wait_send()
        half_recv.wait_recv()

    def both():
        for copy in ffn_copies:
            copy.wait()

    due = s.ag(0, EARLY, GATHERED) + s.ag(1, SECOND_BANK) + [(SECOND_BANK - EARLY - 0.1, both)]
    due += [(SWAPS, functools.partial(swap, i)) for i in range(3)] + [(LATE_SWAP, functools.partial(swap, 3))]
    gather = Steps(sorted(due, key=lambda step: step[0]))
    gather.until(EARLY)

    def swapped(i):
        src, dst, far = swaps[i]

        @pl.when(s.kept)
        def _():
            pltpu.make_async_copy(src, dst, s.lc.at[4 + i]).wait()

        @pl.when(away)
        def _():
            s.remote(src, far, s.sw_s.at[i], s.sw_r.at[i], s.partner).wait_send()
            s.remote(src, dst, s.sw_s.at[i], s.sw_r.at[i], s.partner).wait_recv()

    gather.until(GATHERED)
    for i in range(3):
        swapped(i)
    s.share(s.xf, 0)
    s.share(s.mf, 1)
    for part in range(len(ag_parts)):
        s.ag_last(0, part)
    s.shared(s.xf, 0)
    s.shared(s.mf, 1)

    def clock(time):
        return GATHERED + RATE * time

    s.project(s.qkv1, 0, s.xf, 0, 3)
    gather.until(clock(2.0))
    s.project(s.qkv2, 1, s.mf, 5, 2)
    gather.until(clock(3.5))

    @pl.loop(0, TILE // PAIR)
    def _(p):
        s.attend(p, s.qkv1, s.o1, s.lse1, True, gather.timed(p, TILE // PAIR, 4, clock(3.5), RATE * 8.0))

    def branch(o, b):
        return lambda which: [dot(o[s.rows_of(which), :], s.wrow(b, h)) for h in range(2)]

    s.give(0, branch(s.o1, 3))
    gather.until(clock(13.5))
    s.taken(0)

    def first_norm(own, full):
        summed = alpha_scale * s.xf[full, :].astype(F32) + s.pacc[own, :] + s.rb[0, own, :].astype(F32)
        normed, inv = s.norm(summed)
        s.dtok[own, :] = normed
        s.inv1[own, :] = inv
        result = normed * s.norms[0:1, :] + s.norms[3:4, :]
        s.nbuf[own, :] = result
        s.n1r[full, :] = result.astype(BF)

    s.norm_rows(first_norm)
    s.share(s.n1r, 2)
    gather.until(clock(16.0))
    s.shared(s.n1r, 2)

    s.project(s.qkv2, 0, s.n1r, 4, 1)

    @pl.loop(0, TILE // PAIR)
    def _(p):
        s.attend(p, s.qkv2, s.o2, s.lse2, False, gather.timed(p, TILE // PAIR, 4, clock(17.0), RATE * 8.0))

    s.give(1, branch(s.o2, 7))
    gather.until(clock(27.0))
    s.taken(1)

    def second_norm(own, full):
        summed = alpha_scale * s.nbuf[own, :] + s.pacc[own, :] + s.rb[1, own, :].astype(F32)
        normed, inv = s.norm(summed)
        s.dmem[own, :] = normed
        s.inv2[own, :] = inv
        result = normed * s.norms[1:2, :] + s.norms[4:5, :]
        s.nbuf[own, :] = result
        s.n2r[full, :] = result.astype(BF)

    s.norm_rows(second_norm)
    s.share(s.n2r, 3)
    gather.until(clock(29.5))
    s.shared(s.n2r, 3)
    gather.until(1e9)
    for part in range(len(ag_parts)):
        s.ag_last(1, part)
    swapped(3)

    tiles = 2 * A * R // TILE

    @pl.loop(0, tiles)
    def _(j):
        for m in range(2):
            rows = slice(m * T, (m + 1) * T)
            pre = dot_nt(s.n2r[rows, :TILE], s.win(j, 0)) + dot_nt(s.n2r[rows, TILE:], s.win(j, 1))
            gate = 1.0 / (1.0 + jnp.exp(-pre))
            s.act_set(tiles + j, m, pre * gate)
            s.act_set(j, m, gate * (1.0 + pre * (1.0 - gate)))

    def ffn_out(which):
        return [sum(dot(s.act_get(tiles + j, which), s.wout(j, h)) for j in range(tiles)) for h in range(2)]

    s.give(2, ffn_out)
    s.taken(2)

    def third_norm(own, full):
        summed = alpha_scale * s.nbuf[own, :] + s.pacc[own, :] + s.rb[0, own, :].astype(F32)
        normed, inv = s.norm(summed)
        result = normed * s.norms[2:3, :] + s.norms[5:6, :]
        s.out[own, :] = result
        s.osb[0, own, :] = result.astype(BF)
        grad = s.norm_back(2, s.cotb[own, :].astype(F32), normed, inv)
        s.nbuf[own, :] = grad
        s.ga[full, :] = grad.astype(BF)

    s.norm_rows(third_norm)
    s.share(s.ga, 4)

    def send_back(k):
        @pl.when(away)
        def _():
            s.remote(s.osb.at[k], s.orb.at[k], s.ob_s.at[k], s.ob_r.at[k], s.partner).start()

    send_back(0)
    s.ag_drain()
    s.shared(s.ga, 4)

    @pl.loop(0, tiles)
    def _(j):
        for m in range(2):
            rows = slice(m * T, (m + 1) * T)
            da = dot_nt(s.ga[rows, :TILE], s.wout(j, 0)) + dot_nt(s.ga[rows, TILE:], s.wout(j, 1))
            s.act_set(j, m, da * s.act_get(j, m).astype(F32))

    def ffn_in(which):
        return [sum(dot(s.act_get(j, which), s.win(j, h)) for j in range(tiles)) for h in range(2)]

    s.give(3, ffn_in)

    def hidden_terms(tile):
        hidden = s.act_all(tile)
        for h in range(2):
            terms = dot_tn(hidden, s.nga[tile // tiles, :, h * TILE : (h + 1) * TILE]).astype(BF)
            s.wb[pl.ds(2 * A + tile * s.nt, s.nt), h] = terms.reshape(s.nt, 2 * R, TILE)

    spread = Steps(s.rs(s.dffn, s.fin), ACROSS * A)
    if s.nt == 1:
        for x in range(2):
            hidden_terms(2 * s.turns[0] + x)
        spread.until(0.0)

        @pl.loop(2, 2 * A)
        def _(k):
            hidden_terms(2 * s.turn(k // 2) + lax.rem(k, 2))
    else:

        @pl.loop(0, 2 * tiles)
        def _(k):
            hidden_terms(k)

        spread.until(0.0)

    s.f_credit(None, 0)
    s.taken(3)

    def second_back(own, full):
        dy = alpha_scale * s.nbuf[own, :] + s.pacc[own, :] + s.rb[1, own, :].astype(F32)
        grad = s.norm_back(1, dy, s.dmem[own, :], s.inv2[own, :])
        s.nbuf[own, :] = grad
        s.gb[full, :] = grad.astype(BF)

    s.norm_rows(second_back)
    s.share(s.gb, 5)
    spread.until(3.0)
    s.shared(s.gb, 5)

    def mixed_back(grad, o, b):
        for m in range(2):
            rows = slice(m * T, (m + 1) * T)
            s.do[rows, :] = (
                dot_nt(grad[rows, :TILE], s.wrow(b, 0)) + dot_nt(grad[rows, TILE:], s.wrow(b, 1))
            ).astype(BF)
        for h in range(2):
            cols = slice(h * TILE, (h + 1) * TILE)
            terms = dot_tn(o[...], grad[:, cols]).astype(BF)
            s.wb[pl.ds(b * s.nzx, s.nzx), h] = terms.reshape(s.nzx, 2 * R, TILE)

    def weight_terms(b, source, grad):
        for h in range(2):
            cols = slice(h * TILE, (h + 1) * TILE)
            terms = dot_tn(source[:, cols], grad).astype(BF)
            half = s.nzx // 2 if s.nzx > 1 else 0
            if half:
                s.wb[pl.ds(b * s.nzx + h * half, half)] = terms.reshape(half, 2, 2 * R, TILE)
            else:
                s.wb[b, h] = terms

    def spread_back(which, blocks):
        rows = s.rows_of(which)
        halves = []
        for h in range(2):
            total = 0.0
            for b, k in blocks:
                total += dot_nt(s.dqkv[k, rows, :], s.wcol(b)[h * TILE : (h + 1) * TILE])
            halves.append(total)
        return halves

    mixed_back(s.gb, s.o2, 7)
    spread.until(5.0)

    @pl.loop(0, TILE // PAIR)
    def _(p):
        s.attend_back(p, s.qkv2, s.do, s.lse2, False, spread.timed(p, TILE // PAIR, 4, 5.0, 8.0))

    s.give(4, lambda which: spread_back(which, [(5, 1), (6, 2)]))
    spread.until(15.0)
    s.taken(4)

    def memory_rows(own, full):
        total = s.pacc[own, :] + s.rb[0, own, :].astype(F32)
        s.dmem[own, :] = total
        s.osb[1, own, :] = total.astype(BF)

    s.norm_rows(memory_rows)
    send_back(1)
    s.give(5, lambda which: spread_back(which, [(4, 0)]))
    spread.until(18.0)
    weight_terms(4, s.n1r, s.dqkv[0])
    weight_terms(5, s.mf, s.dqkv[1])
    weight_terms(6, s.mf, s.dqkv[2])
    spread.until(21.0)
    s.taken(5)

    def first_back(own, full):
        dy = alpha_scale * s.nbuf[own, :] + s.pacc[own, :] + s.rb[1, own, :].astype(F32)
        grad = s.norm_back(0, dy, s.dtok[own, :], s.inv1[own, :])
        s.nbuf[own, :] = grad
        s.ga[full, :] = grad.astype(BF)

    s.norm_rows(first_back)
    s.share(s.ga, 6)
    spread.until(24.0)
    s.shared(s.ga, 6)

    def norm_sum():
        for k, device in enumerate((s.sib, s.near["x"], s.near["y"])):
            copy = s.remote(s.ngs.at[k], s.ngr.at[k], s.nm_s.at[k], s.nm_r.at[k], device)
            s.ngs[k] = s.ng[...]
            copy.start()
            yield
            copy.wait()
            s.ng[...] = s.ng[...] + s.ngr[k]
        s.ngz[s.z] = s.ng[...]
        for other in range(A):

            @pl.when(s.z != other)
            def _():
                s.remote(
                    s.ng, s.ngz.at[s.z], s.nm_s.at[3 + other], s.nm_r.at[3 + s.z],
                    (s.dp + 4 * (other - s.z), s.y),
                ).start()

        yield
        for other in range(A):

            @pl.when(s.z != other)
            def _():
                s.remote(s.ng, s.ngz.at[other], s.nm_s.at[3 + other], s.nm_r.at[3 + other], s.sib).wait()

        total = s.ngz[0]
        for other in range(1, A):
            total = total + s.ngz[other]
        s.dnorm[...] = total[:6, :]
        yield

    sums = norm_sum()
    next(sums)

    mixed_back(s.ga, s.o1, 3)
    spread.until(27.0)
    next(sums)

    @pl.loop(0, TILE // PAIR)
    def _(p):
        s.attend_back(p, s.qkv1, s.do, s.lse1, True, spread.timed(p, TILE // PAIR, 4, 27.0, 9.0))

    next(sums)
    s.give(6, lambda which: spread_back(which, [(0, 0), (1, 1), (2, 2)]))
    next(sums)

    @pl.loop(0, 3)
    def _(k):
        weight_terms(k, s.xf, s.dqkv[k])

    next(sums, None)
    s.taken(6)

    def token_rows(own, full):
        total = alpha_scale * s.nbuf[own, :] + s.pacc[own, :] + s.rb[0, own, :].astype(F32)
        s.dtok[own, :] = total
        s.osb[2, own, :] = total.astype(BF)

    s.norm_rows(token_rows)
    send_back(2)
    spread.until(1e9)
    s.f_credit(pl.semaphore_wait, 0)
    spread.limit = 1e9

    spread.until(MIDDLE)

    @pl.when(away)
    def _():
        for k, dst in enumerate((s.out, s.dmem, s.dtok)):
            s.remote(s.osb.at[k], s.orb.at[k], s.ob_s.at[k], s.ob_r.at[k], s.partner).wait()

            @pl.loop(0, T // LN_ROWS)
            def _(i):
                own = pl.ds(pl.multiple_of(i * LN_ROWS, LN_ROWS), LN_ROWS)
                dst[own, :] = s.orb[k, own, :].astype(F32)

    spread.until(1e9)

    tail_send = s.remote(
        s.fin.at[:, half[3]], s.dattn.at[:, half[2]], s.misc_s.at[1], s.misc_r.at[1], s.sib
    )
    tail_recv = s.remote(
        s.fin.at[:, half[3]], s.dattn.at[:, half[3]], s.misc_s.at[1], s.misc_r.at[1], s.sib
    )

    @pl.when(by_rows)
    def _():
        s.dattn[...] = s.fin[...]

    @pl.when(jnp.logical_not(by_rows))
    def _():
        tail_send.start()
        s.dattn[:, half[2]] = s.fin[:, half[2]]
        tail_send.wait_send()
        tail_recv.wait_recv()

    s.rs_drain()


def hand_on(*refs):
    for src, dst in zip(refs[: len(refs) // 2], refs[len(refs) // 2 :]):
        dst[...] = src[...]


def hand_specs(outputs):
    return [
        pl.BlockSpec(shape, lambda i: (0, 0))
        if shape[0] % (8 * HANDS)
        else pl.BlockSpec((shape[0] // HANDS, shape[1]), lambda i: (i, 0))
        for shape in outputs.values()
    ]


def on_device(A, tokens, memory, attn_bank, ffn_bank, norm_params, prefix, cotangent):
    T, D = tokens.shape
    R = attn_bank.shape[0]
    ag_parts, rs_parts = cut(R, GATHER), cut(R, SCATTER)
    groups = D // (4 * R)
    tiles = 2 * A * R // TILE

    block = (lax.axis_index("dp") // 2) // groups
    by_rows = jnp.logical_or(block == 3, block == 7)
    attn_rows = attn_bank
    if groups > 1:
        by_core = attn_bank.reshape(R, groups, 2, 2 * R).transpose(0, 2, 1, 3).reshape(R, D)
        attn_rows = jnp.where(by_rows, attn_bank, by_core)
    slots = sum(landing(order, A) for order, _, _ in rs_parts)

    inputs = dict(
        tokens=tokens,
        memory=memory,
        cot=cotangent,
        pfx=prefix,
        attn_rows=attn_rows,
        ffn_rows=ffn_bank,
        norms=norm_params,
    )
    where = dict(pfx=pltpu.SMEM, norms=pltpu.VMEM)
    outputs = dict(
        out=(T, D), dtok=(T, D), dmem=(T, D), dattn=(R, D), dffn=(R, D), dnorm=(6, D)
    )
    wide = lambda *shape: pltpu.VMEM(shape, F32)
    low = lambda *shape: pltpu.VMEM(shape, BF)
    dma = lambda count: pltpu.SemaphoreType.DMA((count,))
    scratch = dict(
        wb=low(4 * A, 2, 2 * R, TILE),
        xf=low(2 * T, D),
        mf=low(2 * T, D),
        n1r=low(2 * T, D),
        nga=low(2, 2 * T, D),
        gb=low(2 * T, D),
        cotb=low(T, D),
        act=low(2 * A, 2, R, TILE),
        qkv1=low(3, 2 * T, TILE),
        qkv2=low(3, 2 * T, TILE),
        dqkv=low(3, 2 * T, TILE),
        o1=low(2 * T, TILE),
        o2=low(2 * T, TILE),
        do=low(2 * T, TILE),
        sb=low(2, T, D),
        rb=low(2, T, D),
        osb=low(3, T, D),
        orb=low(3, T, D),
        nbuf=wide(T, D),
        pacc=wide(T, D),
        fin=wide(R, D),
        pfx_own=wide(8, 128),
        pfx_now=wide(8, 128),
        lse1=wide(TILE // PAIR, 8, 2 * T),
        lse2=wide(TILE // PAIR, 8, 2 * T),
        inv1=wide(T, 1),
        inv2=wide(T, 1),
        ng=wide(8, D),
        ngs=wide(3, 8, D),
        ngr=wide(3, 8, D),
        ngz=wide(A, 8, D),
        lc=dma(8),
        misc_s=dma(2),
        misc_r=dma(2),
        sw_s=dma(4),
        sw_r=dma(4),
        ag_s=dma(len(ag_parts) * 4),
        ag_r=dma(2 * len(ag_parts) * (2 * A + 1)),
        rs_s=dma(len(rs_parts) * 4),
        rs_r=dma(slots + len(rs_parts) * 2 * A),
        cg_s=dma(7),
        cg_r=dma(7),
        ex_s=dma(7),
        ex_r=dma(7),
        ob_s=dma(3),
        ob_r=dma(3),
        nm_s=dma(3 + A),
        nm_r=dma(3 + A),
        credit=pltpu.SemaphoreType.REGULAR((6,)),
    )
    for i, (order, _, rows) in enumerate(rs_parts):
        scratch[f"land{i}"] = low(landing(order, A), 2, rows, TILE)
    names = list(inputs) + list(outputs) + list(scratch)
    results = pl.pallas_call(
        functools.partial(kernel, A, R, T, ag_parts, rs_parts, names),
        out_shape=[jax.ShapeDtypeStruct(shape, F32) for shape in outputs.values()],
        in_specs=[pl.BlockSpec(memory_space=where.get(n, pl.ANY)) for n in inputs],
        out_specs=[pl.BlockSpec(memory_space=pltpu.VMEM)] * len(outputs),
        scratch_shapes=list(scratch.values()),
        compiler_params=pltpu.CompilerParams(
            collective_id=0, has_side_effects=True, vmem_limit_bytes=64 * 2**20
        ),
        name="layer",
    )(*inputs.values())

    results = pl.pallas_call(
        hand_on,
        grid=(HANDS,),
        out_shape=[jax.ShapeDtypeStruct(shape, F32) for shape in outputs.values()],
        in_specs=hand_specs(outputs),
        out_specs=hand_specs(outputs),
        name="hand_on",
    )(*results)
    out, dtok, dmem, dattn, dffn, dnorm = results
    if groups > 1:
        by_core = dattn.reshape(R, 2, groups, 2 * R).transpose(0, 2, 1, 3).reshape(R, D)
        dattn = jnp.where(by_rows, dattn, by_core)
    return (out, dtok, dmem, dattn, dffn, dnorm)


def solution(mesh):
    rows = P(("dp", "seq"), None)
    return jax.shard_map(
        functools.partial(on_device, mesh.shape["dp"] // 4),
        mesh=mesh,
        in_specs=(rows, rows, rows, rows, P(), P("dp"), rows),
        out_specs=(rows, rows, rows, rows, rows, P()),
        check_vma=False,
    )
```

```python
import functools

import jax
import jax.numpy as jnp
from jax import lax
from jax.experimental import pallas as pl
from jax.experimental.pallas import tpu as pltpu
from jax.sharding import PartitionSpec as P

HD = 64
PAIR = 2 * HD
TILE = 512
SUB = 16
LN_ROWS = 32
HANDS = 2
AHEAD = 8
ACROSS = 11.63
ALONG = 12.12
HOP = 9.52
LAG_BIG = 0.06
LAG_SMALL = 0.71
START = 12.51
FIRST = 3.0
SECOND = 10.05
SUMS = (56.0, 74.0, 94.0)
EARLY = 5.87
COME = 10.6
PLANE = 13.85
STEP = 1.58
BESIDE = 9.75
CROSS = 10.02
SECOND_BANK = 51.38
SWAPS = 35.59
LATE_SWAP = 64.42
GATHERED = 66.95
RATE = 1.06
GATHER = (5, 6, 2, 3)
SCATTER = (4, 6, 3, 3)

alpha_scale = 300.0**0.25
norm_eps = 1e-05
masked_score = -1e30
score_scale = HD**-0.5

BF = jnp.bfloat16
F32 = jnp.float32
MESH = pl.DeviceIdType.MESH


def dot(left, right):
    return jnp.dot(left, right, preferred_element_type=F32)


def dot_nt(left, right):
    return lax.dot_general(left, right, (((1,), (1,)), ((), ())), preferred_element_type=F32)


def dot_tn(left, right):
    return lax.dot_general(left, right, (((0,), (0,)), ((), ())), preferred_element_type=F32)


def turned(block):
    return block.astype(F32).T.astype(BF)


def cut(rows, split):
    units = rows // SUB
    shares = [(units * share + 8) // 16 for share in split[1:]]
    sizes = list(zip(("xzy", "yzx", "zxy", "zyx"), [units - sum(shares)] + shares))
    parts, start = [], 0
    for order, size in sizes:
        if size > 0:
            parts.append((order, start * SUB, size * SUB))
        start += size
    return parts


def slots_of(order, A):
    return 4 * A + 3 if order[0] != "z" else 4 * A + 1


def landing(order, A):
    return slots_of(order, A) + (3 if order[0] != "z" else 1)


class Layer:
    def __init__(self, A, R, T, ag_parts, rs_parts, refs):
        self.A, self.R, self.T = A, R, T
        self.ag_parts, self.rs_parts = ag_parts, rs_parts
        self.D = 1024
        self.nzx = self.D // (4 * R)
        self.nt = TILE // (2 * R)
        for name, ref in refs.items():
            setattr(self, name, ref)
        self.dp, self.y = lax.axis_index("dp"), lax.axis_index("seq")
        self.c = lax.rem(self.dp, 2)
        self.x = lax.rem(self.dp // 2, 2)
        self.z = self.dp // 4
        self.zx = self.dp // 2
        self.sib = (self.dp + 1 - 2 * self.c, self.y)
        self.near = {"x": (self.dp + 2 - 4 * self.x, self.y), "y": (self.dp, 1 - self.y)}
        self.up = (self.dp + 4, self.y)
        self.down = (self.dp - 4, self.y)
        self.partner = (self.dp - self.c + self.y, self.c)
        self.has_up = self.z < A - 1
        self.has_down = self.z > 0
        self.kept = self.c == self.y
        self.turns = [self.turn(j) for j in range(A)]


    def remote(self, src, dst, send, recv, device):
        return pltpu.make_async_remote_copy(
            src_ref=src, dst_ref=dst, send_sem=send, recv_sem=recv, device_id=device, device_id_type=MESH
        )

    def own(self, axis):
        return self.x if axis == "x" else self.y

    def spot(self, bank, part, z, x, y):
        order, start, rows = part
        row = pl.multiple_of(y * self.R + start, SUB)
        return self.wb.at[bank * 2 * self.A + z * 2 + x, :, pl.ds(row, rows), :]

    def place(self, axis, f, l):
        return (f, l) if axis == "x" else (l, f)


    def barrier(self):
        bar = pltpu.get_barrier_semaphore()

        def greet(device):
            pl.semaphore_signal(bar, inc=1, device_id=device, device_id_type=MESH)

        greet(self.sib)
        greet(self.near["x"])
        greet(self.near["y"])
        for other in range(self.A):

            @pl.when(self.z != other)
            def _():
                greet((self.dp + 4 * (other - self.z), self.y))

        @pl.when(jnp.logical_not(self.kept))
        def _():
            greet(self.partner)
            pl.semaphore_wait(bar, 3 + self.A)

        @pl.when(self.kept)
        def _():
            pl.semaphore_wait(bar, 2 + self.A)


    def ag_index(self, bank, part, z, x, y, last):
        base = (bank * len(self.ag_parts) + part) * (2 * self.A + 1)
        if last:
            return base + 2 * self.A
        return base + z * 2 + (x if self.ag_parts[part][0][2] == "y" else y)

    def ag_send(self, bank, part, z, x, y, kind, device):
        ref = self.spot(bank, self.ag_parts[part], z, x, y)
        recv = self.ag_r.at[self.ag_index(bank, part, z, x, y, kind == 3)]
        self.remote(ref, ref, self.ag_s.at[part * 4 + kind], recv, device).start()

    def ag_wait(self, bank, part, z, x, y):
        ref = self.spot(bank, self.ag_parts[part], z, x, y)
        recv = self.ag_r.at[self.ag_index(bank, part, z, x, y, False)]
        self.remote(ref, ref, self.ag_s.at[0], recv, self.sib).wait_recv()

    def ag_last(self, bank, part):
        _, _, rows = self.ag_parts[part]
        ref = self.wb.at[0 : 2 * self.A, :, pl.ds(0, rows), :]
        recv = self.ag_r.at[self.ag_index(bank, part, 0, 0, 0, True)]
        self.remote(ref, ref, self.ag_s.at[0], recv, self.sib).wait_recv()

    def ag(self, bank, start, latest=1e9):
        A = self.A
        info = self.orders(self.ag_parts)

        def z_sends(part, f, fc, lc, w):
            px, py = self.place(f, fc, lc)

            @pl.when(self.has_up)
            def _():
                self.ag_send(bank, part, self.z, px, py, w, self.up)

            @pl.when(self.has_down)
            def _():
                self.ag_send(bank, part, self.z, px, py, w, self.down)

        def send(part, f, fc, lc, z, kind, axis):
            px, py = self.place(f, fc, lc)
            self.ag_send(bank, part, z, px, py, kind, self.near[axis])

        def early():
            for part, big, f, l, fo, lo in info:
                if big:
                    send(part, f, fo, lo, self.z, 2, f)

        def begin():
            for part, big, f, l, fo, lo in info:
                z_sends(part, f, fo, lo, 0)
            for part, big, f, l, fo, lo in info:
                if not big:
                    send(part, f, fo, lo, self.z, 2, f)
                send(part, f, fo, lo, self.z, 3, l)

        def beside(part, big, f, l, fo, lo):
            px, py = self.place(f, 1 - fo, lo)
            self.ag_wait(bank, part, self.z, px, py)
            z_sends(part, f, 1 - fo, lo, 1)
            send(part, f, 1 - fo, lo, self.z, 3, l)

        def arrive(d, w, part, big, f, l, fo, lo):
            fc = fo if w == 0 else 1 - fo
            px, py = self.place(f, fc, lo)

            def arrived(z, on, device):
                self.ag_wait(bank, part, z, px, py)

                @pl.when(on)
                def _():
                    self.ag_send(bank, part, z, px, py, w, device)

                if not big:
                    send(part, f, fc, lo, z, 2, f)
                send(part, f, fc, lo, z, 3, l)

            @pl.when(self.z >= d)
            def _():
                arrived(self.z - d, self.has_up, self.up)

            @pl.when(self.z + d < A)
            def _():
                arrived(self.z + d, self.has_down, self.down)

        def cross(d, part, big, f, l, fo, lo):
            px, py = self.place(f, 1 - fo, lo)

            def crossed(z):
                self.ag_wait(bank, part, z, px, py)
                send(part, f, 1 - fo, lo, z, 3, l)

            self.planes_at(d, crossed)

        bigs = [row for row in info if row[1]]
        smalls = [row for row in info if not row[1]]
        due = [(start - EARLY, early), (start, begin)]
        for d in range(1, A):
            for k, row in enumerate(info):
                come = start + COME + PLANE * (d - 1) + STEP * k
                due.append((come, functools.partial(arrive, d, 0, *row)))
                if row[1]:
                    side = start + BESIDE + STEP * k
                    if d == 1:
                        due.append((side, functools.partial(beside, *row)))
                    due.append((max(come + STEP * len(info), side + 0.1), functools.partial(arrive, d, 1, *row)))
                else:
                    if d == 1:
                        due.append((start + CROSS + STEP * k, functools.partial(cross, 0, *row)))
                    over = start + CROSS + PLANE * d + STEP * k
                    due.append((max(over, come + 0.1), functools.partial(cross, d, *row)))
        return [(min(time, latest), step) for time, step in due]

    def planes_at(self, d, act):
        if d == 0:
            act(self.z)
            return

        @pl.when(self.z >= d)
        def _():
            act(self.z - d)

        @pl.when(self.z + d < self.A)
        def _():
            act(self.z + d)

    def orders(self, parts):
        info = []
        for part, (order, _, _) in enumerate(parts):
            l = order[2]
            f = "x" if l == "y" else "y"
            info.append((part, order[0] != "z", f, l, self.own(f), self.own(l)))
        return info

    def ag_drain(self):
        A = self.A
        inner = jnp.logical_and(self.has_up, self.has_down)
        for part, (order, _, rows) in enumerate(self.ag_parts):
            big = order[0] != "z"

            def sent(kind, count):
                ref = self.wb.at[0 : 2 * count, :, pl.ds(0, rows), :]
                self.remote(ref, ref, self.ag_s.at[part * 4 + kind], self.ag_r.at[0], self.sib).wait_send()

            for kind in (0, 1) if big else (0,):

                @pl.when(inner)
                def _():
                    sent(kind, A + 1)

                @pl.when(jnp.logical_not(inner))
                def _():
                    sent(kind, 1)

            sent(2, 1 if big else A)
            sent(3, 2 * A)


    def turn(self, j):
        A = self.A
        mirrored = self.z >= A // 2
        w = jnp.where(mirrored, A - 1 - self.z, self.z)
        d = jnp.where(j < A - 1 - w, A - 1 - j, jnp.where(j < A - 1, j - (A - 1 - w), w))
        return jnp.where(mirrored, A - 1 - d, d)

    def rs_land(self, bank, part, slot, first):
        if bank == 0 and first:
            _, start, rows = self.rs_parts[part]
            return self.act.at[slot, :, start : start + rows, :]
        return self.land[part].at[slot]

    def rs_index(self, bank, part, slot, first):
        room = [landing(order, self.A) for order, _, _ in self.rs_parts]
        if bank == 0 and first:
            return sum(room) + part * 2 * self.A + slot
        return sum(room[:part]) + slot

    def rs_send(self, bank, part, z, x, y, slot, kind, device):
        sem = part * 4 + kind
        self.remote(
            self.spot(bank, self.rs_parts[part], z, x, y),
            self.rs_land(bank, part, slot, kind == 3),
            self.rs_s.at[sem],
            self.rs_r.at[self.rs_index(bank, part, slot, kind == 3)],
            device,
        ).start()

    def rs_add(self, bank, part, z, x, y, slot, out=None, first=False):
        landed = self.rs_land(bank, part, slot, first)
        self.remote(
            landed, landed, self.rs_s.at[0], self.rs_r.at[self.rs_index(bank, part, slot, first)], self.sib
        ).wait_recv()
        order, start, rows = self.rs_parts[part]
        at = bank * 2 * self.A + z * 2 + x
        row = pl.multiple_of(y * self.R + start, SUB)

        @pl.loop(0, 2)
        def _(h):
            total = self.wb[at, h, pl.ds(row, rows), :].astype(F32) + landed[h].astype(F32)
            if out is None:
                self.wb[at, h, pl.ds(row, rows), :] = total.astype(BF)
            else:
                out[start : start + rows, pl.ds(pl.multiple_of(h * TILE, TILE), TILE)] = total.astype(out.dtype)

    def rs_firsts(self, bank):
        sends = []

        def send(z, w, part, big, f, l, fo, lo):
            fc = fo if w == 0 else 1 - fo
            px, py = self.place(f, fc, 1 - lo)
            self.rs_send(bank, part, z, px, py, z * 2 + fc, 3, self.near[l])

        for z in self.turns:
            for row in self.orders(self.rs_parts):
                for w in (1, 0):
                    sends.append(functools.partial(send, z, w, *row))
        return sends

    def rs_slot(self, bank, part, slot):
        if bank == 1:
            return slot
        A = self.A
        more = slots_of(self.rs_parts[part][0], A)
        slot = slot - 2 * A
        return jnp.where(slot < 2 * A, slot, slot - 2 * A + more)

    def chain(self, bank, part, big, f, fc, lo, w, z, final):
        A = self.A
        base = 2 * A + w * (A + 1) if big else 3 * A
        px, py = self.place(f, fc, lo)

        def slot(k):
            return self.rs_slot(bank, part, base + k)

        def onward(device, next_z, up):
            self.rs_send(bank, part, z, px, py, slot(z if up else jnp.where(z == next_z, A, z)), w, device)

        @pl.when(z > self.z)
        def _():
            @pl.when(self.has_down)
            def _():
                self.rs_add(bank, part, z, px, py, slot(z))

            onward(self.up, self.z + 1, True)

        @pl.when(z < self.z)
        def _():
            @pl.when(self.has_up)
            def _():
                self.rs_add(bank, part, z, px, py, slot(z))

            onward(self.down, self.z - 1, False)

        @pl.when(z == self.z)
        def _():
            inner = jnp.logical_and(self.has_down, self.has_up)

            @pl.when(inner)
            def _():
                self.rs_add(bank, part, z, px, py, slot(z))
                self.rs_add(bank, part, z, px, py, slot(A), final)

            @pl.when(jnp.logical_not(inner))
            def _():
                self.rs_add(bank, part, z, px, py, slot(jnp.where(self.has_down, z, A)), final)

    def rs_across(self, bank, j, sends, start):
        A, z = self.A, self.turns[j]

        def across(w, more, part, big, f, l, fo, lo):
            fc = fo if w == 0 else 1 - fo
            px, py = self.place(f, fc, lo)
            self.rs_add(bank, part, z, px, py, z * 2 + fc, first=True)
            if more:
                more()
            if w == 1 and not big:
                self.rs_send(bank, part, z, px, py, self.rs_slot(bank, part, 2 * A + z), 2, self.near[f])

        rows = [(w, row) for row in self.orders(self.rs_parts) for w in (1, 0)]
        return [
            (
                start + ACROSS * (j + (k + 1) / len(rows)),
                functools.partial(across, w, sends.pop(0) if sends else None, *row),
            )
            for k, (w, row) in enumerate(rows)
        ]

    def rs_along(self, bank, j, out, first, start):
        A, z = self.A, self.turns[j]
        at_end = jnp.logical_not(jnp.logical_and(self.has_up, self.has_down))

        def along(w, part, big, f, l, fo, lo):
            if big:
                self.chain(bank, part, big, f, fo if w == 0 else 1 - fo, lo, w, z, None)
            else:
                px, py = self.place(f, fo, lo)
                self.rs_add(bank, part, z, px, py, self.rs_slot(bank, part, 2 * A + z))
                self.chain(bank, part, big, f, fo, lo, 0, z, out if j == A - 1 else None)
                if bank == 0 and j == A - 1:
                    self.tail(part)

        def only(role, step):
            @pl.when(role)
            def _():
                step()

        orders = self.orders(self.rs_parts)
        rows = [(w, row) for row in orders if row[1] for w in (1, 0)] + [(0, row) for row in orders if not row[1]]
        plane = min(j, A - 2 + (0.0 if j == A - 1 else -0.5))
        steps = []
        for k, (w, row) in enumerate(rows):
            step = functools.partial(along, w, *row)
            inner = start + ALONG * (plane + (k + 1) / len(rows)) + HOP
            lag = LAG_BIG if row[1] else LAG_SMALL
            end = first + ACROSS * (j + lag + (k + 1) / len(rows))
            if j == A - 1:
                steps.append((max(inner, end), step))
            else:
                steps.append((max(inner, end), functools.partial(only, jnp.logical_not(at_end), step)))
                steps.append((end, functools.partial(only, at_end, step)))
        return steps

    def rs_last(self, bank, out):
        A = self.A

        def go():
            for part, big, f, l, fo, lo in self.orders(self.rs_parts):
                if big:
                    px, py = self.place(f, 1 - fo, lo)
                    self.rs_send(bank, part, self.z, px, py, self.rs_slot(bank, part, 4 * A + 2), 2, self.near[f])

        def come(part, big, f, l, fo, lo):
            px, py = self.place(f, fo, lo)
            self.rs_add(bank, part, self.z, px, py, self.rs_slot(bank, part, 4 * A + 2), out)
            if bank == 0:
                self.tail(part)

        return [go] + [functools.partial(come, *row) for row in self.orders(self.rs_parts) if row[1]]

    def rs_ready(self):
        for go in (None, pl.semaphore_wait):
            self.z_credit(go)
            self.f_credit(go, 4)

    def rs(self, out1, out0):
        A = self.A
        due = []
        for bank, out, first, start in ((1, out1, 0.0, START), (0, out0, ACROSS * A + FIRST, ALONG * (A - 1) + SECOND)):
            sends = self.rs_firsts(bank)
            due += [(first if bank else first - FIRST / 4, step) for step in sends[:AHEAD]]
            sends = sends[AHEAD:]
            for j in range(A):
                due += self.rs_across(bank, j, sends, first)
                due += self.rs_along(bank, j, out, first, start)
            done = start + ALONG * (A - 1) + HOP
            go, *come = self.rs_last(bank, out)
            due += [(done, go)] + [(done + 2 * HOP, step) for step in come]
        due.append((ACROSS * A + FIRST / 2, self.rs_ready))
        return sorted(due, key=lambda step: step[0])

    def f_credit(self, wait, at):
        for k, axis in enumerate("xy"):
            if wait:
                wait(self.credit.at[at + k], 1)
            else:
                pl.semaphore_signal(self.credit.at[at + k], inc=1, device_id=self.near[axis], device_id_type=MESH)

    def z_credit(self, wait):
        @pl.when(self.has_up)
        def _():
            if wait:
                wait(self.credit.at[3], 1)
            else:
                pl.semaphore_signal(self.credit.at[2], inc=1, device_id=self.up, device_id_type=MESH)

        @pl.when(self.has_down)
        def _():
            if wait:
                wait(self.credit.at[2], 1)
            else:
                pl.semaphore_signal(self.credit.at[3], inc=1, device_id=self.down, device_id_type=MESH)

    def rs_drain(self):
        A = self.A
        for part, (order, _, rows) in enumerate(self.rs_parts):
            big = order[0] != "z"

            def sent(kind, count):
                ref = self.wb.at[0 : 2 * count, :, pl.ds(0, rows), :]
                self.remote(ref, ref, self.rs_s.at[part * 4 + kind], self.rs_r.at[0], self.sib).wait_send()

            sent(0, A - 1)
            if big:
                sent(1, A - 1)
            sent(2, 1 if big else A)
            sent(3, 2 * A)


    def share(self, ref, k):
        rows = ref.at[pl.ds(pl.multiple_of(self.c * self.T, SUB), self.T), :]
        copy = self.remote(rows, rows, self.cg_s.at[k], self.cg_r.at[k], self.sib)
        copy.start()
        return copy

    def shared(self, ref, k):
        rows = ref.at[pl.ds(pl.multiple_of((1 - self.c) * self.T, SUB), self.T), :]
        mine = ref.at[pl.ds(pl.multiple_of(self.c * self.T, SUB), self.T), :]
        self.remote(rows, rows, self.cg_s.at[k], self.cg_r.at[k], self.sib).wait_recv()
        self.remote(mine, mine, self.cg_s.at[k], self.cg_r.at[k], self.sib).wait_send()

    def rows_of(self, which):
        return pl.ds(pl.multiple_of(which * self.T, SUB), self.T)

    def give(self, k, halves):
        buf = k % 2
        for h, value in enumerate(halves(1 - self.c)):
            self.sb[buf, :, h * TILE : (h + 1) * TILE] = value.astype(BF)
        self.remote(self.sb.at[buf], self.rb.at[buf], self.ex_s.at[k], self.ex_r.at[k], self.sib).start()
        for h, value in enumerate(halves(self.c)):
            self.pacc[:, h * TILE : (h + 1) * TILE] = value

    def taken(self, k):
        buf = k % 2
        self.remote(self.sb.at[buf], self.rb.at[buf], self.ex_s.at[k], self.ex_r.at[k], self.sib).wait()


    def act_at(self, j, m):
        if self.nt == 1:
            return (j, m)
        half = self.nt // 2
        return (pl.ds(j * self.nt + m * half, half),)

    def act_get(self, j, m):
        return self.act[self.act_at(j, m)].reshape(self.T, TILE)

    def act_set(self, j, m, value):
        at = self.act_at(j, m)
        self.act[at] = value.astype(BF).reshape(self.act.at[at].shape)

    def act_all(self, j):
        return self.act[pl.ds(j * self.nt, self.nt)].reshape(2 * self.T, TILE)


    def wcol(self, b):
        return self.wb[pl.ds(b * self.nzx, self.nzx)].reshape(self.D, TILE)

    def wrow(self, b, h):
        return self.wb[pl.ds(b * self.nzx, self.nzx), h].reshape(TILE, TILE)

    def win(self, j, h):
        return self.wb[pl.ds(2 * self.A + j * self.nt, self.nt), h].reshape(TILE, TILE)

    def wout(self, j, h):
        return self.wb[pl.ds(3 * self.A + j * self.nt, self.nt), h].reshape(TILE, TILE)

    def project(self, dst, first, source, block, count):
        @pl.loop(0, count)
        def _(i):
            weight = self.wcol(block + i)
            for m in range(2):
                rows = slice(m * self.T, (m + 1) * self.T)
                dst[first + i, rows, :] = dot(source[rows, :], weight).astype(BF)


    def masks(self):
        lane = lax.broadcasted_iota(jnp.int32, (1, PAIR), 1)
        row = lax.broadcasted_iota(jnp.int32, (PAIR, 1), 0)
        return [(lane < HD), (lane >= HD)], (row < HD)

    def visible(self, tile):
        T = self.T
        key = lax.broadcasted_iota(jnp.int32, (2 * T, T), 0)
        query = lax.broadcasted_iota(jnp.int32, (2 * T, T), 1) + tile * T
        edge = self.pfx_now[0:1, 0:1]
        return jnp.logical_or(key <= query, key.astype(F32) < edge)

    def attend(self, p, qkv, o, lse, masked, point):
        T = self.T
        cols = pl.ds(pl.multiple_of(p * PAIR, PAIR), PAIR)
        heads, upper = self.masks()
        keys = qkv[1, :, cols]
        values_t = turned(qkv[2, :, cols])
        for tile in range(2):
            rows = slice(tile * T, (tile + 1) * T)
            query = qkv[0, rows, cols].astype(F32) * score_scale
            vis = self.visible(tile) if masked else None
            mixed = []
            for h in range(2):
                scores = dot_nt(keys, jnp.where(heads[h], query, 0.0).astype(BF))
                if masked:
                    scores = jnp.where(vis, scores, masked_score)
                highest = jnp.max(scores, axis=0, keepdims=True)
                exponent = jnp.exp(scores - highest)
                total = jnp.sum(exponent, axis=0, keepdims=True)
                lse[p, h : h + 1, rows] = highest + jnp.log(total)
                mixed.append(dot(values_t, exponent.astype(BF)) * (1.0 / total))
                point(2 * tile + h)
            o[rows, cols] = jnp.where(upper, mixed[0], mixed[1]).T.astype(BF)

    def attend_back(self, p, qkv, do, lse, masked, point):
        T = self.T
        cols = pl.ds(pl.multiple_of(p * PAIR, PAIR), PAIR)
        heads, upper = self.masks()
        keys, values = qkv[1, :, cols], qkv[2, :, cols]
        keys_t = turned(keys)
        dk = [0.0, 0.0]
        dv = [0.0, 0.0]
        for tile in range(2):
            rows = slice(tile * T, (tile + 1) * T)
            query = qkv[0, rows, cols]
            grad = do[rows, cols]
            query_wide = query.astype(F32) * score_scale
            grad_wide = grad.astype(F32)
            vis = self.visible(tile) if masked else None
            dq = []
            for h in range(2):
                scores = dot_nt(keys, jnp.where(heads[h], query_wide, 0.0).astype(BF))
                if masked:
                    scores = jnp.where(vis, scores, masked_score)
                probs = jnp.exp(scores - lse[p, h : h + 1, rows])
                dprobs = dot_nt(values, jnp.where(heads[h], grad_wide, 0.0).astype(BF))
                delta = jnp.sum(dprobs * probs, axis=0, keepdims=True)
                dscores = (probs * (dprobs - delta)).astype(BF)
                dq.append(dot(keys_t, dscores))
                dk[h] += dot(dscores, query)
                dv[h] += dot(probs.astype(BF), grad)
                point(2 * tile + h)
            self.dqkv[0, rows, cols] = (jnp.where(upper, dq[0], dq[1]) * score_scale).T.astype(BF)
        self.dqkv[1, :, cols] = (jnp.where(heads[0], dk[0], dk[1]) * score_scale).astype(BF)
        self.dqkv[2, :, cols] = jnp.where(heads[0], dv[0], dv[1]).astype(BF)


    def norm(self, summed):
        centred = summed - jnp.mean(summed, axis=-1, keepdims=True)
        inv = lax.rsqrt(jnp.mean(centred * centred, axis=-1, keepdims=True) + norm_eps)
        return centred * inv, inv

    def norm_back(self, k, dy, normed, inv):
        gain = self.norms[k : k + 1, :]
        self.ng[k : k + 1, :] += jnp.sum(dy * normed, axis=0, keepdims=True)
        self.ng[3 + k : 4 + k, :] += jnp.sum(dy, axis=0, keepdims=True)
        scaled = dy * gain
        plain = jnp.mean(scaled, axis=-1, keepdims=True)
        along = jnp.mean(scaled * normed, axis=-1, keepdims=True)
        return inv * (scaled - plain - normed * along)

    def norm_rows(self, body):
        @pl.loop(0, self.T // LN_ROWS)
        def _(i):
            own = pl.ds(pl.multiple_of(i * LN_ROWS, LN_ROWS), LN_ROWS)
            full = pl.ds(pl.multiple_of(self.c * self.T + i * LN_ROWS, LN_ROWS), LN_ROWS)
            body(own, full)


class Steps:
    def __init__(self, steps, limit=1e9):
        self.steps, self.limit = list(steps), limit

    def run(self, count):
        now, self.steps = self.steps[:count], self.steps[count:]
        for step in now:
            step()

    def finish(self):
        self.run(len(self.steps))

    def until(self, time):
        while self.steps and self.steps[0][0] <= min(time, self.limit):
            self.steps.pop(0)[1]()

    def timed(self, index, turns, points, start, length):
        groups = []
        for place in range(turns * points):
            time, group = start + length * (place + 1) / (turns * points), []
            while self.steps and self.steps[0][0] <= min(time, self.limit):
                group.append(self.steps.pop(0)[1])
            groups.append(group)

        def at(point):
            for turn in range(turns):
                if groups[turn * points + point]:

                    @pl.when(index == turn)
                    def _():
                        for step in groups[turn * points + point]:
                            step()

        return at

    def spread(self, index, turns, points, count=1):
        total = turns * points * count
        now, self.steps = self.steps[:total], self.steps[total:]

        def at(point):
            for turn in range(turns):
                place = (turn * points + point) * count
                if now[place : place + count]:

                    @pl.when(index == turn)
                    def _():
                        for step in now[place : place + count]:
                            step()

        return at


def kernel(A, R, T, ag_parts, rs_parts, names, *arrays):
    s = Layer(A, R, T, ag_parts, rs_parts, dict(zip(names, arrays)))
    s.land = [getattr(s, f"land{i}") for i in range(len(rs_parts))]
    D = s.D
    s.n2r, s.ga = s.nga.at[0], s.nga.at[1]
    away = jnp.logical_not(s.kept)
    s.ng[...] = jnp.zeros_like(s.ng)
    s.pfx_own[...] = jnp.full(s.pfx_own.shape, s.pfx[0], jnp.int32).astype(F32)
    s.barrier()

    block = s.zx // s.nzx
    by_rows = jnp.logical_or(block == 3, block == 7)
    mine = pl.ds(pl.multiple_of(s.y * R, SUB), R)
    half = [pl.ds(pl.multiple_of(h * TILE, TILE), TILE) for h in (0, 1, s.c, 1 - s.c)]
    ffn_copies = [
        pltpu.make_async_copy(s.ffn_rows.at[:, half[h]], s.wb.at[2 * A + s.zx, h, mine, :], s.lc.at[h]) for h in (0, 1)
    ]
    rows_copies = [
        pltpu.make_async_copy(s.attn_rows.at[:, half[h]], s.wb.at[s.zx, h, mine, :], s.lc.at[2 + h]) for h in (0, 1)
    ]
    half_copy = pltpu.make_async_copy(s.attn_rows.at[:, half[2]], s.wb.at[s.zx, s.c, mine, :], s.lc.at[2])
    half_send = s.remote(
        s.attn_rows.at[:, half[3]], s.wb.at[s.zx, s.c, mine, :], s.misc_s.at[0], s.misc_r.at[0], s.sib
    )
    half_recv = s.remote(
        s.attn_rows.at[:, half[3]], s.wb.at[s.zx, 1 - s.c, mine, :], s.misc_s.at[0], s.misc_r.at[0], s.sib
    )
    for copy in ffn_copies:
        copy.start()

    @pl.when(by_rows)
    def _():
        for copy in rows_copies:
            copy.start()

    @pl.when(jnp.logical_not(by_rows))
    def _():
        half_copy.start()
        half_send.start()

    here = s.rows_of(s.c)
    there = s.rows_of(s.y)
    swaps = [
        (s.tokens, s.xf.at[here, :], s.xf.at[there, :]),
        (s.memory, s.mf.at[here, :], s.mf.at[there, :]),
        (s.pfx_own, s.pfx_now, s.pfx_now),
        (s.cot, s.cotb, s.cotb),
    ]

    def swap(i):
        src, dst, far = swaps[i]

        @pl.when(s.kept)
        def _():
            pltpu.make_async_copy(src, dst, s.lc.at[4 + i]).start()

        @pl.when(away)
        def _():
            s.remote(src, far, s.sw_s.at[i], s.sw_r.at[i], s.partner).start()


    @pl.when(by_rows)
    def _():
        for copy in rows_copies:
            copy.wait()

    @pl.when(jnp.logical_not(by_rows))
    def _():
        half_copy.wait()
        half_send.wait_send()
        half_recv.wait_recv()

    def both():
        for copy in ffn_copies:
            copy.wait()

    due = s.ag(0, EARLY, GATHERED) + s.ag(1, SECOND_BANK) + [(SECOND_BANK - EARLY - 0.1, both)]
    due += [(SWAPS, functools.partial(swap, i)) for i in range(3)] + [(LATE_SWAP, functools.partial(swap, 3))]
    gather = Steps(sorted(due, key=lambda step: step[0]))
    gather.until(EARLY)

    def swapped(i):
        src, dst, far = swaps[i]

        @pl.when(s.kept)
        def _():
            pltpu.make_async_copy(src, dst, s.lc.at[4 + i]).wait()

        @pl.when(away)
        def _():
            s.remote(src, far, s.sw_s.at[i], s.sw_r.at[i], s.partner).wait_send()
            s.remote(src, dst, s.sw_s.at[i], s.sw_r.at[i], s.partner).wait_recv()

    gather.until(GATHERED)
    for i in range(3):
        swapped(i)
    s.share(s.xf, 0)
    s.share(s.mf, 1)
    for part in range(len(ag_parts)):
        s.ag_last(0, part)
    s.shared(s.xf, 0)
    s.shared(s.mf, 1)

    def clock(time):
        return GATHERED + RATE * time

    s.project(s.qkv1, 0, s.xf, 0, 3)
    gather.until(clock(2.0))
    s.project(s.qkv2, 1, s.mf, 5, 2)
    gather.until(clock(3.5))

    @pl.loop(0, TILE // PAIR)
    def _(p):
        s.attend(p, s.qkv1, s.o1, s.lse1, True, gather.timed(p, TILE // PAIR, 4, clock(3.5), RATE * 8.0))

    def branch(o, b):
        return lambda which: [dot(o[s.rows_of(which), :], s.wrow(b, h)) for h in range(2)]

    s.give(0, branch(s.o1, 3))
    gather.until(clock(13.5))
    s.taken(0)

    def first_norm(own, full):
        summed = alpha_scale * s.xf[full, :].astype(F32) + s.pacc[own, :] + s.rb[0, own, :].astype(F32)
        normed, inv = s.norm(summed)
        s.zh1[own, :] = normed
        s.inv1[own, :] = inv
        result = normed * s.norms[0:1, :] + s.norms[3:4, :]
        s.nbuf[own, :] = result
        s.n1r[full, :] = result.astype(BF)

    s.norm_rows(first_norm)
    s.share(s.n1r, 2)
    gather.until(clock(16.0))
    s.shared(s.n1r, 2)

    s.project(s.qkv2, 0, s.n1r, 4, 1)

    @pl.loop(0, TILE // PAIR)
    def _(p):
        s.attend(p, s.qkv2, s.o2, s.lse2, False, gather.timed(p, TILE // PAIR, 4, clock(17.0), RATE * 8.0))

    s.give(1, branch(s.o2, 7))
    gather.until(clock(27.0))
    s.taken(1)

    def second_norm(own, full):
        summed = alpha_scale * s.nbuf[own, :] + s.pacc[own, :] + s.rb[1, own, :].astype(F32)
        normed, inv = s.norm(summed)
        s.zh2[own, :] = normed
        s.inv2[own, :] = inv
        result = normed * s.norms[1:2, :] + s.norms[4:5, :]
        s.nbuf[own, :] = result
        s.n2r[full, :] = result.astype(BF)

    s.norm_rows(second_norm)
    s.share(s.n2r, 3)
    gather.until(clock(29.5))
    s.shared(s.n2r, 3)
    gather.until(1e9)
    for part in range(len(ag_parts)):
        s.ag_last(1, part)
    swapped(3)

    tiles = 2 * A * R // TILE

    @pl.loop(0, tiles)
    def _(j):
        for m in range(2):
            rows = slice(m * T, (m + 1) * T)
            pre = dot_nt(s.n2r[rows, :TILE], s.win(j, 0)) + dot_nt(s.n2r[rows, TILE:], s.win(j, 1))
            gate = 1.0 / (1.0 + jnp.exp(-pre))
            s.act_set(tiles + j, m, pre * gate)
            s.act_set(j, m, gate * (1.0 + pre * (1.0 - gate)))

    def ffn_out(which):
        return [sum(dot(s.act_get(tiles + j, which), s.wout(j, h)) for j in range(tiles)) for h in range(2)]

    s.give(2, ffn_out)
    s.taken(2)

    def third_norm(own, full):
        summed = alpha_scale * s.nbuf[own, :] + s.pacc[own, :] + s.rb[0, own, :].astype(F32)
        normed, inv = s.norm(summed)
        result = normed * s.norms[2:3, :] + s.norms[5:6, :]
        s.osb[0, own, :] = result.astype(BF)
        grad = s.norm_back(2, s.cotb[own, :].astype(F32), normed, inv)
        s.nbuf[own, :] = grad
        s.ga[full, :] = grad.astype(BF)

    s.norm_rows(third_norm)
    s.share(s.ga, 4)

    def send_back(k):
        dst = (s.out, s.dmem, s.dtok)[k]
        there = s.remote(s.osb.at[k], dst, s.ob_s.at[k], s.ob_r.at[k], s.partner)
        here = pltpu.make_async_copy(s.osb.at[k], dst, s.ob_s.at[k])

        @pl.when(away)
        def _():
            there.start()

        @pl.when(s.kept)
        def _():
            here.start()

        return here, there

    sent_back = [send_back(0)]
    s.ag_drain()

    def hidden_back(which):
        rows = s.rows_of(which)

        @pl.loop(0, tiles)
        def _(j):
            da = dot_nt(s.ga[rows, :TILE], s.wout(j, 0)) + dot_nt(s.ga[rows, TILE:], s.wout(j, 1))
            s.act_set(j, which, da * s.act_get(j, which).astype(F32))

    hidden_back(s.c)
    s.shared(s.ga, 4)
    hidden_back(1 - s.c)

    def ffn_in(which):
        return [sum(dot(s.act_get(j, which), s.win(j, h)) for j in range(tiles)) for h in range(2)]

    s.give(3, ffn_in)

    def hidden_terms(tile):
        hidden = s.act_all(tile)
        for h in range(2):
            terms = dot_tn(hidden, s.nga[tile // tiles, :, h * TILE : (h + 1) * TILE]).astype(BF)
            s.wb[pl.ds(2 * A + tile * s.nt, s.nt), h] = terms.reshape(s.nt, 2 * R, TILE)

    def tail_copies(part):
        _, start, rows = rs_parts[part]
        fin, dst = s.fin.at[start : start + rows], s.dattn.at[start : start + rows]
        sems = s.tail_s.at[part], s.tail_r.at[part]
        return (
            s.remote(fin.at[:, half[3]], dst.at[:, half[2]], *sems, s.sib),
            s.remote(fin.at[:, half[3]], dst.at[:, half[3]], *sems, s.sib),
        )

    def tail(part):
        _, start, rows = rs_parts[part]
        own = slice(start, start + rows)

        @pl.when(by_rows)
        def _():
            s.dattn[own, :] = s.fin[own, :]

        @pl.when(jnp.logical_not(by_rows))
        def _():
            tail_copies(part)[0].start()
            s.dattn[own, half[2]] = s.fin[own, half[2]]

    s.tail = tail
    spread = Steps(s.rs(s.dffn, s.fin), ACROSS * A)
    if s.nt == 1:
        for x in range(2):
            hidden_terms(2 * s.turns[0] + x)
        spread.until(0.0)

        @pl.loop(2, 2 * A)
        def _(k):
            hidden_terms(2 * s.turn(k // 2) + lax.rem(k, 2))
    else:

        @pl.loop(0, 2 * tiles)
        def _(k):
            hidden_terms(k)

        spread.until(0.0)

    s.f_credit(None, 0)
    s.taken(3)

    def second_back(own, full):
        dy = alpha_scale * s.nbuf[own, :] + s.pacc[own, :] + s.rb[1, own, :].astype(F32)
        grad = s.norm_back(1, dy, s.zh2[own, :], s.inv2[own, :])
        s.nbuf[own, :] = grad
        s.gb[full, :] = grad.astype(BF)

    s.norm_rows(second_back)
    s.share(s.gb, 5)
    spread.until(3.0)
    s.shared(s.gb, 5)

    def mixed_back(grad, o, b):
        for m in range(2):
            rows = slice(m * T, (m + 1) * T)
            s.do[rows, :] = (
                dot_nt(grad[rows, :TILE], s.wrow(b, 0)) + dot_nt(grad[rows, TILE:], s.wrow(b, 1))
            ).astype(BF)
        for h in range(2):
            cols = slice(h * TILE, (h + 1) * TILE)
            terms = dot_tn(o[...], grad[:, cols]).astype(BF)
            s.wb[pl.ds(b * s.nzx, s.nzx), h] = terms.reshape(s.nzx, 2 * R, TILE)

    def weight_terms(b, source, grad):
        for h in range(2):
            cols = slice(h * TILE, (h + 1) * TILE)
            terms = dot_tn(source[:, cols], grad).astype(BF)
            half = s.nzx // 2 if s.nzx > 1 else 0
            if half:
                s.wb[pl.ds(b * s.nzx + h * half, half)] = terms.reshape(half, 2, 2 * R, TILE)
            else:
                s.wb[b, h] = terms

    def spread_back(which, blocks):
        rows = s.rows_of(which)
        halves = []
        for h in range(2):
            total = 0.0
            for b, k in blocks:
                total += dot_nt(s.dqkv[k, rows, :], s.wcol(b)[h * TILE : (h + 1) * TILE])
            halves.append(total)
        return halves

    mixed_back(s.gb, s.o2, 7)
    spread.until(5.0)

    @pl.loop(0, TILE // PAIR)
    def _(p):
        s.attend_back(p, s.qkv2, s.do, s.lse2, False, spread.timed(p, TILE // PAIR, 4, 5.0, 8.0))

    s.give(4, lambda which: spread_back(which, [(5, 1), (6, 2)]))
    spread.until(15.0)
    s.taken(4)

    def memory_rows(own, full):
        total = s.pacc[own, :] + s.rb[0, own, :].astype(F32)
        s.osb[1, own, :] = total.astype(BF)

    s.norm_rows(memory_rows)
    sent_back.append(send_back(1))
    s.give(5, lambda which: spread_back(which, [(4, 0)]))
    spread.until(18.0)
    weight_terms(4, s.n1r, s.dqkv[0])
    weight_terms(5, s.mf, s.dqkv[1])
    weight_terms(6, s.mf, s.dqkv[2])
    spread.until(21.0)
    s.taken(5)

    def first_back(own, full):
        dy = alpha_scale * s.nbuf[own, :] + s.pacc[own, :] + s.rb[1, own, :].astype(F32)
        grad = s.norm_back(0, dy, s.zh1[own, :], s.inv1[own, :])
        s.nbuf[own, :] = grad
        s.ga[full, :] = grad.astype(BF)

    s.norm_rows(first_back)
    s.share(s.ga, 6)
    spread.until(24.0)
    s.shared(s.ga, 6)

    def norm_sum():
        for k, device in enumerate((s.sib, s.near["x"], s.near["y"])):
            copy = s.remote(s.ngs.at[k], s.ngr.at[k], s.nm_s.at[k], s.nm_r.at[k], device)
            s.ngs[k] = s.ng[...]
            copy.start()
            yield
            copy.wait()
            s.ng[...] = s.ng[...] + s.ngr[k]
        s.ngz[s.z] = s.ng[...]
        for other in range(A):

            @pl.when(s.z != other)
            def _():
                s.remote(
                    s.ng, s.ngz.at[s.z], s.nm_s.at[3 + other], s.nm_r.at[3 + s.z],
                    (s.dp + 4 * (other - s.z), s.y),
                ).start()

        yield
        for other in range(A):

            @pl.when(s.z != other)
            def _():
                s.remote(s.ng, s.ngz.at[other], s.nm_s.at[3 + other], s.nm_r.at[3 + other], s.sib).wait()

        total = s.ngz[0]
        for other in range(1, A):
            total = total + s.ngz[other]
        s.dnorm[...] = total[:6, :]
        yield

    sums = norm_sum()
    next(sums)

    mixed_back(s.ga, s.o1, 3)
    spread.until(27.0)
    next(sums)

    @pl.loop(0, TILE // PAIR)
    def _(p):
        s.attend_back(p, s.qkv1, s.do, s.lse1, True, spread.timed(p, TILE // PAIR, 4, 27.0, 9.0))

    s.give(6, lambda which: spread_back(which, [(0, 0), (1, 1), (2, 2)]))

    @pl.loop(0, 3)
    def _(k):
        weight_terms(k, s.xf, s.dqkv[k])

    for due in SUMS:
        spread.steps.append((due, lambda: next(sums, None)))
    spread.steps.sort(key=lambda step: step[0])
    s.taken(6)

    def token_rows(own, full):
        total = alpha_scale * s.nbuf[own, :] + s.pacc[own, :] + s.rb[0, own, :].astype(F32)
        s.osb[2, own, :] = total.astype(BF)

    s.norm_rows(token_rows)
    sent_back.append(send_back(2))
    spread.until(1e9)
    s.f_credit(pl.semaphore_wait, 0)
    spread.limit = 1e9

    spread.until(1e9)

    for here_copy, there_copy in sent_back:

        @pl.when(s.kept)
        def _():
            here_copy.wait()

        @pl.when(away)
        def _():
            there_copy.wait()

    for part in range(len(rs_parts)):

        @pl.when(jnp.logical_not(by_rows))
        def _():
            sent, come = tail_copies(part)
            sent.wait_send()
            come.wait_recv()

    s.rs_drain()


def hand_on(*refs):
    for src, dst in zip(refs[: len(refs) // 2], refs[len(refs) // 2 :]):
        dst[...] = src[...].astype(F32)


def hand_specs(outputs):
    return [
        pl.BlockSpec(shape, lambda i: (0, 0))
        if shape[0] % (8 * HANDS)
        else pl.BlockSpec((shape[0] // HANDS, shape[1]), lambda i: (i, 0))
        for shape in outputs.values()
    ]


def on_device(A, tokens, memory, attn_bank, ffn_bank, norm_params, prefix, cotangent):
    T, D = tokens.shape
    R = attn_bank.shape[0]
    ag_parts, rs_parts = cut(R, GATHER), cut(R, SCATTER)
    groups = D // (4 * R)
    tiles = 2 * A * R // TILE

    block = (lax.axis_index("dp") // 2) // groups
    by_rows = jnp.logical_or(block == 3, block == 7)
    attn_rows = attn_bank
    if groups > 1:
        by_core = attn_bank.reshape(R, groups, 2, 2 * R).transpose(0, 2, 1, 3).reshape(R, D)
        attn_rows = jnp.where(by_rows, attn_bank, by_core)
    slots = sum(landing(order, A) for order, _, _ in rs_parts)

    inputs = dict(
        tokens=tokens,
        memory=memory,
        cot=cotangent,
        pfx=prefix,
        attn_rows=attn_rows,
        ffn_rows=ffn_bank,
        norms=norm_params,
    )
    where = dict(pfx=pltpu.SMEM, norms=pltpu.VMEM)
    outputs = dict(
        out=(T, D), dtok=(T, D), dmem=(T, D), dattn=(R, D), dffn=(R, D), dnorm=(6, D)
    )
    wide = lambda *shape: pltpu.VMEM(shape, F32)
    low = lambda *shape: pltpu.VMEM(shape, BF)
    dma = lambda count: pltpu.SemaphoreType.DMA((count,))
    scratch = dict(
        wb=low(4 * A, 2, 2 * R, TILE),
        xf=low(2 * T, D),
        mf=low(2 * T, D),
        n1r=low(2 * T, D),
        nga=low(2, 2 * T, D),
        gb=low(2 * T, D),
        cotb=low(T, D),
        act=low(2 * A, 2, R, TILE),
        qkv1=low(3, 2 * T, TILE),
        qkv2=low(3, 2 * T, TILE),
        dqkv=low(3, 2 * T, TILE),
        o1=low(2 * T, TILE),
        o2=low(2 * T, TILE),
        do=low(2 * T, TILE),
        sb=low(2, T, D),
        rb=low(2, T, D),
        osb=low(3, T, D),
        zh1=wide(T, D),
        zh2=wide(T, D),
        nbuf=wide(T, D),
        pacc=wide(T, D),
        fin=low(R, D),
        pfx_own=wide(8, 128),
        pfx_now=wide(8, 128),
        lse1=wide(TILE // PAIR, 8, 2 * T),
        lse2=wide(TILE // PAIR, 8, 2 * T),
        inv1=wide(T, 1),
        inv2=wide(T, 1),
        ng=wide(8, D),
        ngs=wide(3, 8, D),
        ngr=wide(3, 8, D),
        ngz=wide(A, 8, D),
        lc=dma(8),
        misc_s=dma(1),
        misc_r=dma(1),
        tail_s=dma(len(rs_parts)),
        tail_r=dma(len(rs_parts)),
        sw_s=dma(4),
        sw_r=dma(4),
        ag_s=dma(len(ag_parts) * 4),
        ag_r=dma(2 * len(ag_parts) * (2 * A + 1)),
        rs_s=dma(len(rs_parts) * 4),
        rs_r=dma(slots + len(rs_parts) * 2 * A),
        cg_s=dma(7),
        cg_r=dma(7),
        ex_s=dma(7),
        ex_r=dma(7),
        ob_s=dma(3),
        ob_r=dma(3),
        nm_s=dma(3 + A),
        nm_r=dma(3 + A),
        credit=pltpu.SemaphoreType.REGULAR((6,)),
    )
    for i, (order, _, rows) in enumerate(rs_parts):
        scratch[f"land{i}"] = low(landing(order, A), 2, rows, TILE)
    names = list(inputs) + list(outputs) + list(scratch)
    results = pl.pallas_call(
        functools.partial(kernel, A, R, T, ag_parts, rs_parts, names),
        out_shape=[
            jax.ShapeDtypeStruct(shape, F32 if name == "dnorm" else BF) for name, shape in outputs.items()
        ],
        in_specs=[pl.BlockSpec(memory_space=where.get(n, pl.ANY)) for n in inputs],
        out_specs=[pl.BlockSpec(memory_space=pltpu.VMEM)] * len(outputs),
        scratch_shapes=list(scratch.values()),
        compiler_params=pltpu.CompilerParams(
            collective_id=0, has_side_effects=True, vmem_limit_bytes=64 * 2**20
        ),
        name="layer",
    )(*inputs.values())

    results = pl.pallas_call(
        hand_on,
        grid=(HANDS,),
        out_shape=[jax.ShapeDtypeStruct(shape, F32) for shape in outputs.values()],
        in_specs=hand_specs(outputs),
        out_specs=hand_specs(outputs),
        name="hand_on",
    )(*results)
    out, dtok, dmem, dattn, dffn, dnorm = results
    if groups > 1:
        by_core = dattn.reshape(R, 2, groups, 2 * R).transpose(0, 2, 1, 3).reshape(R, D)
        dattn = jnp.where(by_rows, dattn, by_core)
    return (out, dtok, dmem, dattn, dffn, dnorm)


def solution(mesh):
    rows = P(("dp", "seq"), None)
    return jax.shard_map(
        functools.partial(on_device, mesh.shape["dp"] // 4),
        mesh=mesh,
        in_specs=(rows, rows, rows, rows, P(), P("dp"), rows),
        out_specs=(rows, rows, rows, rows, rows, P()),
        check_vma=False,
    )
```

```python
import functools

import jax
import jax.numpy as jnp
from jax import lax
from jax.experimental import pallas as pl
from jax.experimental.pallas import tpu as pltpu
from jax.sharding import PartitionSpec as P

HD = 64
PAIR = 2 * HD
TILE = 512
SUB = 16
LN_ROWS = 32
CHUNKS = 4
HANDS = 2
AHEAD = 8
ACROSS = 11.63
ALONG = 12.12
HOP = 9.52
LAG_BIG = 0.06
LAG_SMALL = 0.71
START = 12.51
FIRST = 3.0
SECOND = 10.05
SUMS = (56.0, 74.0, 94.0)
EARLY = 5.87
COME = 10.6
PLANE = 13.85
STEP = 1.58
BESIDE = 9.75
CROSS = 10.02
SECOND_BANK = 51.38
SWAPS = 35.59
LATE_SWAP = 64.42
GATHERED = 66.95
RATE = 1.06
GATHER = (5, 6, 2, 3)
SCATTER = (4, 6, 3, 3)

alpha_scale = 300.0**0.25
norm_eps = 1e-05
masked_score = -1e30
score_scale = HD**-0.5

BF = jnp.bfloat16
F32 = jnp.float32
MESH = pl.DeviceIdType.MESH


def dot(left, right):
    return jnp.dot(left, right, preferred_element_type=F32)


def dot_nt(left, right):
    return lax.dot_general(left, right, (((1,), (1,)), ((), ())), preferred_element_type=F32)


def dot_tn(left, right):
    return lax.dot_general(left, right, (((0,), (0,)), ((), ())), preferred_element_type=F32)


def turned(block):
    return block.astype(F32).T.astype(BF)


def cut(rows, split):
    units = rows // SUB
    shares = [(units * share + 8) // 16 for share in split[1:]]
    sizes = list(zip(("xzy", "yzx", "zxy", "zyx"), [units - sum(shares)] + shares))
    parts, start = [], 0
    for order, size in sizes:
        if size > 0:
            parts.append((order, start * SUB, size * SUB))
        start += size
    return parts


def slots_of(order, A):
    return 4 * A + 3 if order[0] != "z" else 4 * A + 1


def landing(order, A):
    return slots_of(order, A) + (3 if order[0] != "z" else 1)


class Layer:
    def __init__(self, A, R, T, ag_parts, rs_parts, refs):
        self.A, self.R, self.T = A, R, T
        self.ag_parts, self.rs_parts = ag_parts, rs_parts
        self.D = 1024
        self.nzx = self.D // (4 * R)
        self.nt = TILE // (2 * R)
        for name, ref in refs.items():
            setattr(self, name, ref)
        self.dp, self.y = lax.axis_index("dp"), lax.axis_index("seq")
        self.c = lax.rem(self.dp, 2)
        self.x = lax.rem(self.dp // 2, 2)
        self.z = self.dp // 4
        self.zx = self.dp // 2
        self.sib = (self.dp + 1 - 2 * self.c, self.y)
        self.near = {"x": (self.dp + 2 - 4 * self.x, self.y), "y": (self.dp, 1 - self.y)}
        self.up = (self.dp + 4, self.y)
        self.down = (self.dp - 4, self.y)
        self.partner = (self.dp - self.c + self.y, self.c)
        self.has_up = self.z < A - 1
        self.has_down = self.z > 0
        self.kept = self.c == self.y
        self.turns = [self.turn(j) for j in range(A)]


    def remote(self, src, dst, send, recv, device):
        return pltpu.make_async_remote_copy(
            src_ref=src, dst_ref=dst, send_sem=send, recv_sem=recv, device_id=device, device_id_type=MESH
        )

    def own(self, axis):
        return self.x if axis == "x" else self.y

    def spot(self, bank, part, z, x, y):
        order, start, rows = part
        row = pl.multiple_of(y * self.R + start, SUB)
        return self.wb.at[bank * 2 * self.A + z * 2 + x, :, pl.ds(row, rows), :]

    def place(self, axis, f, l):
        return (f, l) if axis == "x" else (l, f)


    def barrier(self):
        bar = pltpu.get_barrier_semaphore()

        def greet(device):
            pl.semaphore_signal(bar, inc=1, device_id=device, device_id_type=MESH)

        greet(self.sib)
        greet(self.near["x"])
        greet(self.near["y"])
        for other in range(self.A):

            @pl.when(self.z != other)
            def _():
                greet((self.dp + 4 * (other - self.z), self.y))

        @pl.when(jnp.logical_not(self.kept))
        def _():
            greet(self.partner)
            pl.semaphore_wait(bar, 3 + self.A)

        @pl.when(self.kept)
        def _():
            pl.semaphore_wait(bar, 2 + self.A)


    def ag_index(self, bank, part, z, x, y, last):
        base = (bank * len(self.ag_parts) + part) * (2 * self.A + 1)
        if last:
            return base + 2 * self.A
        return base + z * 2 + (x if self.ag_parts[part][0][2] == "y" else y)

    def ag_send(self, bank, part, z, x, y, kind, device):
        ref = self.spot(bank, self.ag_parts[part], z, x, y)
        recv = self.ag_r.at[self.ag_index(bank, part, z, x, y, kind == 3)]
        self.remote(ref, ref, self.ag_s.at[part * 4 + kind], recv, device).start()

    def ag_wait(self, bank, part, z, x, y):
        ref = self.spot(bank, self.ag_parts[part], z, x, y)
        recv = self.ag_r.at[self.ag_index(bank, part, z, x, y, False)]
        self.remote(ref, ref, self.ag_s.at[0], recv, self.sib).wait_recv()

    def ag_last(self, bank, part):
        _, _, rows = self.ag_parts[part]
        ref = self.wb.at[0 : 2 * self.A, :, pl.ds(0, rows), :]
        recv = self.ag_r.at[self.ag_index(bank, part, 0, 0, 0, True)]
        self.remote(ref, ref, self.ag_s.at[0], recv, self.sib).wait_recv()

    def ag(self, bank, start, latest=1e9):
        A = self.A
        info = self.orders(self.ag_parts)

        def z_sends(part, f, fc, lc, w):
            px, py = self.place(f, fc, lc)

            @pl.when(self.has_up)
            def _():
                self.ag_send(bank, part, self.z, px, py, w, self.up)

            @pl.when(self.has_down)
            def _():
                self.ag_send(bank, part, self.z, px, py, w, self.down)

        def send(part, f, fc, lc, z, kind, axis):
            px, py = self.place(f, fc, lc)
            self.ag_send(bank, part, z, px, py, kind, self.near[axis])

        def early():
            for part, big, f, l, fo, lo in info:
                if big:
                    send(part, f, fo, lo, self.z, 2, f)

        def begin():
            for part, big, f, l, fo, lo in info:
                z_sends(part, f, fo, lo, 0)
            for part, big, f, l, fo, lo in info:
                if not big:
                    send(part, f, fo, lo, self.z, 2, f)
                send(part, f, fo, lo, self.z, 3, l)

        def beside(part, big, f, l, fo, lo):
            px, py = self.place(f, 1 - fo, lo)
            self.ag_wait(bank, part, self.z, px, py)
            z_sends(part, f, 1 - fo, lo, 1)
            send(part, f, 1 - fo, lo, self.z, 3, l)

        def arrive(d, w, part, big, f, l, fo, lo):
            fc = fo if w == 0 else 1 - fo
            px, py = self.place(f, fc, lo)

            def arrived(z, on, device):
                self.ag_wait(bank, part, z, px, py)

                @pl.when(on)
                def _():
                    self.ag_send(bank, part, z, px, py, w, device)

                if not big:
                    send(part, f, fc, lo, z, 2, f)
                send(part, f, fc, lo, z, 3, l)

            @pl.when(self.z >= d)
            def _():
                arrived(self.z - d, self.has_up, self.up)

            @pl.when(self.z + d < A)
            def _():
                arrived(self.z + d, self.has_down, self.down)

        def cross(d, part, big, f, l, fo, lo):
            px, py = self.place(f, 1 - fo, lo)

            def crossed(z):
                self.ag_wait(bank, part, z, px, py)
                send(part, f, 1 - fo, lo, z, 3, l)

            self.planes_at(d, crossed)

        bigs = [row for row in info if row[1]]
        smalls = [row for row in info if not row[1]]
        due = [(start - EARLY, early), (start, begin)]
        for d in range(1, A):
            for k, row in enumerate(info):
                come = start + COME + PLANE * (d - 1) + STEP * k
                due.append((come, functools.partial(arrive, d, 0, *row)))
                if row[1]:
                    side = start + BESIDE + STEP * k
                    if d == 1:
                        due.append((side, functools.partial(beside, *row)))
                    due.append((max(come + STEP * len(info), side + 0.1), functools.partial(arrive, d, 1, *row)))
                else:
                    if d == 1:
                        due.append((start + CROSS + STEP * k, functools.partial(cross, 0, *row)))
                    over = start + CROSS + PLANE * d + STEP * k
                    due.append((max(over, come + 0.1), functools.partial(cross, d, *row)))
        return [(min(time, latest), step) for time, step in due]

    def planes_at(self, d, act):
        if d == 0:
            act(self.z)
            return

        @pl.when(self.z >= d)
        def _():
            act(self.z - d)

        @pl.when(self.z + d < self.A)
        def _():
            act(self.z + d)

    def orders(self, parts):
        info = []
        for part, (order, _, _) in enumerate(parts):
            l = order[2]
            f = "x" if l == "y" else "y"
            info.append((part, order[0] != "z", f, l, self.own(f), self.own(l)))
        return info

    def ag_drain(self):
        A = self.A
        inner = jnp.logical_and(self.has_up, self.has_down)
        for part, (order, _, rows) in enumerate(self.ag_parts):
            big = order[0] != "z"

            def sent(kind, count):
                ref = self.wb.at[0 : 2 * count, :, pl.ds(0, rows), :]
                self.remote(ref, ref, self.ag_s.at[part * 4 + kind], self.ag_r.at[0], self.sib).wait_send()

            for kind in (0, 1) if big else (0,):

                @pl.when(inner)
                def _():
                    sent(kind, A + 1)

                @pl.when(jnp.logical_not(inner))
                def _():
                    sent(kind, 1)

            sent(2, 1 if big else A)
            sent(3, 2 * A)


    def turn(self, j):
        A = self.A
        mirrored = self.z >= A // 2
        w = jnp.where(mirrored, A - 1 - self.z, self.z)
        d = jnp.where(j < A - 1 - w, A - 1 - j, jnp.where(j < A - 1, j - (A - 1 - w), w))
        return jnp.where(mirrored, A - 1 - d, d)

    def rs_land(self, bank, part, slot, first):
        if bank == 0 and first:
            _, start, rows = self.rs_parts[part]
            return self.act.at[slot, :, start : start + rows, :]
        return self.land[part].at[slot]

    def rs_index(self, bank, part, slot, first):
        room = [landing(order, self.A) for order, _, _ in self.rs_parts]
        if bank == 0 and first:
            return sum(room) + part * 2 * self.A + slot
        return sum(room[:part]) + slot

    def rs_send(self, bank, part, z, x, y, slot, kind, device):
        sem = part * 4 + kind
        self.remote(
            self.spot(bank, self.rs_parts[part], z, x, y),
            self.rs_land(bank, part, slot, kind == 3),
            self.rs_s.at[sem],
            self.rs_r.at[self.rs_index(bank, part, slot, kind == 3)],
            device,
        ).start()

    def rs_add(self, bank, part, z, x, y, slot, out=None, first=False):
        landed = self.rs_land(bank, part, slot, first)
        self.remote(
            landed, landed, self.rs_s.at[0], self.rs_r.at[self.rs_index(bank, part, slot, first)], self.sib
        ).wait_recv()
        order, start, rows = self.rs_parts[part]
        at = bank * 2 * self.A + z * 2 + x
        row = pl.multiple_of(y * self.R + start, SUB)

        @pl.loop(0, 2)
        def _(h):
            total = self.wb[at, h, pl.ds(row, rows), :].astype(F32) + landed[h].astype(F32)
            if out is None:
                self.wb[at, h, pl.ds(row, rows), :] = total.astype(BF)
            else:
                out[start : start + rows, pl.ds(pl.multiple_of(h * TILE, TILE), TILE)] = total.astype(out.dtype)

    def rs_firsts(self, bank):
        sends = []

        def send(z, w, part, big, f, l, fo, lo):
            fc = fo if w == 0 else 1 - fo
            px, py = self.place(f, fc, 1 - lo)
            self.rs_send(bank, part, z, px, py, z * 2 + fc, 3, self.near[l])

        for z in self.turns:
            for row in self.orders(self.rs_parts):
                for w in (1, 0):
                    sends.append(functools.partial(send, z, w, *row))
        return sends

    def rs_slot(self, bank, part, slot):
        if bank == 1:
            return slot
        A = self.A
        more = slots_of(self.rs_parts[part][0], A)
        slot = slot - 2 * A
        return jnp.where(slot < 2 * A, slot, slot - 2 * A + more)

    def chain(self, bank, part, big, f, fc, lo, w, z, final):
        A = self.A
        base = 2 * A + w * (A + 1) if big else 3 * A
        px, py = self.place(f, fc, lo)

        def slot(k):
            return self.rs_slot(bank, part, base + k)

        def onward(device, next_z, up):
            self.rs_send(bank, part, z, px, py, slot(z if up else jnp.where(z == next_z, A, z)), w, device)

        @pl.when(z > self.z)
        def _():
            @pl.when(self.has_down)
            def _():
                self.rs_add(bank, part, z, px, py, slot(z))

            onward(self.up, self.z + 1, True)

        @pl.when(z < self.z)
        def _():
            @pl.when(self.has_up)
            def _():
                self.rs_add(bank, part, z, px, py, slot(z))

            onward(self.down, self.z - 1, False)

        @pl.when(z == self.z)
        def _():
            inner = jnp.logical_and(self.has_down, self.has_up)

            @pl.when(inner)
            def _():
                self.rs_add(bank, part, z, px, py, slot(z))
                self.rs_add(bank, part, z, px, py, slot(A), final)

            @pl.when(jnp.logical_not(inner))
            def _():
                self.rs_add(bank, part, z, px, py, slot(jnp.where(self.has_down, z, A)), final)

    def rs_across(self, bank, j, sends, start):
        A, z = self.A, self.turns[j]

        def across(w, more, part, big, f, l, fo, lo):
            fc = fo if w == 0 else 1 - fo
            px, py = self.place(f, fc, lo)
            self.rs_add(bank, part, z, px, py, z * 2 + fc, first=True)
            if more:
                more()
            if w == 1 and not big:
                self.rs_send(bank, part, z, px, py, self.rs_slot(bank, part, 2 * A + z), 2, self.near[f])

        rows = [(w, row) for row in self.orders(self.rs_parts) for w in (1, 0)]
        return [
            (
                start + ACROSS * (j + (k + 1) / len(rows)),
                functools.partial(across, w, sends.pop(0) if sends else None, *row),
            )
            for k, (w, row) in enumerate(rows)
        ]

    def rs_along(self, bank, j, out, first, start):
        A, z = self.A, self.turns[j]
        at_end = jnp.logical_not(jnp.logical_and(self.has_up, self.has_down))

        def along(w, part, big, f, l, fo, lo):
            if big:
                self.chain(bank, part, big, f, fo if w == 0 else 1 - fo, lo, w, z, None)
            else:
                px, py = self.place(f, fo, lo)
                self.rs_add(bank, part, z, px, py, self.rs_slot(bank, part, 2 * A + z))
                self.chain(bank, part, big, f, fo, lo, 0, z, out if j == A - 1 else None)
                if bank == 0 and j == A - 1:
                    self.tail(part)

        def only(role, step):
            @pl.when(role)
            def _():
                step()

        orders = self.orders(self.rs_parts)
        rows = [(w, row) for row in orders if row[1] for w in (1, 0)] + [(0, row) for row in orders if not row[1]]
        plane = min(j, A - 2 + (0.0 if j == A - 1 else -0.5))
        steps = []
        for k, (w, row) in enumerate(rows):
            step = functools.partial(along, w, *row)
            inner = start + ALONG * (plane + (k + 1) / len(rows)) + HOP
            lag = LAG_BIG if row[1] else LAG_SMALL
            end = first + ACROSS * (j + lag + (k + 1) / len(rows))
            if j == A - 1:
                steps.append((max(inner, end), step))
            else:
                steps.append((max(inner, end), functools.partial(only, jnp.logical_not(at_end), step)))
                steps.append((end, functools.partial(only, at_end, step)))
        return steps

    def rs_last(self, bank, out):
        A = self.A

        def go():
            for part, big, f, l, fo, lo in self.orders(self.rs_parts):
                if big:
                    px, py = self.place(f, 1 - fo, lo)
                    self.rs_send(bank, part, self.z, px, py, self.rs_slot(bank, part, 4 * A + 2), 2, self.near[f])

        def come(part, big, f, l, fo, lo):
            px, py = self.place(f, fo, lo)
            self.rs_add(bank, part, self.z, px, py, self.rs_slot(bank, part, 4 * A + 2), out)
            if bank == 0:
                self.tail(part)

        return [go] + [functools.partial(come, *row) for row in self.orders(self.rs_parts) if row[1]]

    def rs_ready(self):
        for go in (None, pl.semaphore_wait):
            self.z_credit(go)
            self.f_credit(go, 4)

    def rs(self, out1, out0):
        A = self.A
        due = []
        for bank, out, first, start in ((1, out1, 0.0, START), (0, out0, ACROSS * A + FIRST, ALONG * (A - 1) + SECOND)):
            sends = self.rs_firsts(bank)
            due += [(first if bank else first - FIRST / 4, step) for step in sends[:AHEAD]]
            sends = sends[AHEAD:]
            for j in range(A):
                due += self.rs_across(bank, j, sends, first)
                due += self.rs_along(bank, j, out, first, start)
            done = start + ALONG * (A - 1) + HOP
            go, *come = self.rs_last(bank, out)
            due += [(done, go)] + [(done + 2 * HOP, step) for step in come]
        due.append((ACROSS * A + FIRST / 2, self.rs_ready))
        return sorted(due, key=lambda step: step[0])

    def f_credit(self, wait, at):
        for k, axis in enumerate("xy"):
            if wait:
                wait(self.credit.at[at + k], 1)
            else:
                pl.semaphore_signal(self.credit.at[at + k], inc=1, device_id=self.near[axis], device_id_type=MESH)

    def z_credit(self, wait):
        @pl.when(self.has_up)
        def _():
            if wait:
                wait(self.credit.at[3], 1)
            else:
                pl.semaphore_signal(self.credit.at[2], inc=1, device_id=self.up, device_id_type=MESH)

        @pl.when(self.has_down)
        def _():
            if wait:
                wait(self.credit.at[2], 1)
            else:
                pl.semaphore_signal(self.credit.at[3], inc=1, device_id=self.down, device_id_type=MESH)

    def rs_drain(self):
        A = self.A
        for part, (order, _, rows) in enumerate(self.rs_parts):
            big = order[0] != "z"

            def sent(kind, count):
                ref = self.wb.at[0 : 2 * count, :, pl.ds(0, rows), :]
                self.remote(ref, ref, self.rs_s.at[part * 4 + kind], self.rs_r.at[0], self.sib).wait_send()

            sent(0, A - 1)
            if big:
                sent(1, A - 1)
            sent(2, 1 if big else A)
            sent(3, 2 * A)


    def share(self, ref, k):
        rows = ref.at[pl.ds(pl.multiple_of(self.c * self.T, SUB), self.T), :]
        copy = self.remote(rows, rows, self.cg_s.at[k], self.cg_r.at[k], self.sib)
        copy.start()
        return copy

    def shared(self, ref, k):
        rows = ref.at[pl.ds(pl.multiple_of((1 - self.c) * self.T, SUB), self.T), :]
        mine = ref.at[pl.ds(pl.multiple_of(self.c * self.T, SUB), self.T), :]
        self.remote(rows, rows, self.cg_s.at[k], self.cg_r.at[k], self.sib).wait_recv()
        self.remote(mine, mine, self.cg_s.at[k], self.cg_r.at[k], self.sib).wait_send()

    def rows_of(self, which):
        return pl.ds(pl.multiple_of(which * self.T, SUB), self.T)

    def give(self, k, halves):
        buf = k % 2
        for h, value in enumerate(halves(1 - self.c)):
            self.sb[buf, :, h * TILE : (h + 1) * TILE] = value.astype(BF)
        self.remote(self.sb.at[buf], self.rb.at[buf], self.ex_s.at[k], self.ex_r.at[k], self.sib).start()
        for h, value in enumerate(halves(self.c)):
            self.pacc[:, h * TILE : (h + 1) * TILE] = value

    def taken(self, k):
        buf = k % 2
        self.remote(self.sb.at[buf], self.rb.at[buf], self.ex_s.at[k], self.ex_r.at[k], self.sib).wait()


    def act_at(self, j, m):
        if self.nt == 1:
            return (j, m)
        half = self.nt // 2
        return (pl.ds(j * self.nt + m * half, half),)

    def act_get(self, j, m):
        return self.act[self.act_at(j, m)].reshape(self.T, TILE)

    def act_set(self, j, m, value):
        at = self.act_at(j, m)
        self.act[at] = value.astype(BF).reshape(self.act.at[at].shape)

    def act_all(self, j):
        return self.act[pl.ds(j * self.nt, self.nt)].reshape(2 * self.T, TILE)


    def wcol(self, b):
        return self.wb[pl.ds(b * self.nzx, self.nzx)].reshape(self.D, TILE)

    def wrow(self, b, h):
        return self.wb[pl.ds(b * self.nzx, self.nzx), h].reshape(TILE, TILE)

    def win(self, j, h):
        return self.wb[pl.ds(2 * self.A + j * self.nt, self.nt), h].reshape(TILE, TILE)

    def wout(self, j, h):
        return self.wb[pl.ds(3 * self.A + j * self.nt, self.nt), h].reshape(TILE, TILE)

    def project(self, dst, first, source, block, count):
        @pl.loop(0, count)
        def _(i):
            weight = self.wcol(block + i)
            for m in range(2):
                rows = slice(m * self.T, (m + 1) * self.T)
                dst[first + i, rows, :] = dot(source[rows, :], weight).astype(BF)


    def masks(self):
        lane = lax.broadcasted_iota(jnp.int32, (1, PAIR), 1)
        row = lax.broadcasted_iota(jnp.int32, (PAIR, 1), 0)
        return [(lane < HD), (lane >= HD)], (row < HD)

    def visible(self, tile):
        T = self.T
        key = lax.broadcasted_iota(jnp.int32, (2 * T, T), 0)
        query = lax.broadcasted_iota(jnp.int32, (2 * T, T), 1) + tile * T
        edge = self.pfx_now[0:1, 0:1]
        return jnp.logical_or(key <= query, key.astype(F32) < edge)

    def attend(self, p, qkv, o, lse, masked, point):
        T = self.T
        cols = pl.ds(pl.multiple_of(p * PAIR, PAIR), PAIR)
        heads, upper = self.masks()
        keys = qkv[1, :, cols]
        values_t = turned(qkv[2, :, cols])
        for tile in range(2):
            rows = slice(tile * T, (tile + 1) * T)
            query = qkv[0, rows, cols].astype(F32) * score_scale
            vis = self.visible(tile) if masked else None
            mixed = []
            for h in range(2):
                scores = dot_nt(keys, jnp.where(heads[h], query, 0.0).astype(BF))
                if masked:
                    scores = jnp.where(vis, scores, masked_score)
                highest = jnp.max(scores, axis=0, keepdims=True)
                exponent = jnp.exp(scores - highest)
                total = jnp.sum(exponent, axis=0, keepdims=True)
                lse[p, h : h + 1, rows] = highest + jnp.log(total)
                mixed.append(dot(values_t, exponent.astype(BF)) * (1.0 / total))
                point(2 * tile + h)
            o[rows, cols] = jnp.where(upper, mixed[0], mixed[1]).T.astype(BF)

    def attend_back(self, p, qkv, do, lse, masked, point):
        T = self.T
        cols = pl.ds(pl.multiple_of(p * PAIR, PAIR), PAIR)
        heads, upper = self.masks()
        keys, values = qkv[1, :, cols], qkv[2, :, cols]
        keys_t = turned(keys)
        dk = [0.0, 0.0]
        dv = [0.0, 0.0]
        for tile in range(2):
            rows = slice(tile * T, (tile + 1) * T)
            query = qkv[0, rows, cols]
            grad = do[rows, cols]
            query_wide = query.astype(F32) * score_scale
            grad_wide = grad.astype(F32)
            vis = self.visible(tile) if masked else None
            dq = []
            for h in range(2):
                scores = dot_nt(keys, jnp.where(heads[h], query_wide, 0.0).astype(BF))
                if masked:
                    scores = jnp.where(vis, scores, masked_score)
                probs = jnp.exp(scores - lse[p, h : h + 1, rows])
                dprobs = dot_nt(values, jnp.where(heads[h], grad_wide, 0.0).astype(BF))
                delta = jnp.sum(dprobs * probs, axis=0, keepdims=True)
                dscores = (probs * (dprobs - delta)).astype(BF)
                dq.append(dot(keys_t, dscores))
                dk[h] += dot(dscores, query)
                dv[h] += dot(probs.astype(BF), grad)
                point(2 * tile + h)
            self.dqkv[0, rows, cols] = (jnp.where(upper, dq[0], dq[1]) * score_scale).T.astype(BF)
        self.dqkv[1, :, cols] = (jnp.where(heads[0], dk[0], dk[1]) * score_scale).astype(BF)
        self.dqkv[2, :, cols] = jnp.where(heads[0], dv[0], dv[1]).astype(BF)


    def norm(self, summed):
        centred = summed - jnp.mean(summed, axis=-1, keepdims=True)
        inv = lax.rsqrt(jnp.mean(centred * centred, axis=-1, keepdims=True) + norm_eps)
        return centred * inv, inv

    def norm_back(self, k, dy, normed, inv):
        gain = self.norms[k : k + 1, :]
        self.ng[k : k + 1, :] += jnp.sum(dy * normed, axis=0, keepdims=True)
        self.ng[3 + k : 4 + k, :] += jnp.sum(dy, axis=0, keepdims=True)
        scaled = dy * gain
        plain = jnp.mean(scaled, axis=-1, keepdims=True)
        along = jnp.mean(scaled * normed, axis=-1, keepdims=True)
        return inv * (scaled - plain - normed * along)

    def norm_rows(self, body, first=0, last=None):
        @pl.loop(first, self.T // LN_ROWS if last is None else last)
        def _(i):
            own = pl.ds(pl.multiple_of(i * LN_ROWS, LN_ROWS), LN_ROWS)
            full = pl.ds(pl.multiple_of(self.c * self.T + i * LN_ROWS, LN_ROWS), LN_ROWS)
            body(own, full)


class Steps:
    def __init__(self, steps, limit=1e9):
        self.steps, self.limit = list(steps), limit

    def run(self, count):
        now, self.steps = self.steps[:count], self.steps[count:]
        for step in now:
            step()

    def finish(self):
        self.run(len(self.steps))

    def until(self, time):
        while self.steps and self.steps[0][0] <= min(time, self.limit):
            self.steps.pop(0)[1]()

    def timed(self, index, turns, points, start, length):
        groups = []
        for place in range(turns * points):
            time, group = start + length * (place + 1) / (turns * points), []
            while self.steps and self.steps[0][0] <= min(time, self.limit):
                group.append(self.steps.pop(0)[1])
            groups.append(group)

        def at(point):
            for turn in range(turns):
                if groups[turn * points + point]:

                    @pl.when(index == turn)
                    def _():
                        for step in groups[turn * points + point]:
                            step()

        return at

    def spread(self, index, turns, points, count=1):
        total = turns * points * count
        now, self.steps = self.steps[:total], self.steps[total:]

        def at(point):
            for turn in range(turns):
                place = (turn * points + point) * count
                if now[place : place + count]:

                    @pl.when(index == turn)
                    def _():
                        for step in now[place : place + count]:
                            step()

        return at


def kernel(A, R, T, ag_parts, rs_parts, names, *arrays):
    s = Layer(A, R, T, ag_parts, rs_parts, dict(zip(names, arrays)))
    s.land = [getattr(s, f"land{i}") for i in range(len(rs_parts))]
    D = s.D
    s.n2r, s.ga = s.nga.at[0], s.nga.at[1]
    away = jnp.logical_not(s.kept)
    s.ng[...] = jnp.zeros_like(s.ng)
    s.pfx_own[...] = jnp.full(s.pfx_own.shape, s.pfx[0], jnp.int32).astype(F32)
    s.barrier()

    block = s.zx // s.nzx
    by_rows = jnp.logical_or(block == 3, block == 7)
    mine = pl.ds(pl.multiple_of(s.y * R, SUB), R)
    half = [pl.ds(pl.multiple_of(h * TILE, TILE), TILE) for h in (0, 1, s.c, 1 - s.c)]
    ffn_copies = [
        pltpu.make_async_copy(s.ffn_rows.at[:, half[h]], s.wb.at[2 * A + s.zx, h, mine, :], s.lc.at[h]) for h in (0, 1)
    ]
    rows_copies = [
        pltpu.make_async_copy(s.attn_rows.at[:, half[h]], s.wb.at[s.zx, h, mine, :], s.lc.at[2 + h]) for h in (0, 1)
    ]
    half_copy = pltpu.make_async_copy(s.attn_rows.at[:, half[2]], s.wb.at[s.zx, s.c, mine, :], s.lc.at[2])
    half_send = s.remote(
        s.attn_rows.at[:, half[3]], s.wb.at[s.zx, s.c, mine, :], s.misc_s.at[0], s.misc_r.at[0], s.sib
    )
    half_recv = s.remote(
        s.attn_rows.at[:, half[3]], s.wb.at[s.zx, 1 - s.c, mine, :], s.misc_s.at[0], s.misc_r.at[0], s.sib
    )
    for copy in ffn_copies:
        copy.start()

    @pl.when(by_rows)
    def _():
        for copy in rows_copies:
            copy.start()

    @pl.when(jnp.logical_not(by_rows))
    def _():
        half_copy.start()
        half_send.start()

    here = s.rows_of(s.c)
    there = s.rows_of(s.y)
    swaps = [
        (s.tokens, s.xf.at[here, :], s.xf.at[there, :]),
        (s.memory, s.mf.at[here, :], s.mf.at[there, :]),
        (s.pfx_own, s.pfx_now, s.pfx_now),
        (s.cot, s.cotb, s.cotb),
    ]

    def swap(i):
        src, dst, far = swaps[i]

        @pl.when(s.kept)
        def _():
            pltpu.make_async_copy(src, dst, s.lc.at[4 + i]).start()

        @pl.when(away)
        def _():
            s.remote(src, far, s.sw_s.at[i], s.sw_r.at[i], s.partner).start()


    (_, first_rows), *second = s.ag(1, SECOND_BANK)
    for copy in ffn_copies:
        copy.wait()
    first_rows()

    @pl.when(by_rows)
    def _():
        for copy in rows_copies:
            copy.wait()

    @pl.when(jnp.logical_not(by_rows))
    def _():
        half_copy.wait()
        half_send.wait_send()
        half_recv.wait_recv()

    due = s.ag(0, EARLY, GATHERED) + second
    due += [(SWAPS, functools.partial(swap, i)) for i in range(3)] + [(LATE_SWAP, functools.partial(swap, 3))]
    gather = Steps(sorted(due, key=lambda step: step[0]))
    gather.until(EARLY)

    def swapped(i):
        src, dst, far = swaps[i]

        @pl.when(s.kept)
        def _():
            pltpu.make_async_copy(src, dst, s.lc.at[4 + i]).wait()

        @pl.when(away)
        def _():
            s.remote(src, far, s.sw_s.at[i], s.sw_r.at[i], s.partner).wait_send()
            s.remote(src, dst, s.sw_s.at[i], s.sw_r.at[i], s.partner).wait_recv()

    gather.until(GATHERED)
    for i in range(3):
        swapped(i)
    s.share(s.xf, 0)
    s.share(s.mf, 1)
    for part in range(len(ag_parts)):
        s.ag_last(0, part)
    s.shared(s.xf, 0)
    s.shared(s.mf, 1)

    def clock(time):
        return GATHERED + RATE * time

    s.project(s.qkv1, 0, s.xf, 0, 3)
    gather.until(clock(2.0))
    s.project(s.qkv2, 1, s.mf, 5, 2)
    gather.until(clock(3.5))

    @pl.loop(0, TILE // PAIR)
    def _(p):
        s.attend(p, s.qkv1, s.o1, s.lse1, True, gather.timed(p, TILE // PAIR, 4, clock(3.5), RATE * 8.0))

    def branch(o, b):
        return lambda which: [dot(o[s.rows_of(which), :], s.wrow(b, h)) for h in range(2)]

    s.give(0, branch(s.o1, 3))
    gather.until(clock(13.5))
    s.taken(0)

    def first_norm(own, full):
        summed = alpha_scale * s.xf[full, :].astype(F32) + s.pacc[own, :] + s.rb[0, own, :].astype(F32)
        normed, inv = s.norm(summed)
        s.zh1[own, :] = normed
        s.inv1[own, :] = inv
        result = normed * s.norms[0:1, :] + s.norms[3:4, :]
        s.nbuf[own, :] = result
        s.n1r[full, :] = result.astype(BF)

    s.norm_rows(first_norm)
    s.share(s.n1r, 2)
    gather.until(clock(16.0))
    s.shared(s.n1r, 2)

    s.project(s.qkv2, 0, s.n1r, 4, 1)

    @pl.loop(0, TILE // PAIR)
    def _(p):
        s.attend(p, s.qkv2, s.o2, s.lse2, False, gather.timed(p, TILE // PAIR, 4, clock(17.0), RATE * 8.0))

    s.give(1, branch(s.o2, 7))
    gather.until(clock(27.0))
    s.taken(1)

    def second_norm(own, full):
        summed = alpha_scale * s.nbuf[own, :] + s.pacc[own, :] + s.rb[1, own, :].astype(F32)
        normed, inv = s.norm(summed)
        s.zh2[own, :] = normed
        s.inv2[own, :] = inv
        result = normed * s.norms[1:2, :] + s.norms[4:5, :]
        s.nbuf[own, :] = result
        s.n2r[full, :] = result.astype(BF)

    s.norm_rows(second_norm)
    s.share(s.n2r, 3)
    gather.until(clock(29.5))
    s.shared(s.n2r, 3)
    gather.until(1e9)
    for part in range(len(ag_parts)):
        s.ag_last(1, part)
    swapped(3)

    tiles = 2 * A * R // TILE

    @pl.loop(0, tiles)
    def _(j):
        for m in range(2):
            rows = slice(m * T, (m + 1) * T)
            pre = dot_nt(s.n2r[rows, :TILE], s.win(j, 0)) + dot_nt(s.n2r[rows, TILE:], s.win(j, 1))
            gate = 1.0 / (1.0 + jnp.exp(-pre))
            s.act_set(tiles + j, m, pre * gate)
            s.act_set(j, m, gate * (1.0 + pre * (1.0 - gate)))

    def ffn_out(which):
        return [sum(dot(s.act_get(tiles + j, which), s.wout(j, h)) for j in range(tiles)) for h in range(2)]

    s.give(2, ffn_out)
    s.taken(2)

    def third_norm(own, full):
        summed = alpha_scale * s.nbuf[own, :] + s.pacc[own, :] + s.rb[0, own, :].astype(F32)
        normed, inv = s.norm(summed)
        result = normed * s.norms[2:3, :] + s.norms[5:6, :]
        s.osb[0, own, :] = result.astype(BF)
        grad = s.norm_back(2, s.cotb[own, :].astype(F32), normed, inv)
        s.nbuf[own, :] = grad
        s.ga[full, :] = grad.astype(BF)

    chunk = T // CHUNKS

    def chunk_copy(k, core):
        rows = s.ga.at[pl.ds(pl.multiple_of(core * T + k * chunk, SUB), chunk), :]
        return s.remote(rows, rows, s.ck_s.at[k], s.ck_r.at[k], s.sib)

    for k in range(CHUNKS):
        s.norm_rows(third_norm, k * chunk // LN_ROWS, (k + 1) * chunk // LN_ROWS)
        chunk_copy(k, s.c).start()

    def send_back(k):
        dst = (s.out, s.dmem, s.dtok)[k]
        there = s.remote(s.osb.at[k], dst, s.ob_s.at[k], s.ob_r.at[k], s.partner)
        here = pltpu.make_async_copy(s.osb.at[k], dst, s.ob_s.at[k])

        @pl.when(away)
        def _():
            there.start()

        @pl.when(s.kept)
        def _():
            here.start()

        return here, there

    sent_back = [send_back(0)]
    s.ag_drain()

    def hidden_back(which):
        rows = s.rows_of(which)

        @pl.loop(0, tiles)
        def _(j):
            da = dot_nt(s.ga[rows, :TILE], s.wout(j, 0)) + dot_nt(s.ga[rows, TILE:], s.wout(j, 1))
            s.act_set(j, which, da * s.act_get(j, which).astype(F32))

    hidden_back(s.c)
    for k in range(CHUNKS):
        chunk_copy(k, s.c).wait_send()
        chunk_copy(k, 1 - s.c).wait_recv()
    hidden_back(1 - s.c)

    def ffn_in(which):
        return [sum(dot(s.act_get(j, which), s.win(j, h)) for j in range(tiles)) for h in range(2)]

    s.give(3, ffn_in)

    def hidden_terms(tile):
        hidden = s.act_all(tile)
        for h in range(2):
            terms = dot_tn(hidden, s.nga[tile // tiles, :, h * TILE : (h + 1) * TILE]).astype(BF)
            s.wb[pl.ds(2 * A + tile * s.nt, s.nt), h] = terms.reshape(s.nt, 2 * R, TILE)

    def tail_copies(part):
        _, start, rows = rs_parts[part]
        fin, dst = s.fin.at[start : start + rows], s.dattn.at[start : start + rows]
        sems = s.tail_s.at[part], s.tail_r.at[part]
        return (
            s.remote(fin.at[:, half[3]], dst.at[:, half[2]], *sems, s.sib),
            s.remote(fin.at[:, half[3]], dst.at[:, half[3]], *sems, s.sib),
        )

    def tail(part):
        _, start, rows = rs_parts[part]
        own = slice(start, start + rows)

        @pl.when(by_rows)
        def _():
            s.dattn[own, :] = s.fin[own, :]

        @pl.when(jnp.logical_not(by_rows))
        def _():
            tail_copies(part)[0].start()
            s.dattn[own, half[2]] = s.fin[own, half[2]]

    s.tail = tail
    spread = Steps(s.rs(s.dffn, s.fin), ACROSS * A)
    if s.nt == 1:
        for x in range(2):
            hidden_terms(2 * s.turns[0] + x)
        spread.until(0.0)

        @pl.loop(2, 2 * A)
        def _(k):
            hidden_terms(2 * s.turn(k // 2) + lax.rem(k, 2))
    else:

        @pl.loop(0, 2 * tiles)
        def _(k):
            hidden_terms(k)

        spread.until(0.0)

    s.f_credit(None, 0)
    s.taken(3)

    def second_back(own, full):
        dy = alpha_scale * s.nbuf[own, :] + s.pacc[own, :] + s.rb[1, own, :].astype(F32)
        grad = s.norm_back(1, dy, s.zh2[own, :], s.inv2[own, :])
        s.nbuf[own, :] = grad
        s.gb[full, :] = grad.astype(BF)

    s.norm_rows(second_back)
    s.share(s.gb, 5)
    spread.until(3.0)
    s.shared(s.gb, 5)

    def mixed_back(grad, o, b):
        for m in range(2):
            rows = slice(m * T, (m + 1) * T)
            s.do[rows, :] = (
                dot_nt(grad[rows, :TILE], s.wrow(b, 0)) + dot_nt(grad[rows, TILE:], s.wrow(b, 1))
            ).astype(BF)
        for h in range(2):
            cols = slice(h * TILE, (h + 1) * TILE)
            terms = dot_tn(o[...], grad[:, cols]).astype(BF)
            s.wb[pl.ds(b * s.nzx, s.nzx), h] = terms.reshape(s.nzx, 2 * R, TILE)

    def weight_terms(b, source, grad):
        for h in range(2):
            cols = slice(h * TILE, (h + 1) * TILE)
            terms = dot_tn(source[:, cols], grad).astype(BF)
            half = s.nzx // 2 if s.nzx > 1 else 0
            if half:
                s.wb[pl.ds(b * s.nzx + h * half, half)] = terms.reshape(half, 2, 2 * R, TILE)
            else:
                s.wb[b, h] = terms

    def spread_back(which, blocks):
        rows = s.rows_of(which)
        halves = []
        for h in range(2):
            total = 0.0
            for b, k in blocks:
                total += dot_nt(s.dqkv[k, rows, :], s.wcol(b)[h * TILE : (h + 1) * TILE])
            halves.append(total)
        return halves

    mixed_back(s.gb, s.o2, 7)
    spread.until(5.0)

    @pl.loop(0, TILE // PAIR)
    def _(p):
        s.attend_back(p, s.qkv2, s.do, s.lse2, False, spread.timed(p, TILE // PAIR, 4, 5.0, 8.0))

    s.give(4, lambda which: spread_back(which, [(5, 1), (6, 2)]))
    spread.until(15.0)
    s.taken(4)

    def memory_rows(own, full):
        total = s.pacc[own, :] + s.rb[0, own, :].astype(F32)
        s.osb[1, own, :] = total.astype(BF)

    s.norm_rows(memory_rows)
    sent_back.append(send_back(1))
    s.give(5, lambda which: spread_back(which, [(4, 0)]))
    spread.until(18.0)
    weight_terms(4, s.n1r, s.dqkv[0])
    weight_terms(5, s.mf, s.dqkv[1])
    weight_terms(6, s.mf, s.dqkv[2])
    spread.until(21.0)
    s.taken(5)

    def first_back(own, full):
        dy = alpha_scale * s.nbuf[own, :] + s.pacc[own, :] + s.rb[1, own, :].astype(F32)
        grad = s.norm_back(0, dy, s.zh1[own, :], s.inv1[own, :])
        s.nbuf[own, :] = grad
        s.ga[full, :] = grad.astype(BF)

    s.norm_rows(first_back)
    s.share(s.ga, 6)
    spread.until(24.0)
    s.shared(s.ga, 6)

    def norm_sum():
        for k, device in enumerate((s.sib, s.near["x"], s.near["y"])):
            copy = s.remote(s.ngs.at[k], s.ngr.at[k], s.nm_s.at[k], s.nm_r.at[k], device)
            s.ngs[k] = s.ng[...]
            copy.start()
            yield
            copy.wait()
            s.ng[...] = s.ng[...] + s.ngr[k]
        s.ngz[s.z] = s.ng[...]
        for other in range(A):

            @pl.when(s.z != other)
            def _():
                s.remote(
                    s.ng, s.ngz.at[s.z], s.nm_s.at[3 + other], s.nm_r.at[3 + s.z],
                    (s.dp + 4 * (other - s.z), s.y),
                ).start()

        yield
        for other in range(A):

            @pl.when(s.z != other)
            def _():
                s.remote(s.ng, s.ngz.at[other], s.nm_s.at[3 + other], s.nm_r.at[3 + other], s.sib).wait()

        total = s.ngz[0]
        for other in range(1, A):
            total = total + s.ngz[other]
        s.dnorm[...] = total[:6, :]
        yield

    sums = norm_sum()
    next(sums)

    mixed_back(s.ga, s.o1, 3)
    spread.until(27.0)
    next(sums)

    @pl.loop(0, TILE // PAIR)
    def _(p):
        s.attend_back(p, s.qkv1, s.do, s.lse1, True, spread.timed(p, TILE // PAIR, 4, 27.0, 9.0))

    s.give(6, lambda which: spread_back(which, [(0, 0), (1, 1), (2, 2)]))

    @pl.loop(0, 3)
    def _(k):
        weight_terms(k, s.xf, s.dqkv[k])

    for due in SUMS:
        spread.steps.append((due, lambda: next(sums, None)))
    spread.steps.sort(key=lambda step: step[0])
    s.taken(6)

    def token_rows(own, full):
        total = alpha_scale * s.nbuf[own, :] + s.pacc[own, :] + s.rb[0, own, :].astype(F32)
        s.osb[2, own, :] = total.astype(BF)

    s.norm_rows(token_rows)
    sent_back.append(send_back(2))
    spread.until(1e9)
    s.f_credit(pl.semaphore_wait, 0)
    spread.limit = 1e9

    spread.until(1e9)

    for here_copy, there_copy in sent_back:

        @pl.when(s.kept)
        def _():
            here_copy.wait()

        @pl.when(away)
        def _():
            there_copy.wait()

    for part in range(len(rs_parts)):

        @pl.when(jnp.logical_not(by_rows))
        def _():
            sent, come = tail_copies(part)
            sent.wait_send()
            come.wait_recv()

    s.rs_drain()


def hand_on(*refs):
    for src, dst in zip(refs[: len(refs) // 2], refs[len(refs) // 2 :]):
        dst[...] = src[...].astype(F32)


def hand_specs(outputs):
    return [
        pl.BlockSpec(shape, lambda i: (0, 0))
        if shape[0] % (8 * HANDS)
        else pl.BlockSpec((shape[0] // HANDS, shape[1]), lambda i: (i, 0))
        for shape in outputs.values()
    ]


def on_device(A, tokens, memory, attn_bank, ffn_bank, norm_params, prefix, cotangent):
    T, D = tokens.shape
    R = attn_bank.shape[0]
    ag_parts, rs_parts = cut(R, GATHER), cut(R, SCATTER)
    groups = D // (4 * R)
    tiles = 2 * A * R // TILE

    block = (lax.axis_index("dp") // 2) // groups
    by_rows = jnp.logical_or(block == 3, block == 7)
    attn_rows = attn_bank
    if groups > 1:
        by_core = attn_bank.reshape(R, groups, 2, 2 * R).transpose(0, 2, 1, 3).reshape(R, D)
        attn_rows = jnp.where(by_rows, attn_bank, by_core)
    slots = sum(landing(order, A) for order, _, _ in rs_parts)

    inputs = dict(
        tokens=tokens,
        memory=memory,
        cot=cotangent,
        pfx=prefix,
        attn_rows=attn_rows,
        ffn_rows=ffn_bank,
        norms=norm_params,
    )
    where = dict(pfx=pltpu.SMEM, norms=pltpu.VMEM)
    outputs = dict(
        out=(T, D), dtok=(T, D), dmem=(T, D), dattn=(R, D), dffn=(R, D), dnorm=(6, D)
    )
    wide = lambda *shape: pltpu.VMEM(shape, F32)
    low = lambda *shape: pltpu.VMEM(shape, BF)
    dma = lambda count: pltpu.SemaphoreType.DMA((count,))
    scratch = dict(
        wb=low(4 * A, 2, 2 * R, TILE),
        xf=low(2 * T, D),
        mf=low(2 * T, D),
        n1r=low(2 * T, D),
        nga=low(2, 2 * T, D),
        gb=low(2 * T, D),
        cotb=low(T, D),
        act=low(2 * A, 2, R, TILE),
        qkv1=low(3, 2 * T, TILE),
        qkv2=low(3, 2 * T, TILE),
        dqkv=low(3, 2 * T, TILE),
        o1=low(2 * T, TILE),
        o2=low(2 * T, TILE),
        do=low(2 * T, TILE),
        sb=low(2, T, D),
        rb=low(2, T, D),
        osb=low(3, T, D),
        zh1=wide(T, D),
        zh2=wide(T, D),
        nbuf=wide(T, D),
        pacc=wide(T, D),
        fin=low(R, D),
        pfx_own=wide(8, 128),
        pfx_now=wide(8, 128),
        lse1=wide(TILE // PAIR, 8, 2 * T),
        lse2=wide(TILE // PAIR, 8, 2 * T),
        inv1=wide(T, 1),
        inv2=wide(T, 1),
        ng=wide(8, D),
        ngs=wide(3, 8, D),
        ngr=wide(3, 8, D),
        ngz=wide(A, 8, D),
        lc=dma(8),
        misc_s=dma(1),
        misc_r=dma(1),
        tail_s=dma(len(rs_parts)),
        tail_r=dma(len(rs_parts)),
        sw_s=dma(4),
        sw_r=dma(4),
        ag_s=dma(len(ag_parts) * 4),
        ag_r=dma(2 * len(ag_parts) * (2 * A + 1)),
        rs_s=dma(len(rs_parts) * 4),
        rs_r=dma(slots + len(rs_parts) * 2 * A),
        cg_s=dma(7),
        cg_r=dma(7),
        ck_s=dma(CHUNKS),
        ck_r=dma(CHUNKS),
        ex_s=dma(7),
        ex_r=dma(7),
        ob_s=dma(3),
        ob_r=dma(3),
        nm_s=dma(3 + A),
        nm_r=dma(3 + A),
        credit=pltpu.SemaphoreType.REGULAR((6,)),
    )
    for i, (order, _, rows) in enumerate(rs_parts):
        scratch[f"land{i}"] = low(landing(order, A), 2, rows, TILE)
    names = list(inputs) + list(outputs) + list(scratch)
    results = pl.pallas_call(
        functools.partial(kernel, A, R, T, ag_parts, rs_parts, names),
        out_shape=[
            jax.ShapeDtypeStruct(shape, F32 if name == "dnorm" else BF) for name, shape in outputs.items()
        ],
        in_specs=[pl.BlockSpec(memory_space=where.get(n, pl.ANY)) for n in inputs],
        out_specs=[pl.BlockSpec(memory_space=pltpu.VMEM)] * len(outputs),
        scratch_shapes=list(scratch.values()),
        compiler_params=pltpu.CompilerParams(
            collective_id=0, has_side_effects=True, vmem_limit_bytes=64 * 2**20
        ),
        name="layer",
    )(*inputs.values())

    results = pl.pallas_call(
        hand_on,
        grid=(HANDS,),
        out_shape=[jax.ShapeDtypeStruct(shape, F32) for shape in outputs.values()],
        in_specs=hand_specs(outputs),
        out_specs=hand_specs(outputs),
        name="hand_on",
    )(*results)
    out, dtok, dmem, dattn, dffn, dnorm = results
    if groups > 1:
        by_core = dattn.reshape(R, 2, groups, 2 * R).transpose(0, 2, 1, 3).reshape(R, D)
        dattn = jnp.where(by_rows, dattn, by_core)
    return (out, dtok, dmem, dattn, dffn, dnorm)


def solution(mesh):
    rows = P(("dp", "seq"), None)
    return jax.shard_map(
        functools.partial(on_device, mesh.shape["dp"] // 4),
        mesh=mesh,
        in_specs=(rows, rows, rows, rows, P(), P("dp"), rows),
        out_specs=(rows, rows, rows, rows, rows, P()),
        check_vma=False,
    )
```
